32 devices in a mesh: groups: 2 (over x), row: 16 (over z, y, core).
Axes of the slice: x: 2, y: 2, z: 4, core: 2. Of those that a mesh axis runs over, the one named last changes fastest.
Arguments:
- velocity: float32 [3, 8, 1024, 1024], P(None, 'groups', 'row'), parts along dimension 1, may hold values from -8 to 8
- slope_matrix: float32 [1024, 1024], replicated, may hold values from -0.1875 to 0.1875
- curve_matrix: float32 [1024, 1024], replicated, may hold values from -0.1875 to 0.1875
Outputs:
- advanced: float32 [3, 8, 1024, 1024], P(None, 'groups', 'row'), parts along dimension 1
The draws below stay inside these ranges and needn't reach their ends.
There are 2 independent parts, one for each index of `groups`. The reference program is written for one: setup_inputs(seed, part) draws one part's arguments, and reference() takes and returns one part's arrays. A program takes and returns all parts, laid end to end along the dimension named above; an argument that names none is the same for every part. Nothing has to cross between parts.
All inputs are finite; a program needn't handle non-finite values.
Results may differ from the reference program's by a relative error of at most 0.00005.
Values sent between devices are 32-bit elements; how exact they have to be, the bound alone decides.
No kernel may reach another device: no remote copies, remote signals or barrier semaphores. Data moves between devices by JAX's collectives and lax.ppermute only.
A program may use at most 192 MiB of HBM per device.

```python
import jax
import jax.numpy as jnp
from jax import lax

NX = 1024
NY = 1024
NZ = 4


def draw_velocity(key, part):
    key = jax.random.fold_in(key, 11)
    first_key = jax.random.fold_in(key, 0)
    shape = (3, NZ, NY, NX)
    rising = 0.6 + 1.2 * jnp.arange(NY, dtype=jnp.float32) / (NY - 1)
    rising = rising.reshape(1, 1, NY, 1)
    return jnp.clip(jax.random.normal(first_key, shape, jnp.float32), -4.0, 4.0) * rising


def normal_values(key, extent, scale, limit, held_as=jnp.bfloat16):
    entries = jax.random.normal(key, extent, jnp.float32) * scale
    return jnp.minimum(jnp.maximum(entries, -limit), limit).astype(held_as)


def setup_inputs(seed: int = 0, part: int = 0) -> dict:
    key_list = jax.random.split(jax.random.key(seed), 4)
    own_keys = jax.random.split(jax.random.fold_in(key_list[3], part), 4)
    return {
        "velocity": draw_velocity(jax.random.fold_in(jax.random.fold_in(key_list[3], part), 71), part),
        "slope_matrix": normal_values(key_list[1], (NX, NX), NX ** -0.5, 0.1875, jnp.float32),
        "curve_matrix": normal_values(key_list[2], (NX, NX), NX ** -0.5, 0.1875, jnp.float32),
    }


viscosity = 0.2
power_input = 2.0
time_step = 0.5


def along_x(field, matrix):
    return jnp.einsum('czyk,kx->czyx', field, matrix, precision=lax.Precision.HIGHEST)


def along_y(field, matrix):
    return jnp.einsum('czkx,ky->czyx', field, matrix, precision=lax.Precision.HIGHEST)


def tendency(field, slope_matrix, curve_matrix):
    total = jnp.sum(field * field)
    forcing = power_input / (total / (3 * NZ * NY * NX))
    convect = field[0:1] * along_x(field, slope_matrix) + along_x(field[0:1] * field, slope_matrix)
    convect = convect + field[1:2] * along_y(field, slope_matrix) + along_y(field[1:2] * field, slope_matrix)
    diffuse = along_x(field, curve_matrix) + along_y(field, curve_matrix)
    return -0.5 * convect + viscosity * diffuse + forcing * field


def reference(velocity, slope_matrix, curve_matrix):
    first = tendency(velocity, slope_matrix, curve_matrix)
    middle = velocity + time_step * (8.0 / 15.0) * first
    second = tendency(middle, slope_matrix, curve_matrix)
    return middle + time_step * ((5.0 / 12.0) * second - (17.0 / 60.0) * first)
```

```python
import functools

import jax
import jax.numpy as jnp
from jax import lax
from jax.experimental import pallas as pl
from jax.experimental.pallas import tpu as pltpu
from jax.sharding import PartitionSpec as P

viscosity = 0.2
power_input = 2.0
time_step = 0.5
first_weight = 8.0 / 15.0
second_weight = 5.0 / 12.0
back_weight = 17.0 / 60.0

BF16 = jnp.bfloat16
F32 = jnp.float32
VMEM_BYTES = 50 * 1024 * 1024


def halves(x):
    high = x.astype(BF16)
    return high, (x - high.astype(F32)).astype(BF16)


def product(a, b):
    return jnp.dot(a, b, preferred_element_type=F32)


def params():
    return pltpu.CompilerParams(vmem_limit_bytes=VMEM_BYTES)


def matrices_kernel(count, order_ref, *refs):
    slope_parts, curve_parts = refs[:count], refs[count:2 * count]
    slope_ref, curve_ref, along_x_ref, along_y_ref, turned = refs[2 * count:]
    size = slope_parts[0].shape[0]
    for place, ref, scale in ((0, slope_ref, -0.5), (2, curve_ref, viscosity)):
        high, low = halves(ref[...] * scale)
        along_x_ref[place] = high
        along_x_ref[place + 1] = low
    for high_place, low_place, parts, scale in ((1, 0, slope_parts, -0.5), (2, 3, curve_parts, viscosity)):
        turned[...] = jnp.concatenate([part[...] for part in parts], axis=0).T
        for block in range(along_y_ref.shape[1] // size):
            source = pl.ds(pl.multiple_of(order_ref[block] * size, size), size)
            high, low = halves(turned[source, :] * scale)
            along_y_ref[high_place, block * size:(block + 1) * size, :] = high
            along_y_ref[low_place, block * size:(block + 1) * size, :] = low


def prepare_matrices(order, slope_matrix, curve_matrix, size):
    length = slope_matrix.shape[0]
    width = min(128, length)
    count = width // size

    def part(place):
        return pl.BlockSpec((size, length), lambda j, order_ref: (order_ref[count * j + place], 0))

    parts = [part(place) for place in range(count)]
    straight = pl.BlockSpec((width, length), lambda j, order_ref: (j, 0))
    return pl.pallas_call(
        functools.partial(matrices_kernel, count),
        grid_spec=pltpu.PrefetchScalarGridSpec(
            num_scalar_prefetch=1,
            grid=(length // width,),
            in_specs=parts + parts + [straight, straight],
            out_specs=[
                pl.BlockSpec((4, width, length), lambda j, order_ref: (0, j, 0)),
                pl.BlockSpec((4, length // 2, width), lambda j, order_ref: (0, 0, j)),
            ],
            scratch_shapes=[pltpu.VMEM((length, width), F32)],
        ),
        out_shape=[
            jax.ShapeDtypeStruct((4, length, length), BF16),
            jax.ShapeDtypeStruct((4, length // 2, length), BF16),
        ],
        compiler_params=params(),
    )(order, *([slope_matrix] * count), *([curve_matrix] * count), slope_matrix, curve_matrix)


def along_x_kernel(carrier_ref, field_ref, matrix_ref, out_ref, stack):
    rows = field_ref.shape[0]

    @pl.when(pl.program_id(0) == 0)
    def _():
        field = field_ref[...]
        high, low = halves(field)
        stack[0:rows] = low
        stack[rows:2 * rows] = high
        high, low = halves(carrier_ref[...] * field)
        stack[2 * rows:3 * rows] = high
        stack[3 * rows:4 * rows] = low

    tile = out_ref.shape[1]
    columns = pl.ds(pl.multiple_of(pl.program_id(0) * tile, tile), tile)
    a = product(stack[...], matrix_ref[0])
    b = product(stack[rows:3 * rows], matrix_ref[1])
    c = product(stack[0:2 * rows], matrix_ref[2])
    d = product(stack[rows:2 * rows], matrix_ref[3])
    slope = a[0:rows] + a[rows:2 * rows] + b[0:rows]
    rest = a[2 * rows:3 * rows] + a[3 * rows:] + b[rows:] + c[0:rows] + c[rows:] + d
    out_ref[...] = carrier_ref[:, columns] * slope + rest


def along_x(carrier, field, matrix, name):
    rows, length = field.shape
    tile = min(256, length)
    whole = pl.BlockSpec((rows, length), lambda n: (0, 0))
    return pl.pallas_call(
        along_x_kernel,
        grid=(length // tile,),
        in_specs=[whole, whole, pl.BlockSpec((4, length, tile), lambda n: (0, 0, n))],
        out_specs=pl.BlockSpec((rows, tile), lambda n: (0, n)),
        out_shape=jax.ShapeDtypeStruct((rows, length), F32),
        scratch_shapes=[pltpu.VMEM((4 * rows, length), BF16)],
        compiler_params=params(),
        cost_estimate=pl.CostEstimate(
            flops=18 * rows * length * length, bytes_accessed=8 * length * length + 12 * rows * length, transcendentals=0
        ),
        name=name,
    )(carrier, field, matrix)


def y_products(matrix_ref, near_ref, far_ref, carrier_near_ref, carrier_far_ref):
    rows, length = matrix_ref.shape[1:]
    field = jnp.concatenate([near_ref[...], far_ref[...]], axis=0)
    carrier = jnp.concatenate([carrier_near_ref[...], carrier_far_ref[...]], axis=0)
    field_high, field_low = halves(field)
    flux_high, flux_low = halves(field * carrier)
    matrix = matrix_ref[...].reshape(4 * rows, length)
    a = product(matrix, field_high)
    b = product(matrix[rows:3 * rows], field_low)
    c = product(matrix[0:2 * rows], flux_high)
    d = product(matrix[rows:2 * rows], flux_low)
    slope = a[0:rows] + a[rows:2 * rows] + b[0:rows]
    rest = a[2 * rows:3 * rows] + a[3 * rows:] + b[rows:] + c[0:rows] + c[rows:] + d
    return carrier[0:rows] * slope + rest


def first_kernel(forcing_ref, matrix_ref, near, far, carrier_near, carrier_far, x_ref, middle_ref, base_ref, square_ref):
    rows = matrix_ref.shape[1]
    kept = base_ref.shape[0]
    terms = x_ref[...] + y_products(matrix_ref, near, far, carrier_near, carrier_far)
    field = near[0:rows, :]
    first = terms + forcing_ref[0, 0] * field
    middle = field + (time_step * first_weight) * first
    middle_ref[...] = middle
    base_ref[...] = middle[0:kept] - (time_step * back_weight) * first[0:kept]
    square_ref[...] = jnp.sum((middle * middle).reshape(rows // 8, 8, middle.shape[1]), axis=0)


def second_kernel(matrix_ref, near, far, carrier_near, carrier_far, x_ref, base_ref, out_ref):
    terms = x_ref[...] + y_products(matrix_ref, near, far, carrier_near, carrier_far)
    out_ref[...] = base_ref[...] + (time_step * second_weight) * terms


def y_call(kernel, rows, matrix, fields, rest, out_rows, scalars, name):
    half, length = fields[0].shape
    tile = min(256, length)
    columns = lambda count: pl.BlockSpec((count, tile), lambda n: (0, n))
    return pl.pallas_call(
        kernel,
        grid=(length // tile,),
        in_specs=[pl.BlockSpec(memory_space=pltpu.SMEM)] * len(scalars)
        + [pl.BlockSpec((4, rows, length), lambda n: (0, 0, 0))]
        + [columns(x.shape[0]) for x in fields + rest],
        out_specs=[columns(count) for count in out_rows],
        out_shape=[jax.ShapeDtypeStruct((count, length), F32) for count in out_rows],
        compiler_params=params(),
        cost_estimate=pl.CostEstimate(
            flops=18 * rows * length * length,
            bytes_accessed=8 * rows * length + 16 * length * length + 12 * rows * length,
            transcendentals=0,
        ),
        name=name,
    )(*scalars, matrix, *fields, *rest)


def on_device(velocity, slope_matrix, curve_matrix):
    planes, size, length = velocity.shape[1:]
    devices = lax.axis_size("row")
    group = devices // planes
    chips = group // 2
    place = lax.axis_index("row")
    plane, member = place // group, place % group

    def swap(x, distance):
        return lax.ppermute(x, "row", [(r, r ^ distance) for r in range(devices)])

    def order_of(index):
        core, rest = index // (chips * planes), index % (chips * planes)
        chip, far = rest // planes, rest % planes
        return (plane ^ far) * group + (member ^ (2 * chip + core))

    order = jnp.stack([order_of(index) for index in range(devices)]).astype(jnp.int32)
    cells = 3 * planes * size * devices * length

    own = [[lax.dynamic_index_in_dim(velocity[i], plane ^ d, axis=0, keepdims=False) for d in range(planes)] for i in range(3)]
    near, far = [], []
    for i in range(3):
        mine = jnp.concatenate([own[i][0]] + [swap(own[i][d], d * group) for d in range(1, planes)], axis=0)
        others = [swap(mine, 2 * h) for h in range(1, chips)]
        near.append(jnp.concatenate([mine] + others, axis=0))
        far.append(swap(near[i], 1))

    along_x_matrix, along_y_matrix = prepare_matrices(order, slope_matrix, curve_matrix, size)
    total = lax.psum(jnp.sum(velocity * velocity), "row")
    forcing = (power_input / (total / cells)).reshape(1, 1)

    half, kept = length // 2, length // group
    middle_near, middle_far, base, squares = [], [], [], 0.0
    for i in range(3):
        x_terms = along_x(near[0], near[i], along_x_matrix, f"x_first_{i}")
        middle, back, square = y_call(
            first_kernel, half, along_y_matrix, [near[i], far[i], near[1], far[1]], [x_terms],
            [half, kept, 8], [forcing], f"y_first_{i}",
        )
        middle_near.append(middle)
        middle_far.append(swap(middle, 1))
        base.append(back)
        squares = squares + jnp.sum(square)
    total = lax.psum(squares, "row") / chips
    forcing = power_input / (total / cells)

    ends = []
    for i in range(3):
        x_terms = along_x(middle_near[0][:kept], middle_near[i][:kept], along_x_matrix, f"x_second_{i}")
        (end,) = y_call(
            second_kernel, kept, along_y_matrix, [middle_near[i], middle_far[i], middle_near[1], middle_far[1]],
            [x_terms, base[i]], [kept], [], f"y_second_{i}",
        )
        ends.append(end)

    out = jnp.zeros(velocity.shape, F32)
    for i in range(3):
        final = ends[i] + (time_step * second_weight) * forcing * middle_near[i][:kept]
        for d in range(planes):
            block = final[d * size:(d + 1) * size]
            block = swap(block, d * group) if d else block
            out = lax.dynamic_update_slice(out, block[None, None], (i, plane ^ d, 0, 0))
    return out


def solution(mesh):
    placed = (P(None, "groups", "row", None), P(), P())
    return jax.shard_map(
        on_device,
        mesh=mesh,
        in_specs=placed,
        out_specs=P(None, "groups", "row", None),
        check_vma=False,
    )
```

```python
import functools

import jax
import jax.numpy as jnp
from jax import lax
from jax.experimental import pallas as pl
from jax.experimental.pallas import tpu as pltpu
from jax.sharding import PartitionSpec as P

viscosity = 0.2
power_input = 2.0
time_step = 0.5
first_weight = 8.0 / 15.0
second_weight = 5.0 / 12.0
back_weight = 17.0 / 60.0

BF16 = jnp.bfloat16
F32 = jnp.float32
VMEM_BYTES = 50 * 1024 * 1024


def halves(x):
    high = x.astype(BF16)
    return high, (x - high.astype(F32)).astype(BF16)


def product(a, b):
    return jnp.dot(a, b, preferred_element_type=F32)


def params():
    return pltpu.CompilerParams(vmem_limit_bytes=VMEM_BYTES)


def matrices_kernel(count, order_ref, *refs):
    slope_parts, curve_parts = refs[:count], refs[count:2 * count]
    slope_ref, curve_ref, along_x_ref, along_y_ref, turned = refs[2 * count:]
    size = slope_parts[0].shape[0]
    for place, ref, scale in ((0, slope_ref, -0.5), (2, curve_ref, viscosity)):
        high, low = halves(ref[...] * scale)
        along_x_ref[place] = high
        along_x_ref[place + 1] = low
    for high_place, low_place, parts, scale in ((1, 0, slope_parts, -0.5), (2, 3, curve_parts, viscosity)):
        turned[...] = jnp.concatenate([part[...] for part in parts], axis=0).T
        for block in range(along_y_ref.shape[1] // size):
            source = pl.ds(pl.multiple_of(order_ref[block] * size, size), size)
            high, low = halves(turned[source, :] * scale)
            along_y_ref[high_place, block * size:(block + 1) * size, :] = high
            along_y_ref[low_place, block * size:(block + 1) * size, :] = low


def prepare_matrices(order, slope_matrix, curve_matrix, size):
    length = slope_matrix.shape[0]
    width = min(128, length)
    count = width // size

    def part(place):
        return pl.BlockSpec((size, length), lambda j, order_ref: (order_ref[count * j + place], 0))

    parts = [part(place) for place in range(count)]
    straight = pl.BlockSpec((width, length), lambda j, order_ref: (j, 0))
    return pl.pallas_call(
        functools.partial(matrices_kernel, count),
        grid_spec=pltpu.PrefetchScalarGridSpec(
            num_scalar_prefetch=1,
            grid=(length // width,),
            in_specs=parts + parts + [straight, straight],
            out_specs=[
                pl.BlockSpec((4, width, length), lambda j, order_ref: (0, j, 0)),
                pl.BlockSpec((4, length // 2, width), lambda j, order_ref: (0, 0, j)),
            ],
            scratch_shapes=[pltpu.VMEM((length, width), F32)],
        ),
        out_shape=[
            jax.ShapeDtypeStruct((4, length, length), BF16),
            jax.ShapeDtypeStruct((4, length // 2, length), BF16),
        ],
        compiler_params=params(),
    )(order, *([slope_matrix] * count), *([curve_matrix] * count), slope_matrix, curve_matrix)


def along_x_kernel(carrier_ref, field_ref, matrix_ref, out_ref, stack):
    rows = field_ref.shape[0]

    @pl.when(pl.program_id(0) == 0)
    def _():
        field = field_ref[...]
        high, low = halves(field)
        stack[0:rows] = low
        stack[rows:2 * rows] = high
        high, low = halves(carrier_ref[...] * field)
        stack[2 * rows:3 * rows] = high
        stack[3 * rows:4 * rows] = low

    tile = out_ref.shape[1]
    columns = pl.ds(pl.multiple_of(pl.program_id(0) * tile, tile), tile)
    a = product(stack[...], matrix_ref[0])
    b = product(stack[rows:3 * rows], matrix_ref[1])
    c = product(stack[0:2 * rows], matrix_ref[2])
    d = product(stack[rows:2 * rows], matrix_ref[3])
    slope = a[0:rows] + a[rows:2 * rows] + b[0:rows]
    rest = a[2 * rows:3 * rows] + a[3 * rows:] + b[rows:] + c[0:rows] + c[rows:] + d
    out_ref[...] = carrier_ref[:, columns] * slope + rest


def along_x(carrier, field, matrix, rows, name):
    length = field.shape[1]
    tile = min(256, length)
    whole = pl.BlockSpec((rows, length), lambda n: (0, 0))
    return pl.pallas_call(
        along_x_kernel,
        grid=(length // tile,),
        in_specs=[whole, whole, pl.BlockSpec((4, length, tile), lambda n: (0, 0, n))],
        out_specs=pl.BlockSpec((rows, tile), lambda n: (0, n)),
        out_shape=jax.ShapeDtypeStruct((rows, length), F32),
        scratch_shapes=[pltpu.VMEM((4 * rows, length), BF16)],
        compiler_params=params(),
        cost_estimate=pl.CostEstimate(
            flops=2 * rows * length * length, bytes_accessed=4 * rows * length, transcendentals=0
        ),
        name=name,
    )(carrier, field, matrix)


def joined(refs):
    return jnp.concatenate([ref[...] for ref in refs], axis=0)


def y_products(matrix_ref, fields, carriers):
    rows, length = matrix_ref.shape[1:]
    field = joined(fields)
    carrier = joined(carriers) if carriers else field
    field_high, field_low = halves(field)
    flux_high, flux_low = halves(field * carrier)
    matrix = matrix_ref[...].reshape(4 * rows, length)
    a = product(matrix, field_high)
    b = product(matrix[rows:3 * rows], field_low)
    c = product(matrix[0:2 * rows], flux_high)
    d = product(matrix[rows:2 * rows], flux_low)
    slope = a[0:rows] + a[rows:2 * rows] + b[0:rows]
    rest = a[2 * rows:3 * rows] + a[3 * rows:] + b[rows:] + c[0:rows] + c[rows:] + d
    return field[0:rows], carrier[0:rows] * slope + rest


def first_kernel(counts, forcing_ref, matrix_ref, *refs):
    fields, carriers, x_terms, (middle_ref, base_ref, square_ref) = cut(refs, counts)
    rows = matrix_ref.shape[1]
    kept = base_ref.shape[0]
    field, terms = y_products(matrix_ref, fields, carriers)
    first = terms + joined(x_terms) + forcing_ref[0, 0] * field
    middle = field + (time_step * first_weight) * first
    middle_ref[...] = middle
    base_ref[...] = middle[0:kept] - (time_step * back_weight) * first[0:kept]
    square_ref[...] = jnp.sum((middle * middle).reshape(rows // 8, 8, middle.shape[1]), axis=0)


def second_kernel(counts, forcing_ref, matrix_ref, *refs):
    fields, carriers, x_terms, (base_ref, *out_refs) = cut(refs, counts)
    field, terms = y_products(matrix_ref, fields, carriers)
    second = terms + joined(x_terms) + forcing_ref[0, 0] * field
    out = base_ref[...] + (time_step * second_weight) * second
    size = out_refs[0].shape[0]
    for place, out_ref in enumerate(out_refs):
        out_ref[...] = out[place * size:(place + 1) * size]


def cut(refs, counts):
    pieces, start = [], 0
    for count in counts:
        pieces.append(refs[start:start + count])
        start += count
    return *pieces, refs[start:]


def y_call(kernel, rows, matrix, fields, carriers, x_terms, rest, out_rows, scalars, name):
    length = fields[0].shape[1]
    tile = min(256, length)
    columns = lambda count: pl.BlockSpec((count, tile), lambda n: (0, n))
    arrays = fields + carriers + x_terms + rest
    return pl.pallas_call(
        functools.partial(kernel, (len(fields), len(carriers), len(x_terms))),
        grid=(length // tile,),
        in_specs=[pl.BlockSpec(memory_space=pltpu.SMEM)] * len(scalars)
        + [pl.BlockSpec((4, rows, length), lambda n: (0, 0, 0))]
        + [columns(x.shape[0]) for x in arrays],
        out_specs=[columns(count) for count in out_rows],
        out_shape=[jax.ShapeDtypeStruct((count, length), F32) for count in out_rows],
        compiler_params=params(),
        cost_estimate=pl.CostEstimate(
            flops=2 * rows * length * length, bytes_accessed=4 * rows * length, transcendentals=0
        ),
        name=name,
    )(*scalars, matrix, *arrays)


def after(values, *earlier):
    return lax.optimization_barrier((values, earlier))[0]


def on_device(velocity, slope_matrix, curve_matrix):
    planes, size, length = velocity.shape[1:]
    devices = lax.axis_size("row")
    group = devices // planes
    chips = group // 2
    half, kept = length // 2, length // group
    place = lax.axis_index("row")
    plane, member = place // group, place % group

    def swap(x, distance):
        return lax.ppermute(x, "row", [(r, r ^ distance) for r in range(devices)])

    def order_of(index):
        core, rest = index // (chips * planes), index % (chips * planes)
        chip, far = rest // planes, rest % planes
        return (plane ^ far) * group + (member ^ (2 * chip + core))

    def exchanged_sum(x, distances, works=()):
        for step, distance in enumerate(distances):
            arrived = swap(x, distance)
            x = x + (after(arrived, works[min(step, len(works) - 1)]) if works else arrived)
        return jnp.sum(x)

    def doubling(start, stop):
        distances = []
        while start < stop:
            distances.append(start)
            start *= 2
        return distances

    order = jnp.stack([order_of(index) for index in range(devices)]).astype(jnp.int32)
    cells = 3 * planes * size * devices * length
    along_x_matrix, along_y_matrix = prepare_matrices(order, slope_matrix, curve_matrix, size)

    def blocks(i):
        return [lax.dynamic_index_in_dim(velocity[i], plane ^ d, axis=0, keepdims=False) for d in range(planes)]

    def send(own):
        return [own[0]] + [swap(block, d * group) for d, block in enumerate(own) if d]

    def x_first(i, pieces, name):
        return [along_x(near[0][p], near[i][p], along_x_matrix, kept, f"{name}_{p}") for p in pieces]

    rest = list(range(1, chips))
    near, far = [None] * 3, [None] * 3
    arriving = [send(blocks(0)), send(blocks(1)), None]
    squares = jnp.sum((velocity * velocity).reshape(-1, 8, length // 128, 128), axis=(0, 2))

    def pass_on(i):
        mine = jnp.concatenate(arriving[i], axis=0)
        near[i] = [mine] + [swap(mine, 2 * h) for h in rest]

    def pass_across(i):
        far[i] = [swap(piece, 1) for piece in near[i]]

    arriving[0] = after(arriving[0], along_x_matrix, along_y_matrix)
    pass_on(0)
    x_terms = [x_first(0, [0], "x_first_0"), None, None]
    arriving[1] = after(arriving[1], x_terms[0])
    arriving[2] = send(after(blocks(2), x_terms[0]))
    pass_on(1)
    pass_across(0)
    x_terms[1] = x_first(1, [0], "x_first_1")
    x_terms[0] += x_first(0, rest, "x_first_0")
    arriving[2] = after(arriving[2], x_terms[0], x_terms[1])
    pass_on(2)
    pass_across(1)
    pass_across(2)
    x_terms[1] += x_first(1, rest, "x_first_1")
    total = exchanged_sum(
        squares, doubling(1, devices), [along_x_matrix, x_terms[0][0], x_terms[1][0], x_terms[0][-1]]
    )
    forcing = (power_input / (total / cells)).reshape(1, 1)

    def first_step(i):
        return y_call(
            first_kernel, half, along_y_matrix, near[i] + far[i], near[1] + far[1] if i != 1 else [], x_terms[i], [],
            [half, kept, 8], [forcing], f"y_first_{i}",
        )

    middle_near, middle_far, base, square = [None] * 3, [None] * 3, [None] * 3, [None] * 3
    for i in (0, 1):
        middle_near[i], base[i], square[i] = first_step(i)
        middle_far[i] = swap(middle_near[i], 1)
    x_terms[2] = x_first(2, [0] + rest, "x_first_2")
    far[2] = after(far[2], middle_near[0], middle_near[1], x_terms[2])
    middle_near[2], base[2], square[2] = first_step(2)
    middle_far[2] = swap(middle_near[2], 1)
    squares = jnp.sum((square[0] + square[1] + square[2]).reshape(8, length // 128, 128), axis=1)
    total = exchanged_sum(squares, [1] + doubling(group, devices))
    forcing = (power_input / (total / cells)).reshape(1, 1)

    out = jnp.zeros(velocity.shape, F32)
    previous = square[2]
    for i in range(3):
        carrier, field = after((middle_near[0], middle_near[i]), previous)
        x_second = along_x(carrier, field, along_x_matrix, kept, f"x_second_{i}")
        ends = y_call(
            second_kernel, kept, along_y_matrix, [middle_near[i], middle_far[i]],
            [middle_near[1], middle_far[1]] if i != 1 else [], [x_second], [base[i]], [size] * planes, [forcing], f"y_second_{i}",
        )
        previous = ends
        for d, block in enumerate(ends):
            block = swap(block, d * group) if d else block
            out = lax.dynamic_update_slice(out, block[None, None], (i, plane ^ d, 0, 0))
    return out


def solution(mesh):
    placed = (P(None, "groups", "row", None), P(), P())
    return jax.shard_map(
        on_device,
        mesh=mesh,
        in_specs=placed,
        out_specs=P(None, "groups", "row", None),
        check_vma=False,
    )
```

```python
import functools

import jax
import jax.numpy as jnp
from jax import lax
from jax.experimental import pallas as pl
from jax.experimental.pallas import tpu as pltpu
from jax.sharding import PartitionSpec as P

viscosity = 0.2
power_input = 2.0
time_step = 0.5
first_weight = 8.0 / 15.0
second_weight = 5.0 / 12.0
back_weight = 17.0 / 60.0

BF16 = jnp.bfloat16
F32 = jnp.float32
VMEM_BYTES = 50 * 1024 * 1024


def halves(x):
    high = x.astype(BF16)
    return high, (x - high.astype(F32)).astype(BF16)


def product(a, b):
    return jnp.dot(a, b, preferred_element_type=F32)


def params():
    return pltpu.CompilerParams(vmem_limit_bytes=VMEM_BYTES)


def matrices_kernel(count, order_ref, *refs):
    slope_parts, curve_parts = refs[:count], refs[count:2 * count]
    slope_ref, curve_ref, along_x_ref, along_y_ref, turned = refs[2 * count:]
    size = slope_parts[0].shape[0]
    for place, ref, scale in ((0, slope_ref, -0.5), (2, curve_ref, viscosity)):
        high, low = halves(ref[...] * scale)
        along_x_ref[place] = high
        along_x_ref[place + 1] = low
    for high_place, low_place, parts, scale in ((1, 0, slope_parts, -0.5), (2, 3, curve_parts, viscosity)):
        turned[...] = jnp.concatenate([part[...] for part in parts], axis=0).T
        for block in range(along_y_ref.shape[1] // size):
            source = pl.ds(pl.multiple_of(order_ref[block] * size, size), size)
            high, low = halves(turned[source, :] * scale)
            along_y_ref[high_place, block * size:(block + 1) * size, :] = high
            along_y_ref[low_place, block * size:(block + 1) * size, :] = low


def prepare_matrices(order, slope_matrix, curve_matrix, size):
    length = slope_matrix.shape[0]
    width = min(128, length)
    count = width // size

    def part(place):
        return pl.BlockSpec((size, length), lambda j, order_ref: (order_ref[count * j + place], 0))

    parts = [part(place) for place in range(count)]
    straight = pl.BlockSpec((width, length), lambda j, order_ref: (j, 0))
    return pl.pallas_call(
        functools.partial(matrices_kernel, count),
        grid_spec=pltpu.PrefetchScalarGridSpec(
            num_scalar_prefetch=1,
            grid=(length // width,),
            in_specs=parts + parts + [straight, straight],
            out_specs=[
                pl.BlockSpec((4, width, length), lambda j, order_ref: (0, j, 0)),
                pl.BlockSpec((4, length // 2, width), lambda j, order_ref: (0, 0, j)),
            ],
            scratch_shapes=[pltpu.VMEM((length, width), F32)],
        ),
        out_shape=[
            jax.ShapeDtypeStruct((4, length, length), BF16),
            jax.ShapeDtypeStruct((4, length // 2, length), BF16),
        ],
        compiler_params=params(),
    )(order, *([slope_matrix] * count), *([curve_matrix] * count), slope_matrix, curve_matrix)


def piece_spec(piece, width, column):
    _, component, rows = piece
    if component is None:
        return pl.BlockSpec((rows, width), lambda n: (0, column(n)))
    return pl.BlockSpec((None, rows, width), lambda n: (component, 0, column(n)))


def joined(refs, columns=slice(None)):
    return jnp.concatenate([ref[:, columns] for ref in refs], axis=0)


def pack_kernel(holds_squares, plane_ref, velocity_ref, own_ref, squares_ref, *block_refs):
    components, planes, size, length = velocity_ref.shape
    plane = plane_ref[0]
    velocity = velocity_ref[...].reshape(components * planes * size // 8, 8, length)
    squares = jnp.sum(velocity * velocity, axis=0)
    squares_ref[...] = squares
    for i in range(components):
        own_ref[i] = velocity_ref[i, plane]
        for d in range(1, planes):
            ref = block_refs[i * (planes - 1) + d - 1]
            ref[0:size, :] = velocity_ref[i, plane ^ d]
            if i == holds_squares:
                ref[size:, :] = squares


def pack(plane, velocity, holds_squares):
    components, planes, size, length = velocity.shape
    whole = lambda *shape: pl.BlockSpec(shape, lambda n, plane_ref: (0,) * len(shape))
    shapes = [(components, size, length), (8, length)]
    for i in range(components):
        shapes += [(size + (8 if i == holds_squares else 0), length)] * (planes - 1)
    own, squares, *blocks = pl.pallas_call(
        functools.partial(pack_kernel, holds_squares),
        grid_spec=pltpu.PrefetchScalarGridSpec(
            num_scalar_prefetch=1,
            grid=(1,),
            in_specs=[whole(*velocity.shape)],
            out_specs=[whole(*shape) for shape in shapes],
        ),
        out_shape=[jax.ShapeDtypeStruct(shape, F32) for shape in shapes],
        compiler_params=params(),
        name="pack",
    )(plane.reshape(1).astype(jnp.int32), velocity)
    return own, squares, [blocks[i * (planes - 1):(i + 1) * (planes - 1)] for i in range(components)]


def join_kernel(size, extra, *refs):
    out_ref = refs[-1]
    blocks = refs[:-1]
    if extra:
        *blocks, squares_ref = blocks
        squares = squares_ref[...]
        for ref in blocks:
            squares = squares + ref[size:, :]
        out_ref[len(blocks) * size:, :] = squares
    for place, ref in enumerate(blocks):
        out_ref[place * size:(place + 1) * size, :] = ref[0:size, :]


def join(blocks, size, squares=None):
    extra = [] if squares is None else [squares]
    rows = len(blocks) * size + (8 if extra else 0)
    return pl.pallas_call(
        functools.partial(join_kernel, size, len(extra)),
        out_shape=jax.ShapeDtypeStruct((rows, blocks[0].shape[1]), F32),
        compiler_params=params(),
        name="join",
    )(*blocks, *extra)


def along_x_kernel(counts, *refs):
    fields, carriers, _, (matrix_ref, out_ref, stack) = cut(refs, counts)
    rows = out_ref.shape[0]
    carriers = carriers or fields

    @pl.when(pl.program_id(0) == 0)
    def _():
        field = joined(fields)
        high, low = halves(field)
        stack[0:rows] = low
        stack[rows:2 * rows] = high
        high, low = halves(joined(carriers) * field)
        stack[2 * rows:3 * rows] = high
        stack[3 * rows:4 * rows] = low

    tile = out_ref.shape[1]
    columns = pl.ds(pl.multiple_of(pl.program_id(0) * tile, tile), tile)
    a = product(stack[...], matrix_ref[0])
    b = product(stack[rows:3 * rows], matrix_ref[1])
    c = product(stack[0:2 * rows], matrix_ref[2])
    d = product(stack[rows:2 * rows], matrix_ref[3])
    slope = a[0:rows] + a[rows:2 * rows] + b[0:rows]
    rest = a[2 * rows:3 * rows] + a[3 * rows:] + b[rows:] + c[0:rows] + c[rows:] + d
    out_ref[...] = joined(carriers, columns) * slope + rest


def along_x(fields, carriers, matrix, name):
    rows, length = sum(piece[2] for piece in fields), fields[0][0].shape[-1]
    tile = min(256, length)
    pieces = fields + carriers
    return pl.pallas_call(
        functools.partial(along_x_kernel, (len(fields), len(carriers), 0)),
        grid=(length // tile,),
        in_specs=[piece_spec(piece, length, lambda n: 0) for piece in pieces]
        + [pl.BlockSpec((4, length, tile), lambda n: (0, 0, n))],
        out_specs=pl.BlockSpec((rows, tile), lambda n: (0, n)),
        out_shape=jax.ShapeDtypeStruct((rows, length), F32),
        scratch_shapes=[pltpu.VMEM((4 * rows, length), BF16)],
        compiler_params=params(),
        cost_estimate=pl.CostEstimate(
            flops=2 * rows * length * length, bytes_accessed=4 * rows * length, transcendentals=0
        ),
        name=name,
    )(*[piece[0] for piece in pieces], matrix)


def y_products(matrix_ref, fields, carriers):
    rows, length = matrix_ref.shape[1:]
    field = joined(fields)
    carrier = joined(carriers) if carriers else field
    field_high, field_low = halves(field)
    flux_high, flux_low = halves(field * carrier)
    matrix = matrix_ref[...].reshape(4 * rows, length)
    a = product(matrix, field_high)
    b = product(matrix[rows:3 * rows], field_low)
    c = product(matrix[0:2 * rows], flux_high)
    d = product(matrix[rows:2 * rows], flux_low)
    slope = a[0:rows] + a[rows:2 * rows] + b[0:rows]
    rest = a[2 * rows:3 * rows] + a[3 * rows:] + b[rows:] + c[0:rows] + c[rows:] + d
    return field[0:rows], carrier[0:rows] * slope + rest


def first_kernel(counts, forcing_ref, matrix_ref, *refs):
    fields, carriers, x_terms, (middle_ref, base_ref, square_ref) = cut(refs, counts)
    rows = matrix_ref.shape[1]
    field, terms = y_products(matrix_ref, fields, carriers)
    first = terms + joined(x_terms) + forcing_ref[0, 0] * field
    middle = field + (time_step * first_weight) * first
    middle_ref[...] = middle
    base_ref[...] = middle - (time_step * back_weight) * first
    square_ref[...] = jnp.sum((middle * middle).reshape(rows // 8, 8, middle.shape[1]), axis=0)


def second_kernel(counts, forcing_ref, matrix_ref, *refs):
    fields, carriers, x_terms, (base_ref, *out_refs) = cut(refs, counts)
    field, terms = y_products(matrix_ref, fields, carriers)
    second = terms + joined(x_terms) + forcing_ref[0, 0] * field
    out = base_ref[...] + (time_step * second_weight) * second
    size = out_refs[0].shape[0]
    for place, out_ref in enumerate(out_refs):
        out_ref[...] = out[place * size:(place + 1) * size]


def cut(refs, counts):
    pieces, start = [], 0
    for count in counts:
        pieces.append(refs[start:start + count])
        start += count
    return *pieces, refs[start:]


def y_call(kernel, rows, matrix, fields, carriers, x_terms, rest, out_rows, forcing, name):
    length = fields[0][0].shape[-1]
    tile = min(256, length)
    columns = lambda count: pl.BlockSpec((count, tile), lambda n: (0, n))
    pieces = fields + carriers + [(x, None, rows) for x in [x_terms] + rest]
    return pl.pallas_call(
        functools.partial(kernel, (len(fields), len(carriers), 1)),
        grid=(length // tile,),
        in_specs=[
            pl.BlockSpec(memory_space=pltpu.SMEM),
            pl.BlockSpec((4, rows, length), lambda n: (0, 0, 0)),
            *[piece_spec(piece, tile, lambda n: n) for piece in pieces],
        ],
        out_specs=[columns(count) for count in out_rows],
        out_shape=[jax.ShapeDtypeStruct((count, length), F32) for count in out_rows],
        compiler_params=params(),
        cost_estimate=pl.CostEstimate(
            flops=2 * rows * length * length, bytes_accessed=4 * rows * length, transcendentals=0
        ),
        name=name,
    )(forcing, matrix, *[piece[0] for piece in pieces])


def after(values, *earlier):
    return lax.optimization_barrier((values, earlier))[0]


def on_device(velocity, slope_matrix, curve_matrix):
    planes, size, length = velocity.shape[1:]
    devices = lax.axis_size("row")
    group = devices // planes
    chips = group // 2
    kept = length // group
    place = lax.axis_index("row")
    plane, member = place // group, place % group
    cells = 3 * planes * size * devices * length

    def swap(x, distance):
        return lax.ppermute(x, "row", [(r, r ^ distance) for r in range(devices)])

    def swap_sum(x, distances):
        for distance in distances:
            x = x + swap(x, distance)
        return x

    def doubling(start, stop):
        return [start << step for step in range((stop // start).bit_length() - 1)]

    def order_of(index):
        core, rest = index // (chips * planes), index % (chips * planes)
        chip, far = rest // planes, rest % planes
        return (plane ^ far) * group + (member ^ (2 * chip + core))

    def forcing_of(total):
        return (power_input / (jnp.sum(total) / cells)).reshape(1, 1)

    order = jnp.stack([order_of(index) for index in range(devices)]).astype(jnp.int32)

    def send(blocks):
        return [swap(block, d * group) for d, block in enumerate(blocks, 1)]

    def across_chips(mine):
        return [mine] + [swap(mine, 2 * h) for h in range(1, chips)]

    def across_cores(near):
        return near + [swap(piece, 1) for piece in near]

    def pieces_of(i, own, rest):
        return [x for a, b in zip(own, rest) for x in ((a, i, size), (b, None, kept - size))]

    def x_terms_of(i, field, carrier, name):
        return along_x(field, carrier if i else [], along_x_matrix, name)

    def whole_piece(x):
        return (x, None, kept)

    own, squares, blocks = pack(plane, velocity, 1)
    own_near = across_chips(own)
    arriving = [None] * 3
    arriving[1] = send(blocks[1])
    arriving[0] = send(blocks[0])
    arriving[2] = send(blocks[2])
    along_x_matrix, along_y_matrix = prepare_matrices(order, slope_matrix, curve_matrix, size)

    arriving[1] = after(arriving[1], along_x_matrix, along_y_matrix)
    rest = [None] * 3
    rest[1] = across_chips(join(arriving[1], size, squares))
    own_whole = across_cores(after(own_near, rest[1][0]))
    rest[0] = across_chips(join(arriving[0], size))
    rest[1] = after(rest[1], rest[0][0])
    whole_rest = [None] * 3
    whole_rest[1] = across_cores(rest[1])
    forcing = forcing_of(sum(piece[kept - size:] for piece in whole_rest[1]))

    x_terms, near, whole = [None] * 3, [None] * 3, [None] * 3
    near[1], near[0] = pieces_of(1, own_whole[:1], rest[1][:1]), pieces_of(0, own_whole[:1], rest[0][:1])
    x_terms[1] = x_terms_of(1, near[1], near[0], "x_first_1")
    whole[1] = pieces_of(1, own_whole, whole_rest[1])

    def first_step(i):
        return y_call(
            first_kernel, kept, along_y_matrix, whole[i], whole[1] if i != 1 else [], x_terms[i], [],
            [kept, kept, 8], forcing, f"y_first_{i}",
        )

    middle, base, square, middle_near, middle_whole = [None] * 3, [None] * 3, [None] * 3, [None] * 3, [None] * 3
    middle[1], base[1], square[1] = first_step(1)
    near[0] = [(after(array, middle[1]), *place) for array, *place in near[0]]
    x_terms[0] = x_terms_of(0, near[0], [], "x_first_0")
    arriving[2] = after(arriving[2], x_terms[0])
    rest[2] = across_chips(join(arriving[2], size))
    middle_near[1] = across_chips(after(middle[1], rest[2][0]))
    whole_rest[0] = across_cores(rest[0])
    whole[0] = pieces_of(0, own_whole, after(whole_rest[0], rest[2][0]))
    middle[0], base[0], square[0] = first_step(0)
    near[2] = pieces_of(2, own_whole[:1], [after(rest[2][0], middle[0])])
    x_terms[2] = x_terms_of(2, near[2], near[0], "x_first_2")
    whole_rest[2] = across_cores(after(rest[2], x_terms[2]))
    whole[2] = pieces_of(2, own_whole, whole_rest[2])
    middle[2], base[2], square[2] = first_step(2)

    total = jnp.sum((square[0] + square[1] + square[2]).reshape(8, length // 128, 128), axis=1)
    total = swap_sum(total, doubling(group, devices) + doubling(1, group))
    forcing = forcing_of(total)

    carrier = [whole_piece(middle[0])]
    x_terms[1] = x_terms_of(1, [whole_piece(after(middle[1], square[2]))], carrier, "x_second_1")
    middle_whole[1] = across_cores(after(middle_near[1], x_terms[1]))
    middle_near[0] = across_chips(after(middle[0], total))

    def second_step(i):
        return y_call(
            second_kernel, kept, along_y_matrix, [whole_piece(x) for x in middle_whole[i]],
            [whole_piece(x) for x in middle_whole[1]] if i != 1 else [], x_terms[i], [base[i]],
            [size] * planes, forcing, f"y_second_{i}",
        )

    ends = [None] * 3
    ends[1] = second_step(1)
    x_terms[0] = x_terms_of(0, [whole_piece(after(middle[0], ends[1]))], [], "x_second_0")
    middle_near[2] = across_chips(after(middle[2], x_terms[0]))
    middle_whole[0] = across_cores(after(middle_near[0], x_terms[0]))
    x_terms[2] = x_terms_of(2, [whole_piece(after(middle[2], x_terms[0]))], carrier, "x_second_2")
    middle_whole[0] = after(middle_whole[0], x_terms[2])
    ends[0] = second_step(0)
    middle_whole[2] = across_cores(after(middle_near[2], ends[0]))
    ends[2] = second_step(2)

    out = jnp.zeros(velocity.shape, F32)
    for i in (1, 0, 2):
        for d, block in enumerate(ends[i]):
            block = swap(block, d * group) if d else block
            out = lax.dynamic_update_slice(out, block[None, None], (i, plane ^ d, 0, 0))
    return out


def solution(mesh):
    placed = (P(None, "groups", "row", None), P(), P())
    return jax.shard_map(
        on_device,
        mesh=mesh,
        in_specs=placed,
        out_specs=P(None, "groups", "row", None),
        check_vma=False,
    )
```

```python
import functools

import jax
import jax.numpy as jnp
from jax import lax
from jax.experimental import pallas as pl
from jax.experimental.pallas import tpu as pltpu
from jax.sharding import PartitionSpec as P

viscosity = 0.2
power_input = 2.0
time_step = 0.5
first_weight = 8.0 / 15.0
second_weight = 5.0 / 12.0
back_weight = 17.0 / 60.0

BF16 = jnp.bfloat16
F32 = jnp.float32
VMEM_BYTES = 50 * 1024 * 1024


def halves(x):
    high = x.astype(BF16)
    return high, (x - high.astype(F32)).astype(BF16)


def product(a, b):
    return jnp.dot(a, b, preferred_element_type=F32)


def params():
    return pltpu.CompilerParams(vmem_limit_bytes=VMEM_BYTES)


def matrices_kernel(count, order_ref, own_ref, *refs):
    slope_parts, curve_parts = refs[:count], refs[count:2 * count]
    slope_ref, curve_ref, along_x_ref, along_y_ref, turned = refs[2 * count:]
    size = slope_parts[0].shape[0]
    for place, ref, scale in ((0, slope_ref, -0.5), (2, curve_ref, viscosity)):
        high, low = halves(ref[...] * scale)
        along_x_ref[place] = high
        along_x_ref[place + 1] = low
    for high_place, low_place, parts, scale in ((1, 0, slope_parts, -0.5), (2, 3, curve_parts, viscosity)):
        turned[...] = jnp.concatenate([part[...] for part in parts], axis=0).T
        for block in range(along_y_ref.shape[1] // size):
            source = pl.ds(pl.multiple_of(own_ref[block] * size, size), size)
            high, low = halves(turned[source, :] * scale)
            along_y_ref[high_place, block * size:(block + 1) * size, :] = high
            along_y_ref[low_place, block * size:(block + 1) * size, :] = low


def prepare_matrices(order, own, slope_matrix, curve_matrix, size):
    length = slope_matrix.shape[0]
    width = min(128, length)
    count = width // size
    kept = own.shape[0] * size

    def part(place):
        return pl.BlockSpec((size, length), lambda j, order_ref, own_ref: (order_ref[count * j + place], 0))

    parts = [part(place) for place in range(count)]
    straight = pl.BlockSpec((width, length), lambda j, order_ref, own_ref: (j, 0))
    return pl.pallas_call(
        functools.partial(matrices_kernel, count),
        grid_spec=pltpu.PrefetchScalarGridSpec(
            num_scalar_prefetch=2,
            grid=(length // width,),
            in_specs=parts + parts + [straight, straight],
            out_specs=[
                pl.BlockSpec((4, width, length), lambda j, order_ref, own_ref: (0, j, 0)),
                pl.BlockSpec((4, kept, width), lambda j, order_ref, own_ref: (0, 0, j)),
            ],
            scratch_shapes=[pltpu.VMEM((length, width), F32)],
        ),
        out_shape=[
            jax.ShapeDtypeStruct((4, length, length), BF16),
            jax.ShapeDtypeStruct((4, kept, length), BF16),
        ],
        compiler_params=params(),
        cost_estimate=pl.CostEstimate(flops=16 * length ** 3, bytes_accessed=32 * length * length, transcendentals=0),
    )(order, own, *([slope_matrix] * count), *([curve_matrix] * count), slope_matrix, curve_matrix)


def piece_spec(piece, width, column):
    _, component, rows = piece
    if component is None:
        return pl.BlockSpec((rows, width), lambda n: (0, column(n)))
    return pl.BlockSpec((None, rows, width), lambda n: (component, 0, column(n)))


def joined(refs, columns=slice(None)):
    return jnp.concatenate([ref[:, columns] for ref in refs], axis=0)


def pack_kernel(holds_squares, plane_ref, velocity_ref, squares_ref, *block_refs):
    components, planes, size, length = velocity_ref.shape
    plane = plane_ref[0]
    velocity = velocity_ref[...].reshape(components * planes * size // 8, 8, length)
    squares = jnp.sum(velocity * velocity, axis=0)
    squares_ref[...] = squares
    for i in range(components):
        for d in range(planes):
            ref = block_refs[i * planes + d]
            ref[0:size, :] = velocity_ref[i, plane ^ d]
            if i == holds_squares and d:
                ref[size:, :] = squares


def pack(plane, velocity, holds_squares):
    components, planes, size, length = velocity.shape
    whole = lambda *shape: pl.BlockSpec(shape, lambda n, plane_ref: (0,) * len(shape))
    shapes = [(8, length)]
    for i in range(components):
        for d in range(planes):
            shapes.append((size + (8 if i == holds_squares and d else 0), length))
    squares, *blocks = pl.pallas_call(
        functools.partial(pack_kernel, holds_squares),
        grid_spec=pltpu.PrefetchScalarGridSpec(
            num_scalar_prefetch=1,
            grid=(1,),
            in_specs=[whole(*velocity.shape)],
            out_specs=[whole(*shape) for shape in shapes],
        ),
        out_shape=[jax.ShapeDtypeStruct(shape, F32) for shape in shapes],
        compiler_params=params(),
        name="pack",
    )(plane.reshape(1).astype(jnp.int32), velocity)
    own = [blocks[i * planes] for i in range(components)]
    return own, squares, [blocks[i * planes + 1:(i + 1) * planes] for i in range(components)]


def join_kernel(size, extra, *refs):
    out_ref = refs[-1]
    blocks = refs[:-1]
    if extra:
        *blocks, squares_ref = blocks
        squares = squares_ref[...]
        for ref in blocks[1:]:
            squares = squares + ref[size:, :]
        out_ref[len(blocks) * size:, :] = squares
    for place, ref in enumerate(blocks):
        out_ref[place * size:(place + 1) * size, :] = ref[0:size, :]


def join(blocks, size, squares=None):
    extra = [] if squares is None else [squares]
    rows = len(blocks) * size + (8 if extra else 0)
    return pl.pallas_call(
        functools.partial(join_kernel, size, len(extra)),
        out_shape=jax.ShapeDtypeStruct((rows, blocks[0].shape[1]), F32),
        compiler_params=params(),
        name="join",
    )(*blocks, *extra)


def along_x_kernel(counts, *refs):
    fields, carriers, _, (matrix_ref, out_ref, stack) = cut(refs, counts)
    rows = out_ref.shape[0]
    carriers = carriers or fields

    @pl.when(pl.program_id(0) == 0)
    def _():
        field = joined(fields)
        high, low = halves(field)
        stack[0:rows] = low
        stack[rows:2 * rows] = high
        high, low = halves(joined(carriers) * field)
        stack[2 * rows:3 * rows] = high
        stack[3 * rows:4 * rows] = low

    tile = out_ref.shape[1]
    columns = pl.ds(pl.multiple_of(pl.program_id(0) * tile, tile), tile)
    a = product(stack[...], matrix_ref[0])
    b = product(stack[rows:3 * rows], matrix_ref[1])
    c = product(stack[0:2 * rows], matrix_ref[2])
    d = product(stack[rows:2 * rows], matrix_ref[3])
    slope = a[0:rows] + a[rows:2 * rows] + b[0:rows]
    rest = a[2 * rows:3 * rows] + a[3 * rows:] + b[rows:] + c[0:rows] + c[rows:] + d
    out_ref[...] = joined(carriers, columns) * slope + rest


def along_x(fields, carriers, matrix, name):
    rows, length = sum(piece[2] for piece in fields), fields[0][0].shape[-1]
    tile = min(256, length)
    pieces = fields + carriers
    return pl.pallas_call(
        functools.partial(along_x_kernel, (len(fields), len(carriers), 0)),
        grid=(length // tile,),
        in_specs=[piece_spec(piece, length, lambda n: 0) for piece in pieces]
        + [pl.BlockSpec((4, length, tile), lambda n: (0, 0, n))],
        out_specs=pl.BlockSpec((rows, tile), lambda n: (0, n)),
        out_shape=jax.ShapeDtypeStruct((rows, length), F32),
        scratch_shapes=[pltpu.VMEM((4 * rows, length), BF16)],
        compiler_params=params(),
        cost_estimate=pl.CostEstimate(
            flops=36 * rows * length * length, bytes_accessed=4 * rows * length, transcendentals=0
        ),
        name=name,
    )(*[piece[0] for piece in pieces], matrix)


def y_products(matrix_ref, own, fields, carriers):
    rows, length = matrix_ref.shape[1:]
    field = joined(fields)
    carrier = joined(carriers) if carriers else field
    field_high, field_low = halves(field)
    flux_high, flux_low = halves(field * carrier)
    matrix = matrix_ref[...].reshape(4 * rows, length)
    a = product(matrix, field_high)
    b = product(matrix[rows:3 * rows], field_low)
    c = product(matrix[0:2 * rows], flux_high)
    d = product(matrix[rows:2 * rows], flux_low)
    slope = a[0:rows] + a[rows:2 * rows] + b[0:rows]
    rest = a[2 * rows:3 * rows] + a[3 * rows:] + b[rows:] + c[0:rows] + c[rows:] + d
    return own[1][...] * slope + rest


def first_kernel(counts, forcing_ref, matrix_ref, *refs):
    own, fields, carriers, (x_ref, middle_ref, base_ref, square_ref) = cut(refs, counts)
    rows = matrix_ref.shape[1]
    field = own[0][...]
    first = y_products(matrix_ref, own, fields, carriers) + x_ref[...] + forcing_ref[0, 0] * field
    middle = field + (time_step * first_weight) * first
    middle_ref[...] = middle
    base_ref[...] = middle - (time_step * back_weight) * first
    square_ref[...] = jnp.sum((middle * middle).reshape(rows // 8, 8, middle.shape[1]), axis=0)


def second_kernel(counts, forcing_ref, matrix_ref, *refs):
    own, fields, carriers, (x_ref, base_ref, *out_refs) = cut(refs, counts)
    second = y_products(matrix_ref, own, fields, carriers) + x_ref[...] + forcing_ref[0, 0] * own[0][...]
    out = base_ref[...] + (time_step * second_weight) * second
    size = out_refs[0].shape[0]
    for place, out_ref in enumerate(out_refs):
        out_ref[...] = out[place * size:(place + 1) * size]


def cut(refs, counts):
    pieces, start = [], 0
    for count in counts:
        pieces.append(refs[start:start + count])
        start += count
    return *pieces, refs[start:]


def y_call(kernel, rows, matrix, own, fields, carriers, rest, out_rows, forcing, name):
    length = fields[0][0].shape[-1]
    tile = min(256, length)
    columns = lambda count: pl.BlockSpec((count, tile), lambda n: (0, n))
    pieces = own + fields + carriers + [(x, None, rows) for x in rest]
    return pl.pallas_call(
        functools.partial(kernel, (len(own), len(fields), len(carriers))),
        grid=(length // tile,),
        in_specs=[
            pl.BlockSpec(memory_space=pltpu.SMEM),
            pl.BlockSpec((4, rows, length), lambda n: (0, 0, 0)),
            *[piece_spec(piece, tile, lambda n: n) for piece in pieces],
        ],
        out_specs=[columns(count) for count in out_rows],
        out_shape=[jax.ShapeDtypeStruct((count, length), F32) for count in out_rows],
        compiler_params=params(),
        cost_estimate=pl.CostEstimate(
            flops=36 * rows * length * length, bytes_accessed=4 * rows * length, transcendentals=0
        ),
        name=name,
    )(forcing, matrix, *[piece[0] for piece in pieces])


def after(values, *earlier):
    return lax.optimization_barrier((values, earlier))[0]


def on_device(velocity, slope_matrix, curve_matrix):
    planes, size, length = velocity.shape[1:]
    devices = lax.axis_size("row")
    group = devices // planes
    chips = group // 2
    kept = length // group
    place = lax.axis_index("row")
    plane, member = place // group, place % group
    cells = 3 * planes * size * devices * length

    def swap(x, distance):
        return lax.ppermute(x, "row", [(r, r ^ distance) for r in range(devices)])

    def swap_sum(x, distances):
        for distance in distances:
            x = x + swap(x, distance)
        return x

    def doubling(start, stop):
        return [start << step for step in range((stop // start).bit_length() - 1)]

    def forcing_of(total):
        return (power_input / (jnp.sum(total) / cells)).reshape(1, 1)

    def send(blocks):
        return [swap(block, d * group) for d, block in enumerate(blocks, 1)]

    members = [[g * group + m for m in range(group)] for g in range(planes)]

    def gathered(x):
        return lax.all_gather(x, "row", axis_index_groups=members, axis=0)

    def whole_pieces(x):
        return [(x, m, kept) for m in range(group)]

    order = jnp.stack([(plane ^ d) * group + m for m in range(group) for d in range(planes)]).astype(jnp.int32)
    own_order = jnp.stack([(plane ^ d) * group + member for d in range(planes)]).astype(jnp.int32)

    own, squares, blocks = pack(plane, velocity, 1)
    arriving = [None] * 3
    for i in (1, 0, 2):
        arriving[i] = send(blocks[i])
    along_x_matrix, along_y_matrix = prepare_matrices(order, own_order, slope_matrix, curve_matrix, size)

    def own_pieces(i):
        return (near[i], None, kept)

    x_terms, near, whole = [None] * 3, [None] * 3, [None] * 3
    arriving[1] = after(arriving[1], along_x_matrix, along_y_matrix)
    near[1] = join([own[1]] + arriving[1], size, squares)
    whole[1] = gathered(near[1])
    near[0] = join([own[0]] + arriving[0], size)
    whole[0] = gathered(near[0])
    x_terms[1] = along_x([own_pieces(1)], [own_pieces(0)], along_x_matrix, "x_first_1")
    forcing = forcing_of(whole[1][:, kept:])

    def first_step(i):
        return y_call(
            first_kernel, kept, along_y_matrix, [own_pieces(i), own_pieces(1)], whole_pieces(whole[i]),
            whole_pieces(whole[1]) if i != 1 else [], [x_terms[i]], [kept, kept, 8], forcing, f"y_first_{i}",
        )

    middle, base, square, middle_whole = [None] * 3, [None] * 3, [None] * 3, [None] * 3
    middle[1], base[1], square[1] = first_step(1)
    x_terms[0] = along_x([(after(near[0], middle[1]), None, kept)], [], along_x_matrix, "x_first_0")
    arriving[2] = after(arriving[2], x_terms[0])
    near[2] = join([own[2]] + arriving[2], size)
    whole[2] = gathered(near[2])
    middle_whole[1] = gathered(after(middle[1], near[2]))
    whole[0] = after(whole[0], near[2])
    middle[0], base[0], square[0] = first_step(0)
    x_terms[2] = along_x([(after(near[2], middle[0]), None, kept)], [own_pieces(0)], along_x_matrix, "x_first_2")
    whole[2] = after(whole[2], x_terms[2])
    middle[2], base[2], square[2] = first_step(2)

    total = jnp.sum((square[0] + square[1] + square[2]).reshape(8, length // 128, 128), axis=1)
    total = swap_sum(total, doubling(group, devices) + doubling(1, group))
    forcing = forcing_of(total)

    def piece(x):
        return (x, None, kept)

    x_terms[1] = along_x([piece(after(middle[1], square[2]))], [piece(middle[0])], along_x_matrix, "x_second_1")
    middle_whole[1] = after(middle_whole[1], x_terms[1])
    middle_whole[0] = gathered(middle[0])

    def second_step(i):
        return y_call(
            second_kernel, kept, along_y_matrix, [piece(middle[i]), piece(middle[1])], whole_pieces(middle_whole[i]),
            whole_pieces(middle_whole[1]) if i != 1 else [], [x_terms[i], base[i]], [size] * planes, forcing,
            f"y_second_{i}",
        )

    ends = [None] * 3
    ends[1] = second_step(1)
    x_terms[0] = along_x([piece(after(middle[0], ends[1]))], [], along_x_matrix, "x_second_0")
    middle_whole[2] = gathered(middle[2])
    middle_whole[0] = after(middle_whole[0], x_terms[0])
    ends[0] = second_step(0)
    x_terms[2] = along_x([piece(after(middle[2], ends[0]))], [piece(middle[0])], along_x_matrix, "x_second_2")
    middle_whole[2] = after(middle_whole[2], x_terms[2])
    ends[2] = second_step(2)

    out = jnp.zeros(velocity.shape, F32)
    for i in (1, 0, 2):
        for d, block in enumerate(ends[i]):
            block = swap(block, d * group) if d else block
            out = lax.dynamic_update_slice(out, block[None, None], (i, plane ^ d, 0, 0))
    return out


def solution(mesh):
    placed = (P(None, "groups", "row", None), P(), P())
    return jax.shard_map(
        on_device,
        mesh=mesh,
        in_specs=placed,
        out_specs=P(None, "groups", "row", None),
        check_vma=False,
    )
```

```python
import functools

import jax
import jax.numpy as jnp
from jax import lax
from jax.experimental import pallas as pl
from jax.experimental.pallas import tpu as pltpu
from jax.sharding import PartitionSpec as P

viscosity = 0.2
power_input = 2.0
time_step = 0.5
first_weight = 8.0 / 15.0
second_weight = 5.0 / 12.0
back_weight = 17.0 / 60.0

BF16 = jnp.bfloat16
F32 = jnp.float32
VMEM_BYTES = 50 * 1024 * 1024


def halves(x):
    high = x.astype(BF16)
    return high, (x - high.astype(F32)).astype(BF16)


def product(a, b):
    return jnp.dot(a, b, preferred_element_type=F32)


def params():
    return pltpu.CompilerParams(vmem_limit_bytes=VMEM_BYTES)


def matrices_kernel(count, order_ref, own_ref, *refs):
    slope_parts, curve_parts = refs[:count], refs[count:2 * count]
    slope_ref, curve_ref, along_x_ref, along_y_ref, turned = refs[2 * count:]
    size = slope_parts[0].shape[0]
    for place, ref, scale in ((0, slope_ref, -0.5), (2, curve_ref, viscosity)):
        high, low = halves(ref[...] * scale)
        along_x_ref[place] = high
        along_x_ref[place + 1] = low
    for high_place, low_place, parts, scale in ((1, 0, slope_parts, -0.5), (2, 3, curve_parts, viscosity)):
        turned[...] = jnp.concatenate([part[...] for part in parts], axis=0).T
        for block in range(along_y_ref.shape[1] // size):
            source = pl.ds(pl.multiple_of(own_ref[block] * size, size), size)
            high, low = halves(turned[source, :] * scale)
            along_y_ref[high_place, block * size:(block + 1) * size, :] = high
            along_y_ref[low_place, block * size:(block + 1) * size, :] = low


def prepare_matrices(order, own, slope_matrix, curve_matrix, size):
    length = slope_matrix.shape[0]
    width = min(128, length)
    count = width // size
    kept = own.shape[0] * size

    def part(place):
        return pl.BlockSpec((size, length), lambda j, order_ref, own_ref: (order_ref[count * j + place], 0))

    parts = [part(place) for place in range(count)]
    straight = pl.BlockSpec((width, length), lambda j, order_ref, own_ref: (j, 0))
    return pl.pallas_call(
        functools.partial(matrices_kernel, count),
        grid_spec=pltpu.PrefetchScalarGridSpec(
            num_scalar_prefetch=2,
            grid=(length // width,),
            in_specs=parts + parts + [straight, straight],
            out_specs=[
                pl.BlockSpec((4, width, length), lambda j, order_ref, own_ref: (0, j, 0)),
                pl.BlockSpec((4, kept, width), lambda j, order_ref, own_ref: (0, 0, j)),
            ],
            scratch_shapes=[pltpu.VMEM((length, width), F32)],
        ),
        out_shape=[
            jax.ShapeDtypeStruct((4, length, length), BF16),
            jax.ShapeDtypeStruct((4, kept, length), BF16),
        ],
        compiler_params=params(),
        cost_estimate=pl.CostEstimate(flops=16 * length ** 3, bytes_accessed=32 * length * length, transcendentals=0),
    )(order, own, *([slope_matrix] * count), *([curve_matrix] * count), slope_matrix, curve_matrix)


def piece_spec(piece, width, column):
    _, place, rows = piece
    return pl.BlockSpec((rows, width), lambda n: (place, column(n)))


def joined(refs, columns=slice(None)):
    return jnp.concatenate([ref[:, columns] for ref in refs], axis=0)


def cut(refs, counts):
    pieces, start = [], 0
    for count in counts:
        pieces.append(refs[start:start + count])
        start += count
    return *pieces, refs[start:]


def pack_kernel(plane_ref, velocity_ref, *block_refs):
    components, planes, size, length = velocity_ref.shape
    plane = plane_ref[0]
    velocity = velocity_ref[...].reshape(components * planes * size // 8, 8, length)
    squares = jnp.sum(velocity * velocity, axis=0)
    for d, ref in enumerate(block_refs):
        for i in range(components):
            ref[i * size:(i + 1) * size, :] = velocity_ref[i, plane ^ d]
        ref[components * size:, :] = squares


def pack(plane, velocity):
    components, planes, size, length = velocity.shape
    shape = (components * size + 8, length)
    return pl.pallas_call(
        pack_kernel,
        grid_spec=pltpu.PrefetchScalarGridSpec(
            num_scalar_prefetch=1,
            grid=(1,),
            in_specs=[pl.BlockSpec(velocity.shape, lambda n, plane_ref: (0, 0, 0, 0))],
            out_specs=[pl.BlockSpec(shape, lambda n, plane_ref: (0, 0))] * planes,
        ),
        out_shape=[jax.ShapeDtypeStruct(shape, F32)] * planes,
        compiler_params=params(),
        name="pack",
    )(plane.reshape(1).astype(jnp.int32), velocity)


def along_x_kernel(counts, copies, *refs):
    fields, carriers, (matrix_ref, out_ref, stack) = cut(refs, counts)
    rows = out_ref.shape[0]
    carriers = (carriers or fields) * copies

    @pl.when(pl.program_id(0) == 0)
    def _():
        field = joined(fields)
        high, low = halves(field)
        stack[0:rows] = low
        stack[rows:2 * rows] = high
        high, low = halves(joined(carriers) * field)
        stack[2 * rows:3 * rows] = high
        stack[3 * rows:4 * rows] = low

    tile = out_ref.shape[1]
    columns = pl.ds(pl.multiple_of(pl.program_id(0) * tile, tile), tile)
    a = product(stack[...], matrix_ref[0])
    b = product(stack[rows:3 * rows], matrix_ref[1])
    c = product(stack[0:2 * rows], matrix_ref[2])
    d = product(stack[rows:2 * rows], matrix_ref[3])
    slope = a[0:rows] + a[rows:2 * rows] + b[0:rows]
    rest = a[2 * rows:3 * rows] + a[3 * rows:] + b[rows:] + c[0:rows] + c[rows:] + d
    out_ref[...] = joined(carriers, columns) * slope + rest


def along_x(fields, carriers, matrix, name, weight=36):
    rows, length = sum(piece[2] for piece in fields), fields[0][0].shape[1]
    copies = len(fields) // len(carriers) if carriers else 1
    tile = min(256, length)
    pieces = fields + carriers
    return pl.pallas_call(
        functools.partial(along_x_kernel, (len(fields), len(carriers)), copies),
        grid=(length // tile,),
        in_specs=[piece_spec(piece, length, lambda n: 0) for piece in pieces]
        + [pl.BlockSpec((4, length, tile), lambda n: (0, 0, n))],
        out_specs=pl.BlockSpec((rows, tile), lambda n: (0, n)),
        out_shape=jax.ShapeDtypeStruct((rows, length), F32),
        scratch_shapes=[pltpu.VMEM((4 * rows, length), BF16)],
        compiler_params=params(),
        cost_estimate=pl.CostEstimate(
            flops=weight * rows * length * length, bytes_accessed=4 * rows * length, transcendentals=0
        ),
        name=name,
    )(*[piece[0] for piece in pieces], matrix)


def y_sums(matrix_ref, fields, carriers, sums):
    rows, length = matrix_ref.shape[1:]
    field = joined(fields)
    carrier = joined(carriers) if carriers else field
    field_high, field_low = halves(field)
    flux_high, flux_low = halves(field * carrier)
    matrix = matrix_ref[...].reshape(4 * rows, length)
    a = product(matrix, field_high)
    b = product(matrix[rows:3 * rows], field_low)
    c = product(matrix[0:2 * rows], flux_high)
    d = product(matrix[rows:2 * rows], flux_low)
    slope = a[0:rows] + a[rows:2 * rows] + b[0:rows]
    rest = a[2 * rows:3 * rows] + a[3 * rows:] + b[rows:] + c[0:rows] + c[rows:] + d
    if sums:
        slope, rest = slope + sums[0][...], rest + sums[1][...]
    return slope, rest


def partial_kernel(counts, matrix_ref, *refs):
    fields, carriers, sums, (slope_ref, rest_ref) = cut(refs, counts)
    slope_ref[...], rest_ref[...] = y_sums(matrix_ref, fields, carriers, sums)


def tendency(forcing_ref, field, carrier, x_terms, sums):
    return joined(x_terms) + joined(carrier) * sums[0] + sums[1] + forcing_ref[0, 0] * field


def first_kernel(counts, forcing_ref, matrix_ref, *refs):
    fields, carriers, sums, own, own_carrier, x_terms, (middle_ref, base_ref, square_ref) = cut(refs, counts)
    rows = matrix_ref.shape[1]
    field = joined(own)
    first = tendency(forcing_ref, field, own_carrier, x_terms, y_sums(matrix_ref, fields, carriers, sums))
    middle = field + (time_step * first_weight) * first
    middle_ref[...] = middle
    base_ref[...] = middle - (time_step * back_weight) * first
    square_ref[...] = jnp.sum((middle * middle).reshape(rows // 8, 8, middle.shape[1]), axis=0)


def second_kernel(counts, forcing_ref, matrix_ref, *refs):
    fields, carriers, sums, own, own_carrier, x_terms, (base_ref, *out_refs) = cut(refs, counts)
    field = joined(own)
    second = tendency(forcing_ref, field, own_carrier, x_terms, y_sums(matrix_ref, fields, carriers, sums))
    out = base_ref[...] + (time_step * second_weight) * second
    size = out_refs[0].shape[0]
    for place, out_ref in enumerate(out_refs):
        out_ref[...] = out[place * size:(place + 1) * size]


def y_call(kernel, forcing, matrix, part, groups, out_rows, name, weight=36):
    rows, length = matrix.shape[1], groups[0][0][0].shape[1]
    depth = sum(piece[2] for piece in groups[0])
    tile = min(256, length)
    pieces = [piece for group in groups for piece in group]
    return pl.pallas_call(
        functools.partial(kernel, tuple(len(group) for group in groups[:6])),
        grid=(length // tile,),
        in_specs=[pl.BlockSpec(memory_space=pltpu.SMEM)] * len(forcing)
        + [pl.BlockSpec((4, rows, depth), lambda n: (0, 0, part))]
        + [piece_spec(piece, tile, lambda n: n) for piece in pieces],
        out_specs=[pl.BlockSpec((count, tile), lambda n: (0, n)) for count in out_rows],
        out_shape=[jax.ShapeDtypeStruct((count, length), F32) for count in out_rows],
        compiler_params=params(),
        cost_estimate=pl.CostEstimate(
            flops=weight * rows * depth * length, bytes_accessed=4 * rows * length, transcendentals=0
        ),
        name=name,
    )(*forcing, matrix, *[piece[0] for piece in pieces])


def after(values, *earlier):
    return lax.optimization_barrier((values, earlier))[0]


def on_device(velocity, slope_matrix, curve_matrix):
    components, planes, size, length = velocity.shape
    devices = lax.axis_size("row")
    group = devices // planes
    chips = group // 2
    kept = length // group
    place = lax.axis_index("row")
    plane, member = place // group, place % group
    cells = components * planes * size * devices * length
    parts = [range(planes // 2), range(planes // 2, planes)]

    def swap(x, distance):
        return lax.ppermute(x, "row", [(r, r ^ distance) for r in range(devices)])

    def swap_sum(x, distances):
        for distance in distances:
            x = x + swap(x, distance)
        return x

    def doubling(start, stop):
        return [start << step for step in range((stop // start).bit_length() - 1)]

    def forcing_of(total):
        return (power_input / (jnp.sum(total) / cells)).reshape(1, 1)

    def across_chips(x):
        return [swap(x, 2 * h) for h in range(1, chips)]

    def across_cores(pieces):
        return [swap(piece, 1) for piece in pieces]

    order = jnp.stack([
        (plane ^ d) * group + (member ^ (2 * h + core))
        for part in parts for h in range(chips) for core in range(2) for d in part
    ]).astype(jnp.int32)
    own_order = jnp.stack([(plane ^ d) * group + member for d in range(planes)]).astype(jnp.int32)

    here, others, twins, fars = [None] * planes, [None] * planes, [None] * planes, [None] * planes

    def block_pieces(i, part):
        pieces = []
        for h in range(chips):
            for core in range(2):
                for d in parts[part]:
                    block = ([here[d]] + others[d])[h] if core == 0 else (twins[d] + fars[d])[h]
                    pieces.append((block, i, size))
        return pieces

    def here_pieces(i, distances):
        return [(here[d], i, size) for d in distances]

    def x_first(distances, name, weight=36):
        fields = [piece for i in range(components) for piece in here_pieces(i, distances)]
        return along_x(fields, here_pieces(0, distances), along_x_matrix, name, weight)

    blocks = list(pack(plane, velocity))
    here[0] = blocks[0]
    for d in parts[0][1:]:
        here[d] = swap(blocks[d], d * group)
    for d in parts[1][:-1]:
        here[d] = swap(blocks[d], d * group)
    others[0] = across_chips(here[0])
    along_x_matrix, along_y_matrix = prepare_matrices(order, own_order, slope_matrix, curve_matrix, size)

    for d in parts[0][1:]:
        here[d] = after(here[d], along_x_matrix, along_y_matrix)
        others[d] = across_chips(here[d])
    here[planes - 1] = swap(after(blocks[-1], here[1]), (planes - 1) * group)
    last = planes - 1
    x_terms = [x_first(parts[0], "x_first_near")]
    for d in parts[0]:
        twins[d] = across_cores([after(here[d], x_terms[0])])
    for d in parts[1][:-1]:
        here[d] = after(here[d], x_terms[0])
        others[d] = across_chips(here[d])
        x_terms.append(x_first([d], f"x_first_{d}"))
    for d in parts[0]:
        others[d] = after(others[d], x_terms[-1])
        fars[d] = across_cores(others[d])
    here[last] = after(here[last], x_terms[-1], [twins[d] for d in parts[0]])
    others[last] = across_chips(here[last])
    x_terms.append(x_first([last], f"x_first_{last}"))

    sums, previous = [None] * 3, x_terms[-1]
    for i in (1, 0, 2):
        fields = block_pieces(i, 0)
        fields = [(after(fields[0][0], previous), *fields[0][1:])] + fields[1:]
        sums[i] = y_call(
            partial_kernel, [], along_y_matrix, 0, [fields, block_pieces(1, 0) if i != 1 else [], []],
            [kept, kept], f"y_first_near_{i}",
        )
        previous = sums[i]
    for d in parts[1][:-1]:
        twins[d] = across_cores([after(here[d], sums[1])])
        others[d] = after(others[d], sums[1])
        fars[d] = across_cores(others[d])
    twins[last] = across_cores([after(here[last], sums[0])])
    others[last] = after(others[last], sums[2])
    fars[last] = across_cores(others[last])
    forcing = [forcing_of(sum(
        block[components * size:] for d in range(planes) for block in [here[d]] + others[d] + twins[d] + fars[d]
    ))]

    middle, base, square = [None] * 3, [None] * 3, [None] * 3
    middle_others, middle_twin, middle_far = [None] * 3, [None] * 3, [None] * 3

    def piece(x):
        return (x, 0, x.shape[0])

    for i in (1, 0, 2):
        fields = block_pieces(i, 1)
        fields = [(after(fields[0][0], previous), *fields[0][1:])] + fields[1:]
        own = here_pieces(i, range(planes))
        terms = [(x_terms[0], i, len(parts[0]) * size)] + [(x, i, size) for x in x_terms[1:]]
        middle[i], base[i], square[i] = y_call(
            first_kernel, forcing, along_y_matrix, 1,
            [fields, block_pieces(1, 1) if i != 1 else [], [piece(x) for x in sums[i]], own,
             here_pieces(1, range(planes)), terms], [kept, kept, 8], f"y_first_far_{i}",
        )
        previous = middle[i]
        if i == 1:
            middle_others[1] = across_chips(middle[1])
            middle_twin[1] = across_cores([middle[1]])

    total = jnp.sum((square[0] + square[1] + square[2]).reshape(8, length // 128, 128), axis=1)
    total = swap_sum(total, doubling(group, devices) + [1])
    middle_twin[0] = across_cores([after(middle[0], square[2])])
    middle_twin[2] = across_cores([middle[2]])
    x_terms = [None] * 3
    x_terms[1] = along_x([piece(after(middle[1], total))], [piece(middle[0])], along_x_matrix, "x_second_1")
    middle_others[1] = after(middle_others[1], x_terms[1])
    total = after(swap_sum(total, doubling(2, group)), middle_others[1], middle_twin[0], middle_twin[2])
    middle_others[0] = across_chips(after(middle[0], total))
    middle_others[2] = across_chips(after(middle[2], total))
    forcing = [forcing_of(total)]

    def middle_pieces(i):
        return [
            (x, part, kept // 2) for part in range(2) for pair in
            zip([middle[i]] + middle_others[i], middle_twin[i] + middle_far[i]) for x in pair
        ]

    def second_step(i):
        return y_call(
            second_kernel, forcing, along_y_matrix, 0,
            [middle_pieces(i), middle_pieces(1) if i != 1 else [], [], [piece(middle[i])], [piece(middle[1])],
             [piece(x_terms[i])], [piece(base[i])]], [size] * planes, f"y_second_{i}",
        )

    ends = [None] * 3
    middle_far[1] = across_cores(middle_others[1])
    ends[1] = second_step(1)
    x_terms[0] = along_x([piece(after(middle[0], ends[1]))], [], along_x_matrix, "x_second_0")
    middle_others[0] = after(middle_others[0], x_terms[0])
    middle_far[0] = across_cores(middle_others[0])
    x_terms[2] = along_x([piece(after(middle[2], x_terms[0]))], [piece(middle[0])], along_x_matrix, "x_second_2")
    middle_far[0] = after(middle_far[0], x_terms[2])
    ends[0] = second_step(0)
    middle_others[2] = after(middle_others[2], ends[0])
    middle_far[2] = across_cores(middle_others[2])
    ends[2] = second_step(2)

    out = jnp.zeros(velocity.shape, F32)
    for i in (1, 0, 2):
        for d, block in enumerate(ends[i]):
            block = swap(block, d * group) if d else block
            out = lax.dynamic_update_slice(out, block[None, None], (i, plane ^ d, 0, 0))
    return out


def solution(mesh):
    placed = (P(None, "groups", "row", None), P(), P())
    return jax.shard_map(
        on_device,
        mesh=mesh,
        in_specs=placed,
        out_specs=P(None, "groups", "row", None),
        check_vma=False,
    )
```

```python
import functools

import jax
import jax.numpy as jnp
from jax import lax
from jax.experimental import pallas as pl
from jax.experimental.pallas import tpu as pltpu
from jax.sharding import PartitionSpec as P

viscosity = 0.2
power_input = 2.0
time_step = 0.5
first_weight = 8.0 / 15.0
second_weight = 5.0 / 12.0
back_weight = 17.0 / 60.0

BF16 = jnp.bfloat16
F32 = jnp.float32
VMEM_BYTES = 24 * 1024 * 1024


def halves(x):
    high = x.astype(BF16)
    return high, (x - high.astype(F32)).astype(BF16)


def product(a, b):
    return jnp.dot(a, b, preferred_element_type=F32)


def params():
    return pltpu.CompilerParams(vmem_limit_bytes=VMEM_BYTES)


def matrices_kernel(count, order_ref, own_ref, *refs):
    slope_parts, curve_parts = refs[:count], refs[count:2 * count]
    slope_ref, curve_ref, along_x_ref, along_y_ref, turned = refs[2 * count:]
    size = slope_parts[0].shape[0]
    for place, ref, scale in ((0, slope_ref, -0.5), (2, curve_ref, viscosity)):
        high, low = halves(ref[...] * scale)
        along_x_ref[place] = high
        along_x_ref[place + 1] = low
    for high_place, low_place, parts, scale in ((1, 0, slope_parts, -0.5), (2, 3, curve_parts, viscosity)):
        turned[...] = jnp.concatenate([part[...] for part in parts], axis=0).T
        for block in range(along_y_ref.shape[1] // size):
            source = pl.ds(pl.multiple_of(own_ref[block] * size, size), size)
            high, low = halves(turned[source, :] * scale)
            along_y_ref[high_place, block * size:(block + 1) * size, :] = high
            along_y_ref[low_place, block * size:(block + 1) * size, :] = low


def prepare_matrices(order, own, slope_matrix, curve_matrix, size):
    length = slope_matrix.shape[0]
    width = min(128, length)
    count = width // size
    kept = own.shape[0] * size

    def part(place):
        return pl.BlockSpec((size, length), lambda j, order_ref, own_ref: (order_ref[count * j + place], 0))

    parts = [part(place) for place in range(count)]
    straight = pl.BlockSpec((width, length), lambda j, order_ref, own_ref: (j, 0))
    return pl.pallas_call(
        functools.partial(matrices_kernel, count),
        grid_spec=pltpu.PrefetchScalarGridSpec(
            num_scalar_prefetch=2,
            grid=(length // width,),
            in_specs=parts + parts + [straight, straight],
            out_specs=[
                pl.BlockSpec((4, width, length), lambda j, order_ref, own_ref: (0, j, 0)),
                pl.BlockSpec((4, kept, width), lambda j, order_ref, own_ref: (0, 0, j)),
            ],
            scratch_shapes=[pltpu.VMEM((length, width), F32)],
        ),
        out_shape=[
            jax.ShapeDtypeStruct((4, length, length), BF16),
            jax.ShapeDtypeStruct((4, kept, length), BF16),
        ],
        compiler_params=params(),
        cost_estimate=pl.CostEstimate(flops=16 * length ** 3, bytes_accessed=32 * length * length, transcendentals=0),
    )(order, own, *([slope_matrix] * count), *([curve_matrix] * count), slope_matrix, curve_matrix)


def piece_spec(piece, width, column):
    _, place, rows = piece
    return pl.BlockSpec((rows, width), lambda n: (place, column(n)))


def joined(refs, columns=slice(None)):
    return jnp.concatenate([ref[:, columns] for ref in refs], axis=0)


def cut(refs, counts):
    pieces, start = [], 0
    for count in counts:
        pieces.append(refs[start:start + count])
        start += count
    return *pieces, refs[start:]


def pack_kernel(plane_ref, velocity_ref, *block_refs):
    components, planes, size, length = velocity_ref.shape
    plane = plane_ref[0]
    velocity = velocity_ref[...].reshape(components * planes * size // 8, 8, length)
    squares = jnp.sum(velocity * velocity, axis=0)
    for d, ref in enumerate(block_refs):
        for i in range(components):
            ref[i * size:(i + 1) * size, :] = velocity_ref[i, plane ^ d]
        ref[components * size:, :] = squares


def pack(plane, velocity):
    components, planes, size, length = velocity.shape
    shape = (components * size + 8, length)
    return pl.pallas_call(
        pack_kernel,
        grid_spec=pltpu.PrefetchScalarGridSpec(
            num_scalar_prefetch=1,
            grid=(1,),
            in_specs=[pl.BlockSpec(velocity.shape, lambda n, plane_ref: (0, 0, 0, 0))],
            out_specs=[pl.BlockSpec(shape, lambda n, plane_ref: (0, 0))] * planes,
        ),
        out_shape=[jax.ShapeDtypeStruct(shape, F32)] * planes,
        compiler_params=params(),
        name="pack",
    )(plane.reshape(1).astype(jnp.int32), velocity)


def along_x_kernel(counts, copies, *refs):
    fields, carriers, (matrix_ref, out_ref, stack) = cut(refs, counts)
    rows = out_ref.shape[0]
    carriers = (carriers or fields) * copies

    @pl.when(pl.program_id(0) == 0)
    def _():
        field = joined(fields)
        high, low = halves(field)
        stack[0:rows] = low
        stack[rows:2 * rows] = high
        high, low = halves(joined(carriers) * field)
        stack[2 * rows:3 * rows] = high
        stack[3 * rows:4 * rows] = low

    tile = out_ref.shape[1]
    columns = pl.ds(pl.multiple_of(pl.program_id(0) * tile, tile), tile)
    a = product(stack[...], matrix_ref[0])
    b = product(stack[rows:3 * rows], matrix_ref[1])
    c = product(stack[0:2 * rows], matrix_ref[2])
    d = product(stack[rows:2 * rows], matrix_ref[3])
    slope = a[0:rows] + a[rows:2 * rows] + b[0:rows]
    rest = a[2 * rows:3 * rows] + a[3 * rows:] + b[rows:] + c[0:rows] + c[rows:] + d
    out_ref[...] = joined(carriers, columns) * slope + rest


def along_x(fields, carriers, matrix, name, weight=36):
    rows, length = sum(piece[2] for piece in fields), fields[0][0].shape[1]
    copies = len(fields) // len(carriers) if carriers else 1
    tile = min(256, length)
    pieces = fields + carriers
    return pl.pallas_call(
        functools.partial(along_x_kernel, (len(fields), len(carriers)), copies),
        grid=(length // tile,),
        in_specs=[piece_spec(piece, length, lambda n: 0) for piece in pieces]
        + [pl.BlockSpec((4, length, tile), lambda n: (0, 0, n))],
        out_specs=pl.BlockSpec((rows, tile), lambda n: (0, n)),
        out_shape=jax.ShapeDtypeStruct((rows, length), F32),
        scratch_shapes=[pltpu.VMEM((4 * rows, length), BF16)],
        compiler_params=params(),
        cost_estimate=pl.CostEstimate(
            flops=weight * rows * length * length, bytes_accessed=4 * rows * length, transcendentals=0
        ),
        name=name,
    )(*[piece[0] for piece in pieces], matrix)


def y_sums(matrix_ref, fields, carriers, sums):
    rows, length = matrix_ref.shape[1:]
    field = joined(fields)
    carrier = joined(carriers) if carriers else field
    field_high, field_low = halves(field)
    flux_high, flux_low = halves(field * carrier)
    matrix = matrix_ref[...].reshape(4 * rows, length)
    a = product(matrix, field_high)
    b = product(matrix[rows:3 * rows], field_low)
    c = product(matrix[0:2 * rows], flux_high)
    d = product(matrix[rows:2 * rows], flux_low)
    slope = a[0:rows] + a[rows:2 * rows] + b[0:rows]
    rest = a[2 * rows:3 * rows] + a[3 * rows:] + b[rows:] + c[0:rows] + c[rows:] + d
    if sums:
        slope, rest = slope + sums[0][...], rest + sums[1][...]
    return slope, rest


def partial_kernel(counts, matrix_ref, *refs):
    fields, carriers, sums, (slope_ref, rest_ref) = cut(refs, counts)
    slope_ref[...], rest_ref[...] = y_sums(matrix_ref, fields, carriers, sums)


def tendency(forcing_ref, field, carrier, x_terms, sums):
    return joined(x_terms) + joined(carrier) * sums[0] + sums[1] + forcing_ref[0, 0] * field


def first_kernel(counts, forcing_ref, matrix_ref, *refs):
    fields, carriers, sums, own, own_carrier, x_terms, (middle_ref, base_ref, square_ref) = cut(refs, counts)
    rows = matrix_ref.shape[1]
    field = joined(own)
    first = tendency(forcing_ref, field, own_carrier, x_terms, y_sums(matrix_ref, fields, carriers, sums))
    middle = field + (time_step * first_weight) * first
    middle_ref[...] = middle
    base_ref[...] = middle - (time_step * back_weight) * first
    square_ref[...] = jnp.sum((middle * middle).reshape(rows // 8, 8, middle.shape[1]), axis=0)


def second_kernel(counts, forcing_ref, matrix_ref, *refs):
    fields, carriers, sums, own, own_carrier, x_terms, (base_ref, *out_refs) = cut(refs, counts)
    field = joined(own)
    second = tendency(forcing_ref, field, own_carrier, x_terms, y_sums(matrix_ref, fields, carriers, sums))
    out = base_ref[...] + (time_step * second_weight) * second
    size = out_refs[0].shape[0]
    for place, out_ref in enumerate(out_refs):
        out_ref[...] = out[place * size:(place + 1) * size]


def y_call(kernel, forcing, matrix, part, groups, out_rows, name, weight=36):
    rows, length = matrix.shape[1], groups[0][0][0].shape[1]
    depth = sum(piece[2] for piece in groups[0])
    tile = min(256, length)
    pieces = [piece for group in groups for piece in group]
    return pl.pallas_call(
        functools.partial(kernel, tuple(len(group) for group in groups[:6])),
        grid=(length // tile,),
        in_specs=[pl.BlockSpec(memory_space=pltpu.SMEM)] * len(forcing)
        + [pl.BlockSpec((4, rows, depth), lambda n: (0, 0, part))]
        + [piece_spec(piece, tile, lambda n: n) for piece in pieces],
        out_specs=[pl.BlockSpec((count, tile), lambda n: (0, n)) for count in out_rows],
        out_shape=[jax.ShapeDtypeStruct((count, length), F32) for count in out_rows],
        compiler_params=params(),
        cost_estimate=pl.CostEstimate(
            flops=weight * rows * depth * length, bytes_accessed=4 * rows * length, transcendentals=0
        ),
        name=name,
    )(*forcing, matrix, *[piece[0] for piece in pieces])


def after(values, *earlier):
    return lax.optimization_barrier((values, earlier))[0]


def on_device(velocity, slope_matrix, curve_matrix):
    components, planes, size, length = velocity.shape
    devices = lax.axis_size("row")
    group = devices // planes
    chips = group // 2
    kept = length // group
    place = lax.axis_index("row")
    plane, member = place // group, place % group
    cells = components * planes * size * devices * length
    parts = [range(planes // 2), range(planes // 2, planes)]

    def swap(x, distance):
        return lax.ppermute(x, "row", [(r, r ^ distance) for r in range(devices)])

    def swap_sum(x, distances):
        for distance in distances:
            x = x + swap(x, distance)
        return x

    def doubling(start, stop):
        return [start << step for step in range((stop // start).bit_length() - 1)]

    def forcing_of(total):
        return (power_input / (jnp.sum(total) / cells)).reshape(1, 1)

    def across_chips(x):
        return [swap(x, 2 * h) for h in range(1, chips)]

    def across_cores(pieces):
        return [swap(piece, 1) for piece in pieces]

    order = jnp.stack([
        (plane ^ d) * group + (member ^ (2 * h + core))
        for part in parts for h in range(chips) for core in range(2) for d in part
    ]).astype(jnp.int32)
    own_order = jnp.stack([(plane ^ d) * group + member for d in range(planes)]).astype(jnp.int32)

    here, others, twins, fars = [None] * planes, [None] * planes, [None] * planes, [None] * planes

    def block_pieces(i, part):
        pieces = []
        for h in range(chips):
            for core in range(2):
                for d in parts[part]:
                    block = ([here[d]] + others[d])[h] if core == 0 else (twins[d] + fars[d])[h]
                    pieces.append((block, i, size))
        return pieces

    def here_pieces(i, distances):
        return [(here[d], i, size) for d in distances]

    def x_first(distances, name, weight=36):
        fields = [piece for i in range(components) for piece in here_pieces(i, distances)]
        return along_x(fields, here_pieces(0, distances), along_x_matrix, name, weight)

    blocks = list(pack(plane, velocity))
    here[0] = blocks[0]
    for d in parts[0][1:]:
        here[d] = swap(blocks[d], d * group)
    for d in parts[1][:-1]:
        here[d] = swap(blocks[d], d * group)
    others[0] = across_chips(here[0])
    along_x_matrix, along_y_matrix = prepare_matrices(order, own_order, slope_matrix, curve_matrix, size)

    for d in parts[0][1:]:
        here[d] = after(here[d], along_x_matrix, along_y_matrix)
        others[d] = across_chips(here[d])
    here[planes - 1] = swap(blocks[-1], (planes - 1) * group)
    last = planes - 1
    x_terms = [x_first(parts[0], "x_first_near", 1)]
    for d in parts[0]:
        twins[d] = across_cores([after(here[d], x_terms[0])])
    for d in parts[1][:-1]:
        here[d] = after(here[d], x_terms[0])
        others[d] = across_chips(here[d])
        x_terms.append(x_first([d], f"x_first_{d}", 1))
    for d in parts[0]:
        others[d] = after(others[d], x_terms[-1])
        fars[d] = across_cores(others[d])
    here[last] = after(here[last], x_terms[-1], [twins[d] for d in parts[0]])
    others[last] = across_chips(here[last])
    x_terms.append(x_first([last], f"x_first_{last}"))

    sums, previous = [None] * 3, x_terms[-1]
    for i in (1, 0, 2):
        fields = block_pieces(i, 0)
        fields = [(after(fields[0][0], previous), *fields[0][1:])] + fields[1:]
        sums[i] = y_call(
            partial_kernel, [], along_y_matrix, 0, [fields, block_pieces(1, 0) if i != 1 else [], []],
            [kept, kept], f"y_first_near_{i}",
        )
        previous = sums[i]
    for d in parts[1][:-1]:
        twins[d] = across_cores([after(here[d], sums[1])])
        others[d] = after(others[d], sums[1])
        fars[d] = across_cores(others[d])
    twins[last] = across_cores([after(here[last], sums[0])])
    others[last] = after(others[last], sums[2])
    fars[last] = across_cores(others[last])
    forcing = [forcing_of(sum(
        block[components * size:] for d in range(planes) for block in [here[d]] + others[d] + twins[d] + fars[d]
    ))]

    middle, base, square = [None] * 3, [None] * 3, [None] * 3
    middle_others, middle_twin, middle_far = [None] * 3, [None] * 3, [None] * 3

    def piece(x):
        return (x, 0, x.shape[0])

    for i in (1, 0, 2):
        fields = block_pieces(i, 1)
        fields = [(after(fields[0][0], previous), *fields[0][1:])] + fields[1:]
        own = here_pieces(i, range(planes))
        terms = [(x_terms[0], i, len(parts[0]) * size)] + [(x, i, size) for x in x_terms[1:]]
        middle[i], base[i], square[i] = y_call(
            first_kernel, forcing, along_y_matrix, 1,
            [fields, block_pieces(1, 1) if i != 1 else [], [piece(x) for x in sums[i]], own,
             here_pieces(1, range(planes)), terms], [kept, kept, 8], f"y_first_far_{i}",
        )
        previous = middle[i]
        if i == 1:
            middle_others[1] = across_chips(middle[1])
            middle_twin[1] = across_cores([middle[1]])

    total = jnp.sum((square[0] + square[1] + square[2]).reshape(8, length // 128, 128), axis=1)
    total = swap_sum(total, doubling(group, devices) + [1])
    middle_twin[0] = across_cores([after(middle[0], square[2])])
    middle_twin[2] = across_cores([middle[2]])
    x_terms = [None] * 3
    x_terms[1] = along_x([piece(after(middle[1], total))], [piece(middle[0])], along_x_matrix, "x_second_1")
    middle_others[1] = after(middle_others[1], x_terms[1])
    total = after(swap_sum(total, doubling(2, group)), middle_others[1], middle_twin[0], middle_twin[2])
    middle_others[0] = across_chips(after(middle[0], total))
    forcing = [forcing_of(total)]

    def middle_pieces(i):
        return [
            (x, part, kept // 2) for part in range(2) for pair in
            zip([middle[i]] + middle_others[i], middle_twin[i] + middle_far[i]) for x in pair
        ]

    def second_step(i):
        return y_call(
            second_kernel, forcing, along_y_matrix, 0,
            [middle_pieces(i), middle_pieces(1) if i != 1 else [], [], [piece(middle[i])], [piece(middle[1])],
             [piece(x_terms[i])], [piece(base[i])]], [size] * planes, f"y_second_{i}",
        )

    ends = [None] * 3
    middle_far[1] = across_cores(middle_others[1])
    ends[1] = second_step(1)
    x_terms[0] = along_x([piece(after(middle[0], ends[1]))], [], along_x_matrix, "x_second_0", 1)
    middle_others[0] = after(middle_others[0], x_terms[0])
    middle_others[2] = across_chips(after(middle[2], middle_others[0]))
    middle_far[0] = across_cores(middle_others[0])
    x_terms[2] = along_x([piece(after(middle[2], x_terms[0]))], [piece(middle[0])], along_x_matrix, "x_second_2", 1)
    middle_far[0] = after(middle_far[0], x_terms[2])
    ends[0] = second_step(0)
    middle_others[2] = after(middle_others[2], ends[0])
    middle_far[2] = across_cores(middle_others[2])
    ends[2] = second_step(2)

    out = jnp.zeros(velocity.shape, F32)
    for i in (1, 0, 2):
        for d, block in enumerate(ends[i]):
            block = swap(block, d * group) if d else block
            out = lax.dynamic_update_slice(out, block[None, None], (i, plane ^ d, 0, 0))
    return out


def solution(mesh):
    placed = (P(None, "groups", "row", None), P(), P())
    return jax.shard_map(
        on_device,
        mesh=mesh,
        in_specs=placed,
        out_specs=P(None, "groups", "row", None),
        check_vma=False,
    )
```

```python
import functools

import jax
import jax.numpy as jnp
from jax import lax
from jax.experimental import pallas as pl
from jax.experimental.pallas import tpu as pltpu
from jax.sharding import PartitionSpec as P

viscosity = 0.2
power_input = 2.0
time_step = 0.5
first_weight = 8.0 / 15.0
second_weight = 5.0 / 12.0
back_weight = 17.0 / 60.0

BF16 = jnp.bfloat16
F32 = jnp.float32
VMEM_BYTES = 24 * 1024 * 1024


def halves(x):
    high = x.astype(BF16)
    return high, (x - high.astype(F32)).astype(BF16)


def product(a, b):
    return jnp.dot(a, b, preferred_element_type=F32)


def params():
    return pltpu.CompilerParams(vmem_limit_bytes=VMEM_BYTES)


def matrices_kernel(count, order_ref, own_ref, *refs):
    slope_parts, curve_parts = refs[:count], refs[count:2 * count]
    slope_ref, curve_ref, along_x_ref, along_y_ref, turned = refs[2 * count:]
    size = slope_parts[0].shape[0]
    for place, ref, scale in ((0, slope_ref, -0.5), (2, curve_ref, viscosity)):
        high, low = halves(ref[...] * scale)
        along_x_ref[place] = high
        along_x_ref[place + 1] = low
    for high_place, low_place, parts, scale in ((1, 0, slope_parts, -0.5), (2, 3, curve_parts, viscosity)):
        turned[...] = jnp.concatenate([part[...] for part in parts], axis=0).T
        for block in range(along_y_ref.shape[1] // size):
            source = pl.ds(pl.multiple_of(own_ref[block] * size, size), size)
            high, low = halves(turned[source, :] * scale)
            along_y_ref[high_place, block * size:(block + 1) * size, :] = high
            along_y_ref[low_place, block * size:(block + 1) * size, :] = low


def prepare_matrices(order, own, slope_matrix, curve_matrix, size):
    length = slope_matrix.shape[0]
    width = min(128, length)
    count = width // size
    kept = own.shape[0] * size

    def part(place):
        return pl.BlockSpec((size, length), lambda j, order_ref, own_ref: (order_ref[count * j + place], 0))

    parts = [part(place) for place in range(count)]
    straight = pl.BlockSpec((width, length), lambda j, order_ref, own_ref: (j, 0))
    return pl.pallas_call(
        functools.partial(matrices_kernel, count),
        grid_spec=pltpu.PrefetchScalarGridSpec(
            num_scalar_prefetch=2,
            grid=(length // width,),
            in_specs=parts + parts + [straight, straight],
            out_specs=[
                pl.BlockSpec((4, width, length), lambda j, order_ref, own_ref: (0, j, 0)),
                pl.BlockSpec((4, kept, width), lambda j, order_ref, own_ref: (0, 0, j)),
            ],
            scratch_shapes=[pltpu.VMEM((length, width), F32)],
        ),
        out_shape=[
            jax.ShapeDtypeStruct((4, length, length), BF16),
            jax.ShapeDtypeStruct((4, kept, length), BF16),
        ],
        compiler_params=params(),
        cost_estimate=pl.CostEstimate(flops=16 * length ** 3, bytes_accessed=32 * length * length, transcendentals=0),
    )(order, own, *([slope_matrix] * count), *([curve_matrix] * count), slope_matrix, curve_matrix)


def piece_spec(piece, width, column):
    _, place, rows = piece
    return pl.BlockSpec((rows, width), lambda n: (place, column(n)))


def joined(refs, columns=slice(None)):
    return jnp.concatenate([ref[:, columns] for ref in refs], axis=0)


def cut(refs, counts):
    pieces, start = [], 0
    for count in counts:
        pieces.append(refs[start:start + count])
        start += count
    return *pieces, refs[start:]


def pack_kernel(plane_ref, velocity_ref, *block_refs):
    components, planes, size, length = velocity_ref.shape
    plane = plane_ref[0]
    velocity = velocity_ref[...].reshape(components * planes * size // 8, 8, length)
    squares = jnp.sum(velocity * velocity, axis=0)
    for d, ref in enumerate(block_refs):
        for i in range(components):
            ref[i * size:(i + 1) * size, :] = velocity_ref[i, plane ^ d]
        ref[components * size:, :] = squares


def pack(plane, velocity):
    components, planes, size, length = velocity.shape
    shape = (components * size + 8, length)
    return pl.pallas_call(
        pack_kernel,
        grid_spec=pltpu.PrefetchScalarGridSpec(
            num_scalar_prefetch=1,
            grid=(1,),
            in_specs=[pl.BlockSpec(velocity.shape, lambda n, plane_ref: (0, 0, 0, 0))],
            out_specs=[pl.BlockSpec(shape, lambda n, plane_ref: (0, 0))] * planes,
        ),
        out_shape=[jax.ShapeDtypeStruct(shape, F32)] * planes,
        compiler_params=params(),
        name="pack",
    )(plane.reshape(1).astype(jnp.int32), velocity)


def along_x_kernel(counts, copies, *refs):
    fields, carriers, (matrix_ref, out_ref, stack) = cut(refs, counts)
    rows = out_ref.shape[0]
    carriers = (carriers or fields) * copies

    @pl.when(pl.program_id(0) == 0)
    def _():
        field = joined(fields)
        high, low = halves(field)
        stack[0:rows] = low
        stack[rows:2 * rows] = high
        high, low = halves(joined(carriers) * field)
        stack[2 * rows:3 * rows] = high
        stack[3 * rows:4 * rows] = low

    tile = out_ref.shape[1]
    columns = pl.ds(pl.multiple_of(pl.program_id(0) * tile, tile), tile)
    a = product(stack[...], matrix_ref[0])
    b = product(stack[rows:3 * rows], matrix_ref[1])
    c = product(stack[0:2 * rows], matrix_ref[2])
    d = product(stack[rows:2 * rows], matrix_ref[3])
    slope = a[0:rows] + a[rows:2 * rows] + b[0:rows]
    rest = a[2 * rows:3 * rows] + a[3 * rows:] + b[rows:] + c[0:rows] + c[rows:] + d
    out_ref[...] = joined(carriers, columns) * slope + rest


def along_x(fields, carriers, matrix, name, weight=36):
    rows, length = sum(piece[2] for piece in fields), fields[0][0].shape[1]
    copies = len(fields) // len(carriers) if carriers else 1
    tile = min(256, length)
    pieces = fields + carriers
    return pl.pallas_call(
        functools.partial(along_x_kernel, (len(fields), len(carriers)), copies),
        grid=(length // tile,),
        in_specs=[piece_spec(piece, length, lambda n: 0) for piece in pieces]
        + [pl.BlockSpec((4, length, tile), lambda n: (0, 0, n))],
        out_specs=pl.BlockSpec((rows, tile), lambda n: (0, n)),
        out_shape=jax.ShapeDtypeStruct((rows, length), F32),
        scratch_shapes=[pltpu.VMEM((4 * rows, length), BF16)],
        compiler_params=params(),
        cost_estimate=pl.CostEstimate(
            flops=weight * rows * length * length, bytes_accessed=4 * rows * length, transcendentals=0
        ),
        name=name,
    )(*[piece[0] for piece in pieces], matrix)


def y_sums(matrix_ref, fields, carriers, sums):
    rows, length = matrix_ref.shape[1:]
    field = joined(fields)
    carrier = joined(carriers) if carriers else field
    field_high, field_low = halves(field)
    flux_high, flux_low = halves(field * carrier)
    matrix = matrix_ref[...].reshape(4 * rows, length)
    a = product(matrix, field_high)
    b = product(matrix[rows:3 * rows], field_low)
    c = product(matrix[0:2 * rows], flux_high)
    d = product(matrix[rows:2 * rows], flux_low)
    slope = a[0:rows] + a[rows:2 * rows] + b[0:rows]
    rest = a[2 * rows:3 * rows] + a[3 * rows:] + b[rows:] + c[0:rows] + c[rows:] + d
    if sums:
        slope, rest = slope + sums[0][...], rest + sums[1][...]
    return slope, rest


def partial_kernel(counts, matrix_ref, *refs):
    fields, carriers, sums, (slope_ref, rest_ref) = cut(refs, counts)
    slope_ref[...], rest_ref[...] = y_sums(matrix_ref, fields, carriers, sums)


def tendency(cells, totals, field, carrier, x_terms, sums):
    total = jnp.sum(functools.reduce(jnp.add, [ref[...] for ref in totals]), keepdims=True)
    forcing = power_input / (total / cells)
    return joined(x_terms) + joined(carrier) * sums[0] + sums[1] + forcing * field


def first_kernel(cells, counts, matrix_ref, *refs):
    fields, carriers, sums, own, own_carrier, x_terms, totals, (middle_ref, base_ref, square_ref) = cut(refs, counts)
    rows = matrix_ref.shape[1]
    field = joined(own)
    first = tendency(cells, totals, field, own_carrier, x_terms, y_sums(matrix_ref, fields, carriers, sums))
    middle = field + (time_step * first_weight) * first
    middle_ref[...] = middle
    base_ref[...] = middle - (time_step * back_weight) * first
    square_ref[...] = jnp.sum((middle * middle).reshape(rows // 8, 8, middle.shape[1]), axis=0)


def second_kernel(cells, counts, matrix_ref, *refs):
    fields, carriers, sums, own, own_carrier, x_terms, totals, (base_ref, *out_refs) = cut(refs, counts)
    field = joined(own)
    second = tendency(cells, totals, field, own_carrier, x_terms, y_sums(matrix_ref, fields, carriers, sums))
    out = base_ref[...] + (time_step * second_weight) * second
    size = out_refs[0].shape[0]
    for place, out_ref in enumerate(out_refs):
        out_ref[...] = out[place * size:(place + 1) * size]


def y_call(kernel, matrix, part, groups, out_rows, name, totals=(), weight=36):
    rows, length = matrix.shape[1], groups[0][0][0].shape[1]
    depth = sum(piece[2] for piece in groups[0])
    tile = min(256, length)
    pieces = [piece for group in groups for piece in group]
    counts = [len(group) for group in groups]
    specs = [piece_spec(piece, tile, lambda n: n) for piece in pieces]
    if totals:
        start = sum(counts[:6])
        pieces[start:start] = totals
        specs[start:start] = [piece_spec(piece, piece[0].shape[1], lambda n: 0) for piece in totals]
        counts[6:] = [len(totals)]
    return pl.pallas_call(
        functools.partial(kernel, tuple(counts)),
        grid=(length // tile,),
        in_specs=[pl.BlockSpec((4, rows, depth), lambda n: (0, 0, part))] + specs,
        out_specs=[pl.BlockSpec((count, tile), lambda n: (0, n)) for count in out_rows],
        out_shape=[jax.ShapeDtypeStruct((count, length), F32) for count in out_rows],
        compiler_params=params(),
        cost_estimate=pl.CostEstimate(
            flops=weight * rows * depth * length, bytes_accessed=4 * rows * length, transcendentals=0
        ),
        name=name,
    )(matrix, *[piece[0] for piece in pieces])


def fold_kernel(*refs):
    total = functools.reduce(jnp.add, [ref[...] for ref in refs[:-1]])
    refs[-1][...] = functools.reduce(jnp.add, [total[:, k:k + 128] for k in range(0, total.shape[1], 128)])


def fold(arrays, name):
    return pl.pallas_call(
        fold_kernel,
        out_shape=jax.ShapeDtypeStruct((8, 128), F32),
        compiler_params=params(),
        name=name,
    )(*arrays)


def place_kernel(components, planes, plane_ref, *refs):
    out_ref = refs[-1]
    for n in range(components):
        @pl.when(pl.program_id(0) == n)
        def _():
            for d in range(planes):
                out_ref[plane_ref[0] ^ d] = refs[n * planes + d][...]


def place_blocks(plane, blocks, components, shape, out):
    planes, size, length = shape[1:]
    first, step = components[0], components[-1] - components[0]
    whole = pl.BlockSpec((size, length), lambda n, plane_ref: (0, 0))
    arrays = [block for i in components for block in blocks[i]]
    return pl.pallas_call(
        functools.partial(place_kernel, len(components), planes),
        grid_spec=pltpu.PrefetchScalarGridSpec(
            num_scalar_prefetch=1,
            grid=(len(components),),
            in_specs=[whole] * len(arrays) + [pl.BlockSpec(memory_space=pl.ANY)] * (out is not None),
            out_specs=pl.BlockSpec((None, planes, size, length), lambda n, plane_ref: (first + step * n, 0, 0, 0)),
        ),
        out_shape=jax.ShapeDtypeStruct(shape, F32),
        input_output_aliases={} if out is None else {1 + len(arrays): 0},
        compiler_params=params(),
        name="place",
    )(plane.reshape(1).astype(jnp.int32), *arrays, *([] if out is None else [out]))


def after(values, *earlier):
    return lax.optimization_barrier((values, earlier))[0]


def on_device(velocity, slope_matrix, curve_matrix):
    components, planes, size, length = velocity.shape
    devices = lax.axis_size("row")
    group = devices // planes
    chips = group // 2
    kept = length // group
    place = lax.axis_index("row")
    plane, member = place // group, place % group
    cells = components * planes * size * devices * length
    parts = [range(planes // 2), range(planes // 2, planes)]

    def swap(x, distance):
        return lax.ppermute(x, "row", [(r, r ^ distance) for r in range(devices)])

    def across_chips(x):
        return [swap(x, 2 * h) for h in range(1, chips)]

    def across_cores(pieces):
        return [swap(piece, 1) for piece in pieces]

    order = jnp.stack([
        (plane ^ d) * group + (member ^ (2 * h + core))
        for part in parts for h in range(chips) for core in range(2) for d in part
    ]).astype(jnp.int32)
    own_order = jnp.stack([(plane ^ d) * group + member for d in range(planes)]).astype(jnp.int32)

    here, others, twins, fars = [None] * planes, [None] * planes, [None] * planes, [None] * planes

    def block_pieces(i, part):
        pieces = []
        for h in range(chips):
            for core in range(2):
                for d in parts[part]:
                    block = ([here[d]] + others[d])[h] if core == 0 else (twins[d] + fars[d])[h]
                    pieces.append((block, i, size))
        return pieces

    def here_pieces(i, distances):
        return [(here[d], i, size) for d in distances]

    def x_first(distances, name, weight=36):
        fields = [piece for i in range(components) for piece in here_pieces(i, distances)]
        return along_x(fields, here_pieces(0, distances), along_x_matrix, name, weight)

    blocks = list(pack(plane, velocity))
    here[0] = blocks[0]
    for d in parts[0][1:]:
        here[d] = swap(blocks[d], d * group)
    for d in parts[1][:-1]:
        here[d] = swap(blocks[d], d * group)
    others[0] = across_chips(here[0])
    along_x_matrix, along_y_matrix = prepare_matrices(order, own_order, slope_matrix, curve_matrix, size)

    for d in parts[0][1:]:
        here[d] = after(here[d], along_x_matrix, along_y_matrix)
        others[d] = across_chips(here[d])
    here[planes - 1] = swap(blocks[-1], (planes - 1) * group)
    last = planes - 1
    x_terms = [x_first(parts[0], "x_first_near", 1)]
    for d in parts[0]:
        twins[d] = across_cores([after(here[d], x_terms[0])])
    for d in parts[1][:-1]:
        here[d] = after(here[d], x_terms[0])
        others[d] = across_chips(here[d])
        x_terms.append(x_first([d], f"x_first_{d}", 1))
    for d in parts[0]:
        others[d] = after(others[d], x_terms[-1])
        fars[d] = across_cores(others[d])
    here[last] = after(here[last], x_terms[-1], [twins[d] for d in parts[0]], [others[d] for d in parts[1][:-1]])
    others[last] = across_chips(here[last])
    x_terms.append(x_first([last], f"x_first_{last}"))

    sums, previous = [None] * 3, x_terms[-1]
    for i in (1, 0, 2):
        fields = block_pieces(i, 0)
        fields = [(after(fields[0][0], previous), *fields[0][1:])] + fields[1:]
        sums[i] = y_call(
            partial_kernel, along_y_matrix, 0, [fields, block_pieces(1, 0) if i != 1 else [], []],
            [kept, kept], f"y_first_near_{i}",
        )
        previous = sums[i]
    for d in parts[1][:-1]:
        twins[d] = across_cores([after(here[d], sums[1])])
        others[d] = after(others[d], sums[1])
        fars[d] = across_cores(others[d])
    twins[last] = across_cores([after(here[last], sums[0])])
    others[last] = after(others[last], sums[2])
    fars[last] = across_cores(others[last])
    totals = [
        (block, components * size // 8, 8)
        for d in range(planes) for block in [here[d]] + others[d] + twins[d] + fars[d]
    ]

    middle, base, square = [None] * 3, [None] * 3, [None] * 3
    middle_others, middle_twin, middle_far = [None] * 3, [None] * 3, [None] * 3

    def piece(x):
        return (x, 0, x.shape[0])

    for i in (1, 0, 2):
        fields = block_pieces(i, 1)
        fields = [(after(fields[0][0], previous), *fields[0][1:])] + fields[1:]
        own = here_pieces(i, range(planes))
        terms = [(x_terms[0], i, len(parts[0]) * size)] + [(x, i, size) for x in x_terms[1:]]
        middle[i], base[i], square[i] = y_call(
            functools.partial(first_kernel, cells), along_y_matrix, 1,
            [fields, block_pieces(1, 1) if i != 1 else [], [piece(x) for x in sums[i]], own,
             here_pieces(1, range(planes)), terms], [kept, kept, 8], f"y_first_far_{i}", totals,
        )
        previous = middle[i]
        if i == 1:
            middle_others[1] = across_chips(middle[1])
            middle_twin[1] = across_cores([middle[1]])

    total = fold(square, "fold_own")
    total = fold([total] + [swap(total, d * group) for d in range(1, planes)], "fold_planes")
    middle_twin[0] = across_cores([after(middle[0], square[2])])
    middle_twin[2] = across_cores([middle[2]])
    x_terms = [None] * 3
    x_terms[1] = along_x([piece(after(middle[1], total))], [piece(middle[0])], along_x_matrix, "x_second_1")
    middle_others[1] = after(middle_others[1], x_terms[1])
    totals = [total] + [swap(total, m) for m in range(1, group)]
    totals = after(totals, middle_others[1], middle_twin[0], middle_twin[2])
    middle_others[0] = across_chips(after(middle[0], totals))
    totals = [piece(x) for x in totals]

    def middle_pieces(i):
        return [
            (x, part, kept // 2) for part in range(2) for pair in
            zip([middle[i]] + middle_others[i], middle_twin[i] + middle_far[i]) for x in pair
        ]

    def second_step(i):
        return y_call(
            functools.partial(second_kernel, cells), along_y_matrix, 0,
            [middle_pieces(i), middle_pieces(1) if i != 1 else [], [], [piece(middle[i])], [piece(middle[1])],
             [piece(x_terms[i])], [piece(base[i])]], [size] * planes, f"y_second_{i}", totals, {0: 36, 1: 36, 2: 36}[i],
        )

    ends = [None] * 3
    middle_far[1] = across_cores(middle_others[1])
    def leave(i):
        ends[i] = [swap(block, d * group) if d else block for d, block in enumerate(ends[i])]

    ends[1] = second_step(1)
    x_terms[0] = along_x([piece(after(middle[0], ends[1]))], [], along_x_matrix, "x_second_0", 36)
    leave(1)
    middle_others[0] = after(middle_others[0], x_terms[0])
    middle_others[2] = across_chips(after(middle[2], middle_others[0]))
    middle_far[0] = across_cores(middle_others[0])
    x_terms[2] = along_x(
        [piece(after(middle[2], x_terms[0]))], [piece(middle[0])], along_x_matrix, "x_second_2", 36
    )
    middle_far[0] = after(middle_far[0], x_terms[2])
    ends[0] = second_step(0)
    ends[1] = after(ends[1], ends[0])
    out = place_blocks(plane, ends, (1,), velocity.shape, None)
    leave(0)
    middle_others[2] = after(middle_others[2], out)
    middle_far[2] = across_cores(middle_others[2])
    ends[2] = second_step(2)
    leave(2)
    out = place_blocks(plane, ends, (0,), velocity.shape, out)
    return place_blocks(plane, ends, (2,), velocity.shape, out)


def solution(mesh):
    placed = (P(None, "groups", "row", None), P(), P())
    return jax.shard_map(
        on_device,
        mesh=mesh,
        in_specs=placed,
        out_specs=P(None, "groups", "row", None),
        check_vma=False,
    )
```

```python
import functools

import jax
import jax.numpy as jnp
from jax import lax
from jax.experimental import pallas as pl
from jax.experimental.pallas import tpu as pltpu
from jax.sharding import PartitionSpec as P

viscosity = 0.2
power_input = 2.0
time_step = 0.5
first_weight = 8.0 / 15.0
second_weight = 5.0 / 12.0
back_weight = 17.0 / 60.0

BF16 = jnp.bfloat16
F32 = jnp.float32
VMEM_BYTES = 24 * 1024 * 1024


def halves(x):
    high = x.astype(BF16)
    return high, (x - high.astype(F32)).astype(BF16)


def product(a, b):
    return jnp.dot(a, b, preferred_element_type=F32)


def params():
    return pltpu.CompilerParams(vmem_limit_bytes=VMEM_BYTES)


def matrices_kernel(count, order_ref, own_ref, *refs):
    slope_parts, curve_parts = refs[:count], refs[count:2 * count]
    slope_ref, curve_ref, along_x_ref, along_y_ref, turned = refs[2 * count:]
    size = slope_parts[0].shape[0]
    for place, ref, scale in ((0, slope_ref, -0.5), (2, curve_ref, viscosity)):
        high, low = halves(ref[...] * scale)
        along_x_ref[place] = high
        along_x_ref[place + 1] = low
    for high_place, low_place, parts, scale in ((1, 0, slope_parts, -0.5), (2, 3, curve_parts, viscosity)):
        turned[...] = jnp.concatenate([part[...] for part in parts], axis=0).T
        for block in range(along_y_ref.shape[1] // size):
            source = pl.ds(pl.multiple_of(own_ref[block] * size, size), size)
            high, low = halves(turned[source, :] * scale)
            along_y_ref[high_place, block * size:(block + 1) * size, :] = high
            along_y_ref[low_place, block * size:(block + 1) * size, :] = low


def prepare_matrices(order, own, slope_matrix, curve_matrix, size):
    length = slope_matrix.shape[0]
    width = min(128, length)
    count = width // size
    kept = own.shape[0] * size

    def part(place):
        return pl.BlockSpec((size, length), lambda j, order_ref, own_ref: (order_ref[count * j + place], 0))

    parts = [part(place) for place in range(count)]
    straight = pl.BlockSpec((width, length), lambda j, order_ref, own_ref: (j, 0))
    return pl.pallas_call(
        functools.partial(matrices_kernel, count),
        grid_spec=pltpu.PrefetchScalarGridSpec(
            num_scalar_prefetch=2,
            grid=(length // width,),
            in_specs=parts + parts + [straight, straight],
            out_specs=[
                pl.BlockSpec((4, width, length), lambda j, order_ref, own_ref: (0, j, 0)),
                pl.BlockSpec((4, kept, width), lambda j, order_ref, own_ref: (0, 0, j)),
            ],
            scratch_shapes=[pltpu.VMEM((length, width), F32)],
        ),
        out_shape=[
            jax.ShapeDtypeStruct((4, length, length), BF16),
            jax.ShapeDtypeStruct((4, kept, length), BF16),
        ],
        compiler_params=params(),
        cost_estimate=pl.CostEstimate(flops=16 * length ** 3, bytes_accessed=32 * length * length, transcendentals=0),
    )(order, own, *([slope_matrix] * count), *([curve_matrix] * count), slope_matrix, curve_matrix)


def piece_spec(piece, width, column):
    _, place, rows = piece
    return pl.BlockSpec((rows, width), lambda n: (place, column(n)))


def joined(refs, columns=slice(None)):
    return jnp.concatenate([ref[:, columns] for ref in refs], axis=0)


def cut(refs, counts):
    pieces, start = [], 0
    for count in counts:
        pieces.append(refs[start:start + count])
        start += count
    return *pieces, refs[start:]


def pack_kernel(plane_ref, velocity_ref, *block_refs):
    components, planes, size, length = velocity_ref.shape
    plane = plane_ref[0]
    velocity = velocity_ref[...].reshape(components * planes * size // 8, 8, length)
    squares = jnp.sum(velocity * velocity, axis=0)
    for d, ref in enumerate(block_refs):
        for i in range(components):
            ref[i * size:(i + 1) * size, :] = velocity_ref[i, plane ^ d]
        ref[components * size:, :] = squares


def pack(plane, velocity):
    components, planes, size, length = velocity.shape
    shape = (components * size + 8, length)
    return pl.pallas_call(
        pack_kernel,
        grid_spec=pltpu.PrefetchScalarGridSpec(
            num_scalar_prefetch=1,
            grid=(1,),
            in_specs=[pl.BlockSpec(velocity.shape, lambda n, plane_ref: (0, 0, 0, 0))],
            out_specs=[pl.BlockSpec(shape, lambda n, plane_ref: (0, 0))] * planes,
        ),
        out_shape=[jax.ShapeDtypeStruct(shape, F32)] * planes,
        compiler_params=params(),
        name="pack",
    )(plane.reshape(1).astype(jnp.int32), velocity)


def along_x_kernel(counts, copies, *refs):
    fields, carriers, (matrix_ref, out_ref, stack) = cut(refs, counts)
    rows = out_ref.shape[0]
    carriers = (carriers or fields) * copies

    @pl.when(pl.program_id(0) == 0)
    def _():
        field = joined(fields)
        high, low = halves(field)
        stack[0:rows] = low
        stack[rows:2 * rows] = high
        high, low = halves(joined(carriers) * field)
        stack[2 * rows:3 * rows] = high
        stack[3 * rows:4 * rows] = low

    tile = out_ref.shape[1]
    columns = pl.ds(pl.multiple_of(pl.program_id(0) * tile, tile), tile)
    a = product(stack[...], matrix_ref[0])
    b = product(stack[rows:3 * rows], matrix_ref[1])
    c = product(stack[0:2 * rows], matrix_ref[2])
    d = product(stack[rows:2 * rows], matrix_ref[3])
    slope = a[0:rows] + a[rows:2 * rows] + b[0:rows]
    rest = a[2 * rows:3 * rows] + a[3 * rows:] + b[rows:] + c[0:rows] + c[rows:] + d
    out_ref[...] = joined(carriers, columns) * slope + rest


def along_x(fields, carriers, matrix, name, weight=36):
    rows, length = sum(piece[2] for piece in fields), fields[0][0].shape[1]
    copies = len(fields) // len(carriers) if carriers else 1
    tile = min(256, length)
    pieces = fields + carriers
    return pl.pallas_call(
        functools.partial(along_x_kernel, (len(fields), len(carriers)), copies),
        grid=(length // tile,),
        in_specs=[piece_spec(piece, length, lambda n: 0) for piece in pieces]
        + [pl.BlockSpec((4, length, tile), lambda n: (0, 0, n))],
        out_specs=pl.BlockSpec((rows, tile), lambda n: (0, n)),
        out_shape=jax.ShapeDtypeStruct((rows, length), F32),
        scratch_shapes=[pltpu.VMEM((4 * rows, length), BF16)],
        compiler_params=params(),
        cost_estimate=pl.CostEstimate(
            flops=weight * rows * length * length, bytes_accessed=4 * rows * length, transcendentals=0
        ),
        name=name,
    )(*[piece[0] for piece in pieces], matrix)


def y_sums(matrix_ref, fields, carriers, sums):
    rows, length = matrix_ref.shape[1:]
    field = joined(fields)
    carrier = joined(carriers) if carriers else field
    field_high, field_low = halves(field)
    flux_high, flux_low = halves(field * carrier)
    matrix = matrix_ref[...].reshape(4 * rows, length)
    a = product(matrix, field_high)
    b = product(matrix[rows:3 * rows], field_low)
    c = product(matrix[0:2 * rows], flux_high)
    d = product(matrix[rows:2 * rows], flux_low)
    slope = a[0:rows] + a[rows:2 * rows] + b[0:rows]
    rest = a[2 * rows:3 * rows] + a[3 * rows:] + b[rows:] + c[0:rows] + c[rows:] + d
    if sums:
        slope, rest = slope + sums[0][...], rest + sums[1][...]
    return slope, rest


def partial_kernel(counts, matrix_ref, *refs):
    fields, carriers, sums, (slope_ref, rest_ref) = cut(refs, counts)
    slope_ref[...], rest_ref[...] = y_sums(matrix_ref, fields, carriers, sums)


def tendency(cells, totals, field, carrier, x_terms, sums):
    total = jnp.sum(functools.reduce(jnp.add, [ref[...] for ref in totals]), keepdims=True)
    forcing = power_input / (total / cells)
    return joined(x_terms) + joined(carrier) * sums[0] + sums[1] + forcing * field


def first_kernel(cells, counts, matrix_ref, *refs):
    fields, carriers, sums, own, own_carrier, x_terms, totals, (middle_ref, base_ref, square_ref) = cut(refs, counts)
    rows = matrix_ref.shape[1]
    field = joined(own)
    first = tendency(cells, totals, field, own_carrier, x_terms, y_sums(matrix_ref, fields, carriers, sums))
    middle = field + (time_step * first_weight) * first
    middle_ref[...] = middle
    base_ref[...] = middle - (time_step * back_weight) * first
    square_ref[...] = jnp.sum((middle * middle).reshape(rows // 8, 8, middle.shape[1]), axis=0)


def second_kernel(cells, counts, matrix_ref, *refs):
    fields, carriers, sums, own, own_carrier, x_terms, totals, (base_ref, *out_refs) = cut(refs, counts)
    field = joined(own)
    second = tendency(cells, totals, field, own_carrier, x_terms, y_sums(matrix_ref, fields, carriers, sums))
    out = base_ref[...] + (time_step * second_weight) * second
    size = out_refs[0].shape[0]
    for place, out_ref in enumerate(out_refs):
        out_ref[...] = out[place * size:(place + 1) * size]


def y_call(kernel, matrix, part, groups, out_rows, name, totals=(), weight=36):
    rows, length = matrix.shape[1], groups[0][0][0].shape[1]
    depth = sum(piece[2] for piece in groups[0])
    tile = min(256, length)
    pieces = [piece for group in groups for piece in group]
    counts = [len(group) for group in groups]
    specs = [piece_spec(piece, tile, lambda n: n) for piece in pieces]
    if totals:
        start = sum(counts[:6])
        pieces[start:start] = totals
        specs[start:start] = [piece_spec(piece, piece[0].shape[1], lambda n: 0) for piece in totals]
        counts[6:] = [len(totals)]
    return pl.pallas_call(
        functools.partial(kernel, tuple(counts)),
        grid=(length // tile,),
        in_specs=[pl.BlockSpec((4, rows, depth), lambda n: (0, 0, part))] + specs,
        out_specs=[pl.BlockSpec((count, tile), lambda n: (0, n)) for count in out_rows],
        out_shape=[jax.ShapeDtypeStruct((count, length), F32) for count in out_rows],
        compiler_params=params(),
        cost_estimate=pl.CostEstimate(
            flops=weight * rows * depth * length, bytes_accessed=4 * rows * length, transcendentals=0
        ),
        name=name,
    )(matrix, *[piece[0] for piece in pieces])


def fold_kernel(*refs):
    total = functools.reduce(jnp.add, [ref[...] for ref in refs[:-1]])
    refs[-1][...] = functools.reduce(jnp.add, [total[:, k:k + 128] for k in range(0, total.shape[1], 128)])


def fold(arrays, name):
    return pl.pallas_call(
        fold_kernel,
        out_shape=jax.ShapeDtypeStruct((8, 128), F32),
        compiler_params=params(),
        name=name,
    )(*arrays)


def place_kernel(components, planes, plane_ref, *refs):
    out_ref = refs[-1]
    for n in range(components):
        @pl.when(pl.program_id(0) == n)
        def _():
            for d in range(planes):
                out_ref[plane_ref[0] ^ d] = refs[n * planes + d][...]


def place_blocks(plane, blocks, components, shape, out):
    planes, size, length = shape[1:]
    first, step = components[0], components[-1] - components[0]
    whole = pl.BlockSpec((size, length), lambda n, plane_ref: (0, 0))
    arrays = [block for i in components for block in blocks[i]]
    return pl.pallas_call(
        functools.partial(place_kernel, len(components), planes),
        grid_spec=pltpu.PrefetchScalarGridSpec(
            num_scalar_prefetch=1,
            grid=(len(components),),
            in_specs=[whole] * len(arrays) + [pl.BlockSpec(memory_space=pl.ANY)] * (out is not None),
            out_specs=pl.BlockSpec((None, planes, size, length), lambda n, plane_ref: (first + step * n, 0, 0, 0)),
        ),
        out_shape=jax.ShapeDtypeStruct(shape, F32),
        input_output_aliases={} if out is None else {1 + len(arrays): 0},
        compiler_params=params(),
        name="place",
    )(plane.reshape(1).astype(jnp.int32), *arrays, *([] if out is None else [out]))


def after(values, *earlier):
    return lax.optimization_barrier((values, earlier))[0]


def on_device(velocity, slope_matrix, curve_matrix):
    components, planes, size, length = velocity.shape
    devices = lax.axis_size("row")
    group = devices // planes
    chips = group // 2
    kept = length // group
    place = lax.axis_index("row")
    plane, member = place // group, place % group
    cells = components * planes * size * devices * length
    parts = [range(planes // 2), range(planes // 2, planes)]

    def swap(x, distance):
        return lax.ppermute(x, "row", [(r, r ^ distance) for r in range(devices)])

    def across_chips(x):
        return [swap(x, 2 * h) for h in range(1, chips)]

    def across_cores(pieces):
        return [swap(piece, 1) for piece in pieces]

    order = jnp.stack([
        (plane ^ d) * group + (member ^ (2 * h + core))
        for part in parts for h in range(chips) for core in range(2) for d in part
    ]).astype(jnp.int32)
    own_order = jnp.stack([(plane ^ d) * group + member for d in range(planes)]).astype(jnp.int32)

    here, others, twins, fars = [None] * planes, [None] * planes, [None] * planes, [None] * planes

    def block_pieces(i, part):
        pieces = []
        for h in range(chips):
            for core in range(2):
                for d in parts[part]:
                    block = ([here[d]] + others[d])[h] if core == 0 else (twins[d] + fars[d])[h]
                    pieces.append((block, i, size))
        return pieces

    def here_pieces(i, distances):
        return [(here[d], i, size) for d in distances]

    def x_first(distances, name, weight=36):
        fields = [piece for i in range(components) for piece in here_pieces(i, distances)]
        return along_x(fields, here_pieces(0, distances), along_x_matrix, name, weight)

    last = planes - 1
    blocks = list(pack(plane, velocity))
    here[0] = blocks[0]
    for d in range(1, last):
        here[d] = swap(blocks[d], d * group)
    others[0] = across_chips(here[0])
    others[1] = across_chips(blocks[1])
    along_x_matrix, along_y_matrix = prepare_matrices(order, own_order, slope_matrix, curve_matrix, size)
    here[last] = swap(after(blocks[last], along_x_matrix), last * group)
    here[0] = after(here[0], along_x_matrix, along_y_matrix)
    x_terms = [x_first([0], "x_first_0", 120)]
    for d in range(1, last):
        here[d] = after(here[d], x_terms[-1], others[0], others[1])
        x_terms.append(x_first([d], f"x_first_{d}", 1))
    others[1] = [swap(block, group) for block in others[1]]
    for d in range(2, last):
        others[d] = across_chips(here[d])
    here[last] = after(here[last], x_terms[-1])
    others[last] = across_chips(here[last])
    for d in parts[0]:
        twins[d] = across_cores([after(here[d], here[last], others[last - 1])])
        fars[d] = across_cores(after(others[d], here[last], others[last - 1]))
    x_terms.append(x_first([last], f"x_first_{last}"))

    sums, previous = [None] * 3, x_terms[-1]
    for i in (1, 0, 2):
        fields = block_pieces(i, 0)
        fields = [(after(fields[0][0], previous), *fields[0][1:])] + fields[1:]
        sums[i] = y_call(
            partial_kernel, along_y_matrix, 0, [fields, block_pieces(1, 0) if i != 1 else [], []],
            [kept, kept], f"y_first_near_{i}",
        )
        previous = sums[i]
    for d in parts[1][:-1]:
        twins[d] = across_cores([after(here[d], sums[1])])
        others[d] = after(others[d], sums[1])
        fars[d] = across_cores(others[d])
    twins[last] = across_cores([after(here[last], sums[0])])
    others[last] = after(others[last], sums[2])
    fars[last] = across_cores(others[last])
    totals = [
        (block, components * size // 8, 8)
        for d in range(planes) for block in [here[d]] + others[d] + twins[d] + fars[d]
    ]

    middle, base, square = [None] * 3, [None] * 3, [None] * 3
    middle_others, middle_twin, middle_far = [None] * 3, [None] * 3, [None] * 3

    def piece(x):
        return (x, 0, x.shape[0])

    for i in (1, 0, 2):
        earlier = {1: [sums[2]], 0: [middle[1]], 2: [middle[0], middle_twin[1]]}[i]
        fields = block_pieces(i, 1)
        fields = [(after(fields[0][0], earlier), *fields[0][1:])] + fields[1:]
        own = here_pieces(i, range(planes))
        terms = [(x, i, size) for x in x_terms]
        middle[i], base[i], square[i] = y_call(
            functools.partial(first_kernel, cells), along_y_matrix, 1,
            [fields, block_pieces(1, 1) if i != 1 else [], [piece(x) for x in sums[i]], own,
             here_pieces(1, range(planes)), terms], [kept, kept, 8], f"y_first_far_{i}", totals,
        )
        middle_twin[i] = across_cores([middle[i]])
        if i == 1:
            middle_others[1] = across_chips(middle[1])

    total = fold(after(square, middle_twin[0]), "fold_own")
    total = [total] + [swap(total, d * group) for d in range(1, planes)]
    total = fold(after(total, middle_twin[2]), "fold_planes")
    totals = [total] + [swap(total, m) for m in range(1, group)]
    x_terms = [None] * 3
    x_terms[1] = along_x([piece(after(middle[1], total))], [piece(middle[0])], along_x_matrix, "x_second_1")
    totals = after(totals, x_terms[1])
    middle_others[1] = after(middle_others[1], totals)
    middle_others[0] = across_chips(after(middle[0], middle_others[1]))
    totals = [piece(x) for x in totals]

    def middle_pieces(i):
        return [
            (x, part, kept // 2) for part in range(2) for pair in
            zip([middle[i]] + middle_others[i], middle_twin[i] + middle_far[i]) for x in pair
        ]

    def second_step(i):
        return y_call(
            functools.partial(second_kernel, cells), along_y_matrix, 0,
            [middle_pieces(i), middle_pieces(1) if i != 1 else [], [], [piece(middle[i])], [piece(middle[1])],
             [piece(x_terms[i])], [piece(base[i])]], [size] * planes, f"y_second_{i}", totals, {0: 36, 1: 36, 2: 36}[i],
        )

    ends = [None] * 3
    middle_far[1] = across_cores(middle_others[1])
    def leave(i):
        ends[i] = [swap(block, d * group) if d else block for d, block in enumerate(ends[i])]

    ends[1] = second_step(1)
    x_terms[0] = along_x([piece(after(middle[0], ends[1]))], [], along_x_matrix, "x_second_0", 36)
    leave(1)
    middle_others[0] = after(middle_others[0], x_terms[0])
    middle_others[2] = across_chips(after(middle[2], middle_others[0]))
    middle_far[0] = across_cores(middle_others[0])
    x_terms[2] = along_x(
        [piece(after(middle[2], x_terms[0]))], [piece(middle[0])], along_x_matrix, "x_second_2", 36
    )
    middle_far[0] = after(middle_far[0], x_terms[2])
    ends[0] = second_step(0)
    ends[1] = after(ends[1], ends[0])
    out = place_blocks(plane, ends, (1,), velocity.shape, None)
    leave(0)
    middle_others[2] = after(middle_others[2], out)
    middle_far[2] = across_cores(middle_others[2])
    ends[2] = second_step(2)
    leave(2)
    out = place_blocks(plane, ends, (0,), velocity.shape, out)
    return place_blocks(plane, ends, (2,), velocity.shape, out)


def solution(mesh):
    placed = (P(None, "groups", "row", None), P(), P())
    return jax.shard_map(
        on_device,
        mesh=mesh,
        in_specs=placed,
        out_specs=P(None, "groups", "row", None),
        check_vma=False,
    )
```

```python
import functools

import jax
import jax.numpy as jnp
from jax import lax
from jax.experimental import pallas as pl
from jax.experimental.pallas import tpu as pltpu
from jax.sharding import PartitionSpec as P

viscosity = 0.2
power_input = 2.0
time_step = 0.5
first_weight = 8.0 / 15.0
second_weight = 5.0 / 12.0
back_weight = 17.0 / 60.0

BF16 = jnp.bfloat16
F32 = jnp.float32
VMEM_BYTES = 24 * 1024 * 1024


def halves(x):
    high = x.astype(BF16)
    return high, (x - high.astype(F32)).astype(BF16)


def product(a, b):
    return jnp.dot(a, b, preferred_element_type=F32)


def params():
    return pltpu.CompilerParams(vmem_limit_bytes=VMEM_BYTES)


def matrices_kernel(count, order_ref, own_ref, *refs):
    slope_parts, curve_parts = refs[:count], refs[count:2 * count]
    slope_ref, curve_ref, along_x_ref, along_y_ref, turned = refs[2 * count:]
    size = slope_parts[0].shape[0]
    for place, ref, scale in ((0, slope_ref, -0.5), (2, curve_ref, viscosity)):
        high, low = halves(ref[...] * scale)
        along_x_ref[place] = high
        along_x_ref[place + 1] = low
    for high_place, low_place, parts, scale in ((1, 0, slope_parts, -0.5), (2, 3, curve_parts, viscosity)):
        turned[...] = jnp.concatenate([part[...] for part in parts], axis=0).T
        for block in range(along_y_ref.shape[1] // size):
            source = pl.ds(pl.multiple_of(own_ref[block] * size, size), size)
            high, low = halves(turned[source, :] * scale)
            along_y_ref[high_place, block * size:(block + 1) * size, :] = high
            along_y_ref[low_place, block * size:(block + 1) * size, :] = low


def prepare_matrices(order, own, slope_matrix, curve_matrix, size):
    length = slope_matrix.shape[0]
    width = min(128, length)
    count = width // size
    kept = own.shape[0] * size

    def part(place):
        return pl.BlockSpec((size, length), lambda j, order_ref, own_ref: (order_ref[count * j + place], 0))

    parts = [part(place) for place in range(count)]
    straight = pl.BlockSpec((width, length), lambda j, order_ref, own_ref: (j, 0))
    return pl.pallas_call(
        functools.partial(matrices_kernel, count),
        grid_spec=pltpu.PrefetchScalarGridSpec(
            num_scalar_prefetch=2,
            grid=(length // width,),
            in_specs=parts + parts + [straight, straight],
            out_specs=[
                pl.BlockSpec((4, width, length), lambda j, order_ref, own_ref: (0, j, 0)),
                pl.BlockSpec((4, kept, width), lambda j, order_ref, own_ref: (0, 0, j)),
            ],
            scratch_shapes=[pltpu.VMEM((length, width), F32)],
        ),
        out_shape=[
            jax.ShapeDtypeStruct((4, length, length), BF16),
            jax.ShapeDtypeStruct((4, kept, length), BF16),
        ],
        compiler_params=params(),
        cost_estimate=pl.CostEstimate(flops=16 * length ** 3, bytes_accessed=32 * length * length, transcendentals=0),
    )(order, own, *([slope_matrix] * count), *([curve_matrix] * count), slope_matrix, curve_matrix)


def piece_spec(piece, width, column):
    _, place, rows = piece
    return pl.BlockSpec((rows, width), lambda n: (place, column(n)))


def joined(refs, columns=slice(None)):
    return jnp.concatenate([ref[:, columns] for ref in refs], axis=0)


def cut(refs, counts):
    pieces, start = [], 0
    for count in counts:
        pieces.append(refs[start:start + count])
        start += count
    return *pieces, refs[start:]


def pack_kernel(plane_ref, velocity_ref, *block_refs):
    components, planes, size, length = velocity_ref.shape
    plane = plane_ref[0]
    velocity = velocity_ref[...].reshape(components * planes * size // 8, 8, length)
    squares = jnp.sum(velocity * velocity, axis=0)
    *block_refs, tail_ref = block_refs
    for d, ref in enumerate(block_refs):
        count = components if d < planes - 1 else components - 1
        for i in range(count):
            ref[i * size:(i + 1) * size, :] = velocity_ref[i, plane ^ d]
        ref[count * size:, :] = squares
    tail_ref[...] = velocity_ref[components - 1, plane ^ (planes - 1)]


def pack(plane, velocity):
    components, planes, size, length = velocity.shape
    rows = [components * size + 8] * (planes - 1) + [(components - 1) * size + 8, size]
    return pl.pallas_call(
        pack_kernel,
        grid_spec=pltpu.PrefetchScalarGridSpec(
            num_scalar_prefetch=1,
            grid=(1,),
            in_specs=[pl.BlockSpec(velocity.shape, lambda n, plane_ref: (0, 0, 0, 0))],
            out_specs=[pl.BlockSpec((count, length), lambda n, plane_ref: (0, 0)) for count in rows],
        ),
        out_shape=[jax.ShapeDtypeStruct((count, length), F32) for count in rows],
        compiler_params=params(),
        name="pack",
    )(plane.reshape(1).astype(jnp.int32), velocity)


def along_x_kernel(counts, copies, *refs):
    fields, carriers, (matrix_ref, out_ref, stack) = cut(refs, counts)
    rows = out_ref.shape[0]
    carriers = (carriers or fields) * copies

    @pl.when(pl.program_id(0) == 0)
    def _():
        field = joined(fields)
        high, low = halves(field)
        stack[0:rows] = low
        stack[rows:2 * rows] = high
        high, low = halves(joined(carriers) * field)
        stack[2 * rows:3 * rows] = high
        stack[3 * rows:4 * rows] = low

    tile = out_ref.shape[1]
    columns = pl.ds(pl.multiple_of(pl.program_id(0) * tile, tile), tile)
    a = product(stack[...], matrix_ref[0])
    b = product(stack[rows:3 * rows], matrix_ref[1])
    c = product(stack[0:2 * rows], matrix_ref[2])
    d = product(stack[rows:2 * rows], matrix_ref[3])
    slope = a[0:rows] + a[rows:2 * rows] + b[0:rows]
    rest = a[2 * rows:3 * rows] + a[3 * rows:] + b[rows:] + c[0:rows] + c[rows:] + d
    out_ref[...] = joined(carriers, columns) * slope + rest


def along_x(fields, carriers, matrix, name, weight=36):
    rows, length = sum(piece[2] for piece in fields), fields[0][0].shape[1]
    copies = len(fields) // len(carriers) if carriers else 1
    tile = min(256, length)
    pieces = fields + carriers
    return pl.pallas_call(
        functools.partial(along_x_kernel, (len(fields), len(carriers)), copies),
        grid=(length // tile,),
        in_specs=[piece_spec(piece, length, lambda n: 0) for piece in pieces]
        + [pl.BlockSpec((4, length, tile), lambda n: (0, 0, n))],
        out_specs=pl.BlockSpec((rows, tile), lambda n: (0, n)),
        out_shape=jax.ShapeDtypeStruct((rows, length), F32),
        scratch_shapes=[pltpu.VMEM((4 * rows, length), BF16)],
        compiler_params=params(),
        cost_estimate=pl.CostEstimate(
            flops=weight * rows * length * length, bytes_accessed=4 * rows * length, transcendentals=0
        ),
        name=name,
    )(*[piece[0] for piece in pieces], matrix)


def y_sums(matrix_ref, fields, carriers, sums):
    rows, length = matrix_ref.shape[1:]
    field = joined(fields)
    carrier = joined(carriers) if carriers else field
    field_high, field_low = halves(field)
    flux_high, flux_low = halves(field * carrier)
    matrix = matrix_ref[...].reshape(4 * rows, length)
    a = product(matrix, field_high)
    b = product(matrix[rows:3 * rows], field_low)
    c = product(matrix[0:2 * rows], flux_high)
    d = product(matrix[rows:2 * rows], flux_low)
    slope = a[0:rows] + a[rows:2 * rows] + b[0:rows]
    rest = a[2 * rows:3 * rows] + a[3 * rows:] + b[rows:] + c[0:rows] + c[rows:] + d
    if sums:
        slope, rest = slope + sums[0][...], rest + sums[1][...]
    return slope, rest


def partial_kernel(counts, matrix_ref, *refs):
    fields, carriers, sums, (slope_ref, rest_ref) = cut(refs, counts)
    slope_ref[...], rest_ref[...] = y_sums(matrix_ref, fields, carriers, sums)


def tendency(cells, totals, field, carrier, x_terms, sums):
    total = jnp.sum(functools.reduce(jnp.add, [ref[...] for ref in totals]), keepdims=True)
    forcing = power_input / (total / cells)
    return joined(x_terms) + joined(carrier) * sums[0] + sums[1] + forcing * field


def first_kernel(cells, counts, matrix_ref, *refs):
    fields, carriers, sums, own, own_carrier, x_terms, totals, (middle_ref, base_ref, square_ref) = cut(refs, counts)
    rows = matrix_ref.shape[1]
    field = joined(own)
    first = tendency(cells, totals, field, own_carrier, x_terms, y_sums(matrix_ref, fields, carriers, sums))
    middle = field + (time_step * first_weight) * first
    middle_ref[...] = middle
    base_ref[...] = middle - (time_step * back_weight) * first
    square_ref[...] = jnp.sum((middle * middle).reshape(rows // 8, 8, middle.shape[1]), axis=0)


def second_kernel(cells, counts, matrix_ref, *refs):
    fields, carriers, sums, own, own_carrier, x_terms, totals, (base_ref, *out_refs) = cut(refs, counts)
    field = joined(own)
    second = tendency(cells, totals, field, own_carrier, x_terms, y_sums(matrix_ref, fields, carriers, sums))
    out = base_ref[...] + (time_step * second_weight) * second
    size = out_refs[0].shape[0]
    for place, out_ref in enumerate(out_refs):
        out_ref[...] = out[place * size:(place + 1) * size]


def y_call(kernel, matrix, part, groups, out_rows, name, totals=(), weight=36):
    rows, length = matrix.shape[1], groups[0][0][0].shape[1]
    depth = sum(piece[2] for piece in groups[0])
    tile = min(256, length)
    pieces = [piece for group in groups for piece in group]
    counts = [len(group) for group in groups]
    specs = [piece_spec(piece, tile, lambda n: n) for piece in pieces]
    if totals:
        start = sum(counts[:6])
        pieces[start:start] = totals
        specs[start:start] = [piece_spec(piece, piece[0].shape[1], lambda n: 0) for piece in totals]
        counts[6:] = [len(totals)]
    return pl.pallas_call(
        functools.partial(kernel, tuple(counts)),
        grid=(length // tile,),
        in_specs=[pl.BlockSpec((4, rows, depth), lambda n: (0, 0, part))] + specs,
        out_specs=[pl.BlockSpec((count, tile), lambda n: (0, n)) for count in out_rows],
        out_shape=[jax.ShapeDtypeStruct((count, length), F32) for count in out_rows],
        compiler_params=params(),
        cost_estimate=pl.CostEstimate(
            flops=weight * rows * depth * length, bytes_accessed=4 * rows * length, transcendentals=0
        ),
        name=name,
    )(matrix, *[piece[0] for piece in pieces])


def fold_kernel(*refs):
    total = functools.reduce(jnp.add, [ref[...] for ref in refs[:-1]])
    refs[-1][...] = functools.reduce(jnp.add, [total[:, k:k + 128] for k in range(0, total.shape[1], 128)])


def fold(arrays, name):
    return pl.pallas_call(
        fold_kernel,
        out_shape=jax.ShapeDtypeStruct((8, 128), F32),
        compiler_params=params(),
        name=name,
    )(*arrays)


def place_kernel(components, planes, plane_ref, *refs):
    out_ref = refs[-1]
    for n in range(components):
        @pl.when(pl.program_id(0) == n)
        def _():
            for d in range(planes):
                out_ref[plane_ref[0] ^ d] = refs[n * planes + d][...]


def place_blocks(plane, blocks, components, shape, out):
    planes, size, length = shape[1:]
    first, step = components[0], components[-1] - components[0]
    whole = pl.BlockSpec((size, length), lambda n, plane_ref: (0, 0))
    arrays = [block for i in components for block in blocks[i]]
    return pl.pallas_call(
        functools.partial(place_kernel, len(components), planes),
        grid_spec=pltpu.PrefetchScalarGridSpec(
            num_scalar_prefetch=1,
            grid=(len(components),),
            in_specs=[whole] * len(arrays) + [pl.BlockSpec(memory_space=pl.ANY)] * (out is not None),
            out_specs=pl.BlockSpec((None, planes, size, length), lambda n, plane_ref: (first + step * n, 0, 0, 0)),
        ),
        out_shape=jax.ShapeDtypeStruct(shape, F32),
        input_output_aliases={} if out is None else {1 + len(arrays): 0},
        compiler_params=params(),
        name="place",
    )(plane.reshape(1).astype(jnp.int32), *arrays, *([] if out is None else [out]))


def after(values, *earlier):
    return lax.optimization_barrier((values, earlier))[0]


def on_device(velocity, slope_matrix, curve_matrix):
    components, planes, size, length = velocity.shape
    devices = lax.axis_size("row")
    group = devices // planes
    chips = group // 2
    kept = length // group
    place = lax.axis_index("row")
    plane, member = place // group, place % group
    cells = components * planes * size * devices * length
    parts = [range(planes // 2), range(planes // 2, planes)]

    def swap(x, distance):
        return lax.ppermute(x, "row", [(r, r ^ distance) for r in range(devices)])

    def across_chips(x):
        return [swap(x, 2 * h) for h in range(1, chips)]

    def across_cores(pieces):
        return [swap(piece, 1) for piece in pieces]

    order = jnp.stack([
        (plane ^ d) * group + (member ^ (2 * h + core))
        for part in parts for h in range(chips) for core in range(2) for d in part
    ]).astype(jnp.int32)
    own_order = jnp.stack([(plane ^ d) * group + member for d in range(planes)]).astype(jnp.int32)

    last = planes - 1
    here, others, twins, fars = ([None] * (planes + 1) for _ in range(4))

    def piece_of(store, i, d):
        block = store[planes] if d == last and i == components - 1 else store[d]
        return lambda h: (block[h], 0 if d == last and i == components - 1 else i, size)

    def block_pieces(i, part):
        near = [[here[d]] + (others[d] or []) for d in range(planes + 1)]
        far = [(twins[d] or []) + (fars[d] or []) for d in range(planes + 1)]
        return [
            piece_of(store, i, d)(h) for h in range(chips) for store in (near, far) for d in parts[part]
        ]

    def here_pieces(i, distances):
        return [piece_of([[block] for block in here], i, d)(0) for d in distances]

    def x_first(components, distances, name, weight=36):
        fields = [piece for i in components for piece in here_pieces(i, distances)]
        return along_x(fields, here_pieces(0, distances), along_x_matrix, name, weight)

    every = range(components)
    blocks = list(pack(plane, velocity))
    here[0] = blocks[0]
    for d in range(1, last):
        here[d] = swap(blocks[d], d * group)
    others[0] = across_chips(here[0])
    others[1] = across_chips(blocks[1])
    along_x_matrix, along_y_matrix = prepare_matrices(order, own_order, slope_matrix, curve_matrix, size)

    here[1] = after(here[1], along_x_matrix, along_y_matrix)
    others[1] = [swap(after(block, here[1]), group) for block in others[1]]
    here[last] = swap(after(blocks[last], here[1]), last * group)
    here[planes] = swap(after(blocks[planes], here[last - 1]), last * group)
    x_near = x_first(every, parts[0], "x_first_near", 1)
    here[2] = after(here[2], x_near, others[0])
    others[2] = across_chips(here[2])
    x_two = x_first(every, [2], "x_first_2", 1)
    for d in parts[0]:
        twins[d] = across_cores([after(here[d], x_near)])
    here[last] = after(here[last], x_two)
    others[last] = across_chips(here[last])
    for d in parts[0]:
        others[d] = after(others[d], here[last])
        fars[d] = across_cores(others[d])
    sums = [None] * 3

    def near_sums(i, earlier):
        fields = block_pieces(i, 0)
        fields = [(after(fields[0][0], earlier), *fields[0][1:])] + fields[1:]
        sums[i] = y_call(
            partial_kernel, along_y_matrix, 0, [fields, block_pieces(1, 0) if i != 1 else [], []],
            [kept, kept], f"y_first_near_{i}", (), 36,
        )

    near_sums(1, here[last])
    twins[2] = across_cores([after(here[2], here[last])])
    others[2] = after(others[2], here[last])
    fars[2] = across_cores(others[2])
    here[last] = after(here[last], sums[1])
    x_last = x_first(every[:-1], [last], "x_first_last", 36)
    near_sums(0, x_last)
    here[planes] = after(here[planes], sums[0])
    others[planes] = across_chips(here[planes])
    twins[last] = across_cores([after(here[last], sums[1], twins[2], fars[2])])
    near_sums(2, here[planes])
    others[last] = after(others[last], sums[2])
    fars[last] = across_cores(others[last])
    totals = [
        (block, block.shape[0] // 8 - 1, 8)
        for d in range(planes) for block in [here[d]] + others[d] + twins[d] + fars[d]
    ]

    middle, base, square = [None] * 3, [None] * 3, [None] * 3
    middle_others, middle_twin, middle_far = [None] * 3, [None] * 3, [None] * 3

    def piece(x):
        return (x, 0, x.shape[0])

    def first_step(i, terms, earlier, weight=36):
        fields = block_pieces(i, 1)
        fields = [(after(fields[0][0], earlier), *fields[0][1:])] + fields[1:]
        middle[i], base[i], square[i] = y_call(
            functools.partial(first_kernel, cells), along_y_matrix, 1,
            [fields, block_pieces(1, 1) if i != 1 else [], [piece(x) for x in sums[i]],
             here_pieces(i, range(planes)), here_pieces(1, range(planes)), terms],
            [kept, kept, 8], f"y_first_far_{i}", totals, weight,
        )

    def terms_of(i):
        return [(x_near, i, len(parts[0]) * size), (x_two, i, size), (x_last, i, size)]

    first_step(1, terms_of(1), sums[2])
    middle_others[1] = across_chips(middle[1])
    first_step(0, terms_of(0), [middle[1], others[planes]], 36)
    twins[planes] = across_cores([after(here[planes], middle[1])])
    x_tail = x_first(every[-1:], [last], "x_first_tail", 36)
    others[planes] = after(others[planes], middle[1])
    fars[planes] = across_cores(others[planes])
    first_step(2, terms_of(2)[:-1] + [(x_tail, 0, size)], middle[0], 36)

    total = fold(square, "fold_own")
    total = [total] + [swap(total, d * group) for d in range(1, planes)]
    total = fold(total, "fold_planes")
    for i in range(3):
        middle_twin[i] = across_cores([after(middle[i], square[2])])
    x_terms = [None] * 3
    x_terms[1] = along_x([piece(after(middle[1], total))], [piece(middle[0])], along_x_matrix, "x_second_1", 36)
    middle_others[1] = after(middle_others[1], x_terms[1], middle_twin)
    totals = [total] + [swap(after(total, middle_others[1]), m) for m in range(1, group)]
    middle_others[0] = across_chips(after(middle[0], middle_others[1]))
    totals = [piece(x) for x in totals]

    def middle_pieces(i):
        return [
            (x, part, kept // 2) for part in range(2) for pair in
            zip([middle[i]] + middle_others[i], middle_twin[i] + middle_far[i]) for x in pair
        ]

    def second_step(i):
        return y_call(
            functools.partial(second_kernel, cells), along_y_matrix, 0,
            [middle_pieces(i), middle_pieces(1) if i != 1 else [], [], [piece(middle[i])], [piece(middle[1])],
             [piece(x_terms[i])], [piece(base[i])]], [size] * planes, f"y_second_{i}", totals, {0: 36, 1: 36, 2: 36}[i],
        )

    ends = [None] * 3
    middle_far[1] = across_cores(middle_others[1])
    def leave(i):
        ends[i] = [swap(block, d * group) if d else block for d, block in enumerate(ends[i])]

    ends[1] = second_step(1)
    x_terms[0] = along_x([piece(after(middle[0], ends[1]))], [], along_x_matrix, "x_second_0", 36)
    leave(1)
    middle_others[0] = after(middle_others[0], x_terms[0])
    middle_others[2] = across_chips(after(middle[2], middle_others[0]))
    middle_far[0] = across_cores(middle_others[0])
    x_terms[2] = along_x(
        [piece(after(middle[2], x_terms[0]))], [piece(middle[0])], along_x_matrix, "x_second_2", 36
    )
    middle_far[0] = after(middle_far[0], x_terms[2])
    ends[0] = second_step(0)
    ends[1] = after(ends[1], ends[0])
    out = place_blocks(plane, ends, (1,), velocity.shape, None)
    leave(0)
    middle_others[2] = after(middle_others[2], out)
    middle_far[2] = across_cores(middle_others[2])
    ends[2] = second_step(2)
    leave(2)
    out = place_blocks(plane, ends, (0,), velocity.shape, out)
    return place_blocks(plane, ends, (2,), velocity.shape, out)


def solution(mesh):
    placed = (P(None, "groups", "row", None), P(), P())
    return jax.shard_map(
        on_device,
        mesh=mesh,
        in_specs=placed,
        out_specs=P(None, "groups", "row", None),
        check_vma=False,
    )
```

```python
import functools

import jax
import jax.numpy as jnp
from jax import lax
from jax.experimental import pallas as pl
from jax.experimental.pallas import tpu as pltpu
from jax.sharding import PartitionSpec as P

viscosity = 0.2
power_input = 2.0
time_step = 0.5
first_weight = 8.0 / 15.0
second_weight = 5.0 / 12.0
back_weight = 17.0 / 60.0

BF16 = jnp.bfloat16
F32 = jnp.float32
VMEM_BYTES = 24 * 1024 * 1024


def halves(x):
    high = x.astype(BF16)
    return high, (x - high.astype(F32)).astype(BF16)


def product(a, b):
    return jnp.dot(a, b, preferred_element_type=F32)


def params():
    return pltpu.CompilerParams(vmem_limit_bytes=VMEM_BYTES)


def matrices_kernel(count, order_ref, own_ref, *refs):
    slope_parts, curve_parts = refs[:count], refs[count:2 * count]
    slope_ref, curve_ref, along_x_ref, along_y_ref, turned = refs[2 * count:]
    size = slope_parts[0].shape[0]
    for place, ref, scale in ((0, slope_ref, -0.5), (2, curve_ref, viscosity)):
        high, low = halves(ref[...] * scale)
        along_x_ref[place] = high
        along_x_ref[place + 1] = low
    for high_place, low_place, parts, scale in ((1, 0, slope_parts, -0.5), (2, 3, curve_parts, viscosity)):
        turned[...] = jnp.concatenate([part[...] for part in parts], axis=0).T
        for block in range(along_y_ref.shape[1] // size):
            source = pl.ds(pl.multiple_of(own_ref[block] * size, size), size)
            high, low = halves(turned[source, :] * scale)
            along_y_ref[high_place, block * size:(block + 1) * size, :] = high
            along_y_ref[low_place, block * size:(block + 1) * size, :] = low


def prepare_matrices(order, own, slope_matrix, curve_matrix, size):
    length = slope_matrix.shape[0]
    width = min(128, length)
    count = width // size
    kept = own.shape[0] * size

    def part(place):
        return pl.BlockSpec((size, length), lambda j, order_ref, own_ref: (order_ref[count * j + place], 0))

    parts = [part(place) for place in range(count)]
    straight = pl.BlockSpec((width, length), lambda j, order_ref, own_ref: (j, 0))
    return pl.pallas_call(
        functools.partial(matrices_kernel, count),
        grid_spec=pltpu.PrefetchScalarGridSpec(
            num_scalar_prefetch=2,
            grid=(length // width,),
            in_specs=parts + parts + [straight, straight],
            out_specs=[
                pl.BlockSpec((4, width, length), lambda j, order_ref, own_ref: (0, j, 0)),
                pl.BlockSpec((4, kept, width), lambda j, order_ref, own_ref: (0, 0, j)),
            ],
            scratch_shapes=[pltpu.VMEM((length, width), F32)],
        ),
        out_shape=[
            jax.ShapeDtypeStruct((4, length, length), BF16),
            jax.ShapeDtypeStruct((4, kept, length), BF16),
        ],
        compiler_params=params(),
        cost_estimate=pl.CostEstimate(flops=16 * length ** 3, bytes_accessed=32 * length * length, transcendentals=0),
    )(order, own, *([slope_matrix] * count), *([curve_matrix] * count), slope_matrix, curve_matrix)


def piece_spec(piece, width, column):
    _, place, rows = piece
    return pl.BlockSpec((rows, width), lambda n: (place, column(n)))


def joined(refs, columns=slice(None)):
    return jnp.concatenate([ref[:, columns] for ref in refs], axis=0)


def cut(refs, counts):
    pieces, start = [], 0
    for count in counts:
        pieces.append(refs[start:start + count])
        start += count
    return *pieces, refs[start:]


def pack_kernel(plane_ref, velocity_ref, *block_refs):
    components, planes, size, length = velocity_ref.shape
    plane = plane_ref[0]
    velocity = velocity_ref[...].reshape(components * planes * size // 8, 8, length)
    squares = jnp.sum(velocity * velocity, axis=0)
    *block_refs, tail_ref = block_refs
    for d, ref in enumerate(block_refs):
        count = components if d < planes - 1 else components - 1
        for i in range(count):
            ref[i * size:(i + 1) * size, :] = velocity_ref[i, plane ^ d]
        ref[count * size:, :] = squares
    tail_ref[...] = velocity_ref[components - 1, plane ^ (planes - 1)]


def pack(plane, velocity):
    components, planes, size, length = velocity.shape
    rows = [components * size + 8] * (planes - 1) + [(components - 1) * size + 8, size]
    return pl.pallas_call(
        pack_kernel,
        grid_spec=pltpu.PrefetchScalarGridSpec(
            num_scalar_prefetch=1,
            grid=(1,),
            in_specs=[pl.BlockSpec(velocity.shape, lambda n, plane_ref: (0, 0, 0, 0))],
            out_specs=[pl.BlockSpec((count, length), lambda n, plane_ref: (0, 0)) for count in rows],
        ),
        out_shape=[jax.ShapeDtypeStruct((count, length), F32) for count in rows],
        compiler_params=params(),
        name="pack",
    )(plane.reshape(1).astype(jnp.int32), velocity)


def along_x_kernel(counts, copies, *refs):
    fields, carriers, (matrix_ref, out_ref, stack) = cut(refs, counts)
    rows = out_ref.shape[0]
    carriers = (carriers or fields) * copies

    @pl.when(pl.program_id(0) == 0)
    def _():
        field = joined(fields)
        high, low = halves(field)
        stack[0:rows] = low
        stack[rows:2 * rows] = high
        high, low = halves(joined(carriers) * field)
        stack[2 * rows:3 * rows] = high
        stack[3 * rows:4 * rows] = low

    tile = out_ref.shape[1]
    columns = pl.ds(pl.multiple_of(pl.program_id(0) * tile, tile), tile)
    a = product(stack[...], matrix_ref[0])
    b = product(stack[rows:3 * rows], matrix_ref[1])
    c = product(stack[0:2 * rows], matrix_ref[2])
    d = product(stack[rows:2 * rows], matrix_ref[3])
    slope = a[0:rows] + a[rows:2 * rows] + b[0:rows]
    rest = a[2 * rows:3 * rows] + a[3 * rows:] + b[rows:] + c[0:rows] + c[rows:] + d
    out_ref[...] = joined(carriers, columns) * slope + rest


def along_x(fields, carriers, matrix, name, weight=36):
    rows, length = sum(piece[2] for piece in fields), fields[0][0].shape[1]
    copies = len(fields) // len(carriers) if carriers else 1
    tile = min(256, length)
    pieces = fields + carriers
    return pl.pallas_call(
        functools.partial(along_x_kernel, (len(fields), len(carriers)), copies),
        grid=(length // tile,),
        in_specs=[piece_spec(piece, length, lambda n: 0) for piece in pieces]
        + [pl.BlockSpec((4, length, tile), lambda n: (0, 0, n))],
        out_specs=pl.BlockSpec((rows, tile), lambda n: (0, n)),
        out_shape=jax.ShapeDtypeStruct((rows, length), F32),
        scratch_shapes=[pltpu.VMEM((4 * rows, length), BF16)],
        compiler_params=params(),
        cost_estimate=pl.CostEstimate(
            flops=weight * rows * length * length, bytes_accessed=4 * rows * length, transcendentals=0
        ),
        name=name,
    )(*[piece[0] for piece in pieces], matrix)


def y_sums(matrix_ref, fields, carriers, sums):
    rows, length = matrix_ref.shape[1:]
    field = joined(fields)
    carrier = joined(carriers) if carriers else field
    field_high, field_low = halves(field)
    flux_high, flux_low = halves(field * carrier)
    matrix = matrix_ref[...].reshape(4 * rows, length)
    a = product(matrix, field_high)
    b = product(matrix[rows:3 * rows], field_low)
    c = product(matrix[0:2 * rows], flux_high)
    d = product(matrix[rows:2 * rows], flux_low)
    slope = a[0:rows] + a[rows:2 * rows] + b[0:rows]
    rest = a[2 * rows:3 * rows] + a[3 * rows:] + b[rows:] + c[0:rows] + c[rows:] + d
    if sums:
        slope, rest = slope + sums[0][...], rest + sums[1][...]
    return slope, rest


def partial_kernel(counts, matrix_ref, *refs):
    fields, carriers, sums, (slope_ref, rest_ref) = cut(refs, counts)
    slope_ref[...], rest_ref[...] = y_sums(matrix_ref, fields, carriers, sums)


def tendency(cells, totals, field, carrier, x_terms, sums):
    total = jnp.sum(functools.reduce(jnp.add, [ref[...] for ref in totals]), keepdims=True)
    forcing = power_input / (total / cells)
    return joined(x_terms) + joined(carrier) * sums[0] + sums[1] + forcing * field


def first_kernel(cells, counts, matrix_ref, *refs):
    fields, carriers, sums, own, own_carrier, x_terms, totals, (middle_ref, base_ref, square_ref) = cut(refs, counts)
    rows = matrix_ref.shape[1]
    field = joined(own)
    first = tendency(cells, totals, field, own_carrier, x_terms, y_sums(matrix_ref, fields, carriers, sums))
    middle = field + (time_step * first_weight) * first
    middle_ref[...] = middle
    base_ref[...] = middle - (time_step * back_weight) * first
    square_ref[...] = jnp.sum((middle * middle).reshape(rows // 8, 8, middle.shape[1]), axis=0)


def second_kernel(cells, counts, matrix_ref, *refs):
    fields, carriers, sums, own, own_carrier, x_terms, totals, (base_ref, *out_refs) = cut(refs, counts)
    field = joined(own)
    second = tendency(cells, totals, field, own_carrier, x_terms, y_sums(matrix_ref, fields, carriers, sums))
    out = base_ref[...] + (time_step * second_weight) * second
    size = out_refs[0].shape[0]
    for place, out_ref in enumerate(out_refs):
        out_ref[...] = out[place * size:(place + 1) * size]


def y_call(kernel, matrix, part, groups, out_rows, name, totals=(), weight=36):
    rows, length = matrix.shape[1], groups[0][0][0].shape[1]
    depth = sum(piece[2] for piece in groups[0])
    tile = min(256, length)
    pieces = [piece for group in groups for piece in group]
    counts = [len(group) for group in groups]
    specs = [piece_spec(piece, tile, lambda n: n) for piece in pieces]
    if totals:
        start = sum(counts[:6])
        pieces[start:start] = totals
        specs[start:start] = [piece_spec(piece, piece[0].shape[1], lambda n: 0) for piece in totals]
        counts[6:] = [len(totals)]
    return pl.pallas_call(
        functools.partial(kernel, tuple(counts)),
        grid=(length // tile,),
        in_specs=[pl.BlockSpec((4, rows, depth), lambda n: (0, 0, part))] + specs,
        out_specs=[pl.BlockSpec((count, tile), lambda n: (0, n)) for count in out_rows],
        out_shape=[jax.ShapeDtypeStruct((count, length), F32) for count in out_rows],
        compiler_params=params(),
        cost_estimate=pl.CostEstimate(
            flops=weight * rows * depth * length, bytes_accessed=4 * rows * length, transcendentals=0
        ),
        name=name,
    )(matrix, *[piece[0] for piece in pieces])


def fold_kernel(*refs):
    total = functools.reduce(jnp.add, [ref[...] for ref in refs[:-1]])
    refs[-1][...] = functools.reduce(jnp.add, [total[:, k:k + 128] for k in range(0, total.shape[1], 128)])


def fold(arrays, name):
    return pl.pallas_call(
        fold_kernel,
        out_shape=jax.ShapeDtypeStruct((8, 128), F32),
        compiler_params=params(),
        name=name,
    )(*arrays)


def place_kernel(components, planes, plane_ref, *refs):
    out_ref = refs[-1]
    for n in range(components):
        @pl.when(pl.program_id(0) == n)
        def _():
            for d in range(planes):
                out_ref[plane_ref[0] ^ d] = refs[n * planes + d][...]


def place_blocks(plane, blocks, components, shape, out):
    planes, size, length = shape[1:]
    first, step = components[0], components[-1] - components[0]
    whole = pl.BlockSpec((size, length), lambda n, plane_ref: (0, 0))
    arrays = [block for i in components for block in blocks[i]]
    return pl.pallas_call(
        functools.partial(place_kernel, len(components), planes),
        grid_spec=pltpu.PrefetchScalarGridSpec(
            num_scalar_prefetch=1,
            grid=(len(components),),
            in_specs=[whole] * len(arrays) + [pl.BlockSpec(memory_space=pl.ANY)] * (out is not None),
            out_specs=pl.BlockSpec((None, planes, size, length), lambda n, plane_ref: (first + step * n, 0, 0, 0)),
        ),
        out_shape=jax.ShapeDtypeStruct(shape, F32),
        input_output_aliases={} if out is None else {1 + len(arrays): 0},
        compiler_params=params(),
        name="place",
    )(plane.reshape(1).astype(jnp.int32), *arrays, *([] if out is None else [out]))


def after(values, *earlier):
    return lax.optimization_barrier((values, earlier))[0]


def on_device(velocity, slope_matrix, curve_matrix):
    components, planes, size, length = velocity.shape
    devices = lax.axis_size("row")
    group = devices // planes
    chips = group // 2
    kept = length // group
    place = lax.axis_index("row")
    plane, member = place // group, place % group
    cells = components * planes * size * devices * length
    parts = [range(planes // 2), range(planes // 2, planes)]

    def swap(x, distance):
        return lax.ppermute(x, "row", [(r, r ^ distance) for r in range(devices)])

    def across_chips(x):
        return [swap(x, 2 * h) for h in range(1, chips)]

    def across_cores(pieces):
        return [swap(piece, 1) for piece in pieces]

    order = jnp.stack([
        (plane ^ d) * group + (member ^ (2 * h + core))
        for part in parts for h in range(chips) for core in range(2) for d in part
    ]).astype(jnp.int32)
    own_order = jnp.stack([(plane ^ d) * group + member for d in range(planes)]).astype(jnp.int32)

    last = planes - 1
    here, others, twins, fars = ([None] * (planes + 1) for _ in range(4))

    def piece_of(store, i, d):
        block = store[planes] if d == last and i == components - 1 else store[d]
        return lambda h: (block[h], 0 if d == last and i == components - 1 else i, size)

    def block_pieces(i, part):
        near = [[here[d]] + (others[d] or []) for d in range(planes + 1)]
        far = [(twins[d] or []) + (fars[d] or []) for d in range(planes + 1)]
        return [
            piece_of(store, i, d)(h) for h in range(chips) for store in (near, far) for d in parts[part]
        ]

    def here_pieces(i, distances):
        return [piece_of([[block] for block in here], i, d)(0) for d in distances]

    def x_first(components, distances, name, weight=36):
        fields = [piece for i in components for piece in here_pieces(i, distances)]
        return along_x(fields, here_pieces(0, distances), along_x_matrix, name, weight)

    every = range(components)
    blocks = list(pack(plane, velocity))
    here[0] = blocks[0]
    for d in range(1, last):
        here[d] = swap(blocks[d], d * group)
    others[0] = across_chips(here[0])
    others[1] = across_chips(blocks[1])
    along_x_matrix, along_y_matrix = prepare_matrices(order, own_order, slope_matrix, curve_matrix, size)

    here[1] = after(here[1], along_x_matrix, along_y_matrix)
    others[1] = [swap(after(block, here[1]), group) for block in others[1]]
    here[last] = swap(after(blocks[last], here[1]), last * group)
    here[planes] = swap(after(blocks[planes], here[last - 1]), last * group)
    x_near = x_first(every, parts[0], "x_first_near", 1)
    here[2] = after(here[2], x_near, others[0])
    others[2] = across_chips(here[2])
    x_two = x_first(every, [2], "x_first_2", 1)
    for d in parts[0]:
        twins[d] = across_cores([after(here[d], x_near)])
    here[last] = after(here[last], x_two)
    others[last] = across_chips(here[last])
    for d in parts[0]:
        others[d] = after(others[d], here[last])
        fars[d] = across_cores(others[d])
    sums = [None] * 3

    def near_sums(i, earlier):
        fields = block_pieces(i, 0)
        fields = [(after(fields[0][0], earlier), *fields[0][1:])] + fields[1:]
        sums[i] = y_call(
            partial_kernel, along_y_matrix, 0, [fields, block_pieces(1, 0) if i != 1 else [], []],
            [kept, kept], f"y_first_near_{i}", (), 36,
        )

    near_sums(1, here[last])
    twins[2] = across_cores([after(here[2], here[last])])
    others[2] = after(others[2], here[last])
    fars[2] = across_cores(others[2])
    here[last] = after(here[last], sums[1])
    x_last = x_first(every[:-1], [last], "x_first_last", 36)
    near_sums(0, x_last)
    here[planes] = after(here[planes], sums[0])
    others[planes] = across_chips(here[planes])
    twins[last] = across_cores([after(here[last], sums[1], twins[2], fars[2])])
    near_sums(2, here[planes])
    others[last] = after(others[last], sums[2])
    fars[last] = across_cores(others[last])
    totals = [
        (block, block.shape[0] // 8 - 1, 8)
        for d in range(planes) for block in [here[d]] + others[d] + twins[d] + fars[d]
    ]

    middle, base, square = [None] * 3, [None] * 3, [None] * 3
    middle_others, middle_twin, middle_far = [None] * 3, [None] * 3, [None] * 3

    def piece(x):
        return (x, 0, x.shape[0])

    def first_step(i, terms, earlier, weight=36):
        fields = block_pieces(i, 1)
        fields = [(after(fields[0][0], earlier), *fields[0][1:])] + fields[1:]
        middle[i], base[i], square[i] = y_call(
            functools.partial(first_kernel, cells), along_y_matrix, 1,
            [fields, block_pieces(1, 1) if i != 1 else [], [piece(x) for x in sums[i]],
             here_pieces(i, range(planes)), here_pieces(1, range(planes)), terms],
            [kept, kept, 8], f"y_first_far_{i}", totals, weight,
        )

    def terms_of(i):
        return [(x_near, i, len(parts[0]) * size), (x_two, i, size), (x_last, i, size)]

    first_step(1, terms_of(1), sums[2])
    middle_others[1] = across_chips(middle[1])
    first_step(0, terms_of(0), [middle[1], others[planes]], 36)
    twins[planes] = across_cores([after(here[planes], middle[1])])
    x_tail = x_first(every[-1:], [last], "x_first_tail", 36)
    others[planes] = after(others[planes], middle[1])
    fars[planes] = across_cores(others[planes])
    first_step(2, terms_of(2)[:-1] + [(x_tail, 0, size)], middle[0], 36)

    total = fold(square, "fold_own")
    total = [total] + [swap(total, d * group) for d in range(1, planes)]
    x_terms = [None] * 3
    x_terms[1] = along_x([piece(after(middle[1], total[0]))], [piece(middle[0])], along_x_matrix, "x_second_1")
    total = fold(after(total, x_terms[1]), "fold_planes")
    for i in range(3):
        middle_twin[i] = across_cores([after(middle[i], total)])
    middle_others[1] = after(middle_others[1], total)
    totals = [total] + [swap(after(total, middle_others[1]), m) for m in range(1, group)]
    middle_others[0] = across_chips(after(middle[0], middle_others[1]))
    totals = [piece(x) for x in totals]

    def middle_pieces(i):
        return [
            (x, part, kept // 2) for part in range(2) for pair in
            zip([middle[i]] + middle_others[i], middle_twin[i] + middle_far[i]) for x in pair
        ]

    def second_step(i):
        return y_call(
            functools.partial(second_kernel, cells), along_y_matrix, 0,
            [middle_pieces(i), middle_pieces(1) if i != 1 else [], [], [piece(middle[i])], [piece(middle[1])],
             [piece(x_terms[i])], [piece(base[i])]], [size] * planes, f"y_second_{i}", totals, {0: 1, 1: 36, 2: 1}[i],
        )

    ends = [None] * 3
    middle_far[1] = across_cores(middle_others[1])
    def leave(i):
        ends[i] = [swap(block, d * group) if d else block for d, block in enumerate(ends[i])]

    ends[1] = second_step(1)
    x_terms[0] = along_x([piece(after(middle[0], ends[1]))], [], along_x_matrix, "x_second_0", 1)
    leave(1)
    x_terms[2] = along_x(
        [piece(after(middle[2], x_terms[0]))], [piece(middle[0])], along_x_matrix, "x_second_2", 1
    )
    ends[1] = after(ends[1], x_terms[2])
    out = place_blocks(plane, ends, (1,), velocity.shape, None)
    middle_others[0] = after(middle_others[0], out)
    middle_others[2] = across_chips(after(middle[2], middle_others[0]))
    middle_far[0] = across_cores(middle_others[0])
    ends[0] = second_step(0)
    leave(0)
    out = place_blocks(plane, ends, (0,), velocity.shape, out)
    middle_others[2] = after(middle_others[2], out)
    middle_far[2] = across_cores(middle_others[2])
    ends[2] = second_step(2)
    leave(2)
    return place_blocks(plane, ends, (2,), velocity.shape, out)


def solution(mesh):
    placed = (P(None, "groups", "row", None), P(), P())
    return jax.shard_map(
        on_device,
        mesh=mesh,
        in_specs=placed,
        out_specs=P(None, "groups", "row", None),
        check_vma=False,
    )
```

```python
import functools

import jax
import jax.numpy as jnp
from jax import lax
from jax.experimental import pallas as pl
from jax.experimental.pallas import tpu as pltpu
from jax.sharding import PartitionSpec as P

viscosity = 0.2
power_input = 2.0
time_step = 0.5
first_weight = 8.0 / 15.0
second_weight = 5.0 / 12.0
back_weight = 17.0 / 60.0

BF16 = jnp.bfloat16
F32 = jnp.float32
VMEM_BYTES = 24 * 1024 * 1024


def halves(x):
    high = x.astype(BF16)
    return high, (x - high.astype(F32)).astype(BF16)


def product(a, b):
    return jnp.dot(a, b, preferred_element_type=F32)


def params():
    return pltpu.CompilerParams(vmem_limit_bytes=VMEM_BYTES)


def matrices_kernel(count, order_ref, own_ref, *refs):
    slope_parts, curve_parts = refs[:count], refs[count:2 * count]
    slope_ref, curve_ref, along_x_ref, along_y_ref, turned = refs[2 * count:]
    size = slope_parts[0].shape[0]
    for place, ref, scale in ((0, slope_ref, -0.5), (2, curve_ref, viscosity)):
        high, low = halves(ref[...] * scale)
        along_x_ref[place] = high
        along_x_ref[place + 1] = low
    for high_place, low_place, parts, scale in ((1, 0, slope_parts, -0.5), (2, 3, curve_parts, viscosity)):
        turned[...] = jnp.concatenate([part[...] for part in parts], axis=0).T
        for block in range(along_y_ref.shape[1] // size):
            source = pl.ds(pl.multiple_of(own_ref[block] * size, size), size)
            high, low = halves(turned[source, :] * scale)
            along_y_ref[high_place, block * size:(block + 1) * size, :] = high
            along_y_ref[low_place, block * size:(block + 1) * size, :] = low


def prepare_matrices(order, own, slope_matrix, curve_matrix, size):
    length = slope_matrix.shape[0]
    width = min(128, length)
    count = width // size
    kept = own.shape[0] * size

    def part(place):
        return pl.BlockSpec((size, length), lambda j, order_ref, own_ref: (order_ref[count * j + place], 0))

    parts = [part(place) for place in range(count)]
    straight = pl.BlockSpec((width, length), lambda j, order_ref, own_ref: (j, 0))
    return pl.pallas_call(
        functools.partial(matrices_kernel, count),
        grid_spec=pltpu.PrefetchScalarGridSpec(
            num_scalar_prefetch=2,
            grid=(length // width,),
            in_specs=parts + parts + [straight, straight],
            out_specs=[
                pl.BlockSpec((4, width, length), lambda j, order_ref, own_ref: (0, j, 0)),
                pl.BlockSpec((4, kept, width), lambda j, order_ref, own_ref: (0, 0, j)),
            ],
            scratch_shapes=[pltpu.VMEM((length, width), F32)],
        ),
        out_shape=[
            jax.ShapeDtypeStruct((4, length, length), BF16),
            jax.ShapeDtypeStruct((4, kept, length), BF16),
        ],
        compiler_params=params(),
        cost_estimate=pl.CostEstimate(flops=16 * length ** 3, bytes_accessed=32 * length * length, transcendentals=0),
    )(order, own, *([slope_matrix] * count), *([curve_matrix] * count), slope_matrix, curve_matrix)


def piece_spec(piece, width, column):
    _, place, rows = piece
    return pl.BlockSpec((rows, width), lambda n: (place, column(n)))


def joined(refs, columns=slice(None)):
    return jnp.concatenate([ref[:, columns] for ref in refs], axis=0)


def cut(refs, counts):
    pieces, start = [], 0
    for count in counts:
        pieces.append(refs[start:start + count])
        start += count
    return *pieces, refs[start:]


def pack_kernel(plane_ref, velocity_ref, *block_refs):
    components, planes, size, length = velocity_ref.shape
    plane = plane_ref[0]
    velocity = velocity_ref[...].reshape(components * planes * size // 8, 8, length)
    squares = jnp.sum(velocity * velocity, axis=0)
    *block_refs, tail_ref = block_refs
    for d, ref in enumerate(block_refs):
        count = components if d < planes - 1 else components - 1
        for i in range(count):
            ref[i * size:(i + 1) * size, :] = velocity_ref[i, plane ^ d]
        ref[count * size:, :] = squares
    tail_ref[...] = velocity_ref[components - 1, plane ^ (planes - 1)]


def pack(plane, velocity):
    components, planes, size, length = velocity.shape
    rows = [components * size + 8] * (planes - 1) + [(components - 1) * size + 8, size]
    return pl.pallas_call(
        pack_kernel,
        grid_spec=pltpu.PrefetchScalarGridSpec(
            num_scalar_prefetch=1,
            grid=(1,),
            in_specs=[pl.BlockSpec(velocity.shape, lambda n, plane_ref: (0, 0, 0, 0))],
            out_specs=[pl.BlockSpec((count, length), lambda n, plane_ref: (0, 0)) for count in rows],
        ),
        out_shape=[jax.ShapeDtypeStruct((count, length), F32) for count in rows],
        compiler_params=params(),
        name="pack",
    )(plane.reshape(1).astype(jnp.int32), velocity)


def along_x_kernel(counts, copies, *refs):
    fields, carriers, (matrix_ref, out_ref, stack) = cut(refs, counts)
    rows = out_ref.shape[0]
    carriers = (carriers or fields) * copies

    @pl.when(pl.program_id(0) == 0)
    def _():
        field = joined(fields)
        high, low = halves(field)
        stack[0:rows] = low
        stack[rows:2 * rows] = high
        high, low = halves(joined(carriers) * field)
        stack[2 * rows:3 * rows] = high
        stack[3 * rows:4 * rows] = low

    tile = out_ref.shape[1]
    columns = pl.ds(pl.multiple_of(pl.program_id(0) * tile, tile), tile)
    a = product(stack[...], matrix_ref[0])
    b = product(stack[rows:3 * rows], matrix_ref[1])
    c = product(stack[0:2 * rows], matrix_ref[2])
    d = product(stack[rows:2 * rows], matrix_ref[3])
    slope = a[0:rows] + a[rows:2 * rows] + b[0:rows]
    rest = a[2 * rows:3 * rows] + a[3 * rows:] + b[rows:] + c[0:rows] + c[rows:] + d
    out_ref[...] = joined(carriers, columns) * slope + rest


def along_x(fields, carriers, matrix, name, weight=36):
    rows, length = sum(piece[2] for piece in fields), fields[0][0].shape[1]
    copies = len(fields) // len(carriers) if carriers else 1
    tile = min(256, length)
    pieces = fields + carriers
    return pl.pallas_call(
        functools.partial(along_x_kernel, (len(fields), len(carriers)), copies),
        grid=(length // tile,),
        in_specs=[piece_spec(piece, length, lambda n: 0) for piece in pieces]
        + [pl.BlockSpec((4, length, tile), lambda n: (0, 0, n))],
        out_specs=pl.BlockSpec((rows, tile), lambda n: (0, n)),
        out_shape=jax.ShapeDtypeStruct((rows, length), F32),
        scratch_shapes=[pltpu.VMEM((4 * rows, length), BF16)],
        compiler_params=params(),
        cost_estimate=pl.CostEstimate(
            flops=weight * rows * length * length, bytes_accessed=4 * rows * length, transcendentals=0
        ),
        name=name,
    )(*[piece[0] for piece in pieces], matrix)


def y_sums(matrix_ref, fields, carriers, sums):
    rows, length = matrix_ref.shape[1:]
    field = joined(fields)
    carrier = joined(carriers) if carriers else field
    field_high, field_low = halves(field)
    flux_high, flux_low = halves(field * carrier)
    matrix = matrix_ref[...].reshape(4 * rows, length)
    a = product(matrix, field_high)
    b = product(matrix[rows:3 * rows], field_low)
    c = product(matrix[0:2 * rows], flux_high)
    d = product(matrix[rows:2 * rows], flux_low)
    slope = a[0:rows] + a[rows:2 * rows] + b[0:rows]
    rest = a[2 * rows:3 * rows] + a[3 * rows:] + b[rows:] + c[0:rows] + c[rows:] + d
    if sums:
        slope, rest = slope + sums[0][...], rest + sums[1][...]
    return slope, rest


def partial_kernel(counts, matrix_ref, *refs):
    fields, carriers, sums, (slope_ref, rest_ref) = cut(refs, counts)
    slope_ref[...], rest_ref[...] = y_sums(matrix_ref, fields, carriers, sums)


def tendency(cells, totals, field, carrier, x_terms, sums):
    total = jnp.sum(functools.reduce(jnp.add, [ref[...] for ref in totals]), keepdims=True)
    forcing = power_input / (total / cells)
    return joined(x_terms) + joined(carrier) * sums[0] + sums[1] + forcing * field


def first_kernel(cells, counts, matrix_ref, *refs):
    fields, carriers, sums, own, own_carrier, x_terms, totals, (middle_ref, base_ref, square_ref) = cut(refs, counts)
    rows = matrix_ref.shape[1]
    field = joined(own)
    first = tendency(cells, totals, field, own_carrier, x_terms, y_sums(matrix_ref, fields, carriers, sums))
    middle = field + (time_step * first_weight) * first
    middle_ref[...] = middle
    base_ref[...] = middle - (time_step * back_weight) * first
    square_ref[...] = jnp.sum((middle * middle).reshape(rows // 8, 8, middle.shape[1]), axis=0)


def second_kernel(cells, counts, matrix_ref, *refs):
    fields, carriers, sums, own, own_carrier, x_terms, totals, (base_ref, *out_refs) = cut(refs, counts)
    field = joined(own)
    second = tendency(cells, totals, field, own_carrier, x_terms, y_sums(matrix_ref, fields, carriers, sums))
    out = base_ref[...] + (time_step * second_weight) * second
    start = 0
    for out_ref in out_refs:
        out_ref[...] = out[start:start + out_ref.shape[0]]
        start += out_ref.shape[0]


def y_call(kernel, matrix, part, groups, out_rows, name, totals=(), weight=36):
    rows, length = matrix.shape[1], groups[0][0][0].shape[1]
    depth = sum(piece[2] for piece in groups[0])
    tile = min(256, length)
    pieces = [piece for group in groups for piece in group]
    counts = [len(group) for group in groups]
    specs = [piece_spec(piece, tile, lambda n: n) for piece in pieces]
    if totals:
        start = sum(counts[:6])
        pieces[start:start] = totals
        specs[start:start] = [piece_spec(piece, piece[0].shape[1], lambda n: 0) for piece in totals]
        counts[6:] = [len(totals)]
    return pl.pallas_call(
        functools.partial(kernel, tuple(counts)),
        grid=(length // tile,),
        in_specs=[pl.BlockSpec((4, rows, depth), lambda n: (0, 0, part))] + specs,
        out_specs=[pl.BlockSpec((count, tile), lambda n: (0, n)) for count in out_rows],
        out_shape=[jax.ShapeDtypeStruct((count, length), F32) for count in out_rows],
        compiler_params=params(),
        cost_estimate=pl.CostEstimate(
            flops=weight * rows * depth * length, bytes_accessed=4 * rows * length, transcendentals=0
        ),
        name=name,
    )(matrix, *[piece[0] for piece in pieces])


def fold_kernel(*refs):
    total = functools.reduce(jnp.add, [ref[...] for ref in refs[:-1]])
    refs[-1][...] = functools.reduce(jnp.add, [total[:, k:k + 128] for k in range(0, total.shape[1], 128)])


def fold(arrays, name):
    return pl.pallas_call(
        fold_kernel,
        out_shape=jax.ShapeDtypeStruct((8, 128), F32),
        compiler_params=params(),
        name=name,
    )(*arrays)


def place_kernel(spots, plane_ref, *refs):
    out_ref = refs[-1]
    for (d, start, rows), ref in zip(spots, refs):
        out_ref[plane_ref[0] ^ d, start:start + rows, :] = ref[...]


def place_blocks(plane, arrays, spots, component, shape, out):
    planes, size, length = shape[1:]
    before = [] if out is None else [out]
    return pl.pallas_call(
        functools.partial(place_kernel, spots),
        grid_spec=pltpu.PrefetchScalarGridSpec(
            num_scalar_prefetch=1,
            grid=(1,),
            in_specs=[pl.BlockSpec((rows, length), lambda n, plane_ref: (0, 0)) for _, _, rows in spots]
            + [pl.BlockSpec(memory_space=pl.ANY)] * len(before),
            out_specs=pl.BlockSpec((None, planes, size, length), lambda n, plane_ref: (component, 0, 0, 0)),
        ),
        out_shape=jax.ShapeDtypeStruct(shape, F32),
        input_output_aliases={1 + len(arrays): 0} if before else {},
        compiler_params=params(),
        name="place",
    )(plane.reshape(1).astype(jnp.int32), *arrays, *before)


def after(values, *earlier):
    return lax.optimization_barrier((values, earlier))[0]


def on_device(velocity, slope_matrix, curve_matrix):
    components, planes, size, length = velocity.shape
    devices = lax.axis_size("row")
    group = devices // planes
    chips = group // 2
    kept = length // group
    place = lax.axis_index("row")
    plane, member = place // group, place % group
    cells = components * planes * size * devices * length
    parts = [range(planes // 2), range(planes // 2, planes)]

    def swap(x, distance):
        return lax.ppermute(x, "row", [(r, r ^ distance) for r in range(devices)])

    def across_chips(x):
        return [swap(x, 2 * h) for h in range(1, chips)]

    def across_cores(pieces):
        return [swap(piece, 1) for piece in pieces]

    order = jnp.stack([
        (plane ^ d) * group + (member ^ (2 * h + core))
        for part in parts for h in range(chips) for core in range(2) for d in part
    ]).astype(jnp.int32)
    own_order = jnp.stack([(plane ^ d) * group + member for d in range(planes)]).astype(jnp.int32)

    last = planes - 1
    here, others, twins, fars = ([None] * (planes + 1) for _ in range(4))

    def piece_of(store, i, d):
        block = store[planes] if d == last and i == components - 1 else store[d]
        return lambda h: (block[h], 0 if d == last and i == components - 1 else i, size)

    def block_pieces(i, part):
        near = [[here[d]] + (others[d] or []) for d in range(planes + 1)]
        far = [(twins[d] or []) + (fars[d] or []) for d in range(planes + 1)]
        return [
            piece_of(store, i, d)(h) for h in range(chips) for store in (near, far) for d in parts[part]
        ]

    def here_pieces(i, distances):
        return [piece_of([[block] for block in here], i, d)(0) for d in distances]

    def x_first(components, distances, name, weight=36):
        fields = [piece for i in components for piece in here_pieces(i, distances)]
        return along_x(fields, here_pieces(0, distances), along_x_matrix, name, weight)

    every = range(components)
    blocks = list(pack(plane, velocity))
    here[0] = blocks[0]
    for d in range(1, last):
        here[d] = swap(blocks[d], d * group)
    others[0] = across_chips(here[0])
    others[1] = across_chips(blocks[1])
    along_x_matrix, along_y_matrix = prepare_matrices(order, own_order, slope_matrix, curve_matrix, size)

    here[1] = after(here[1], along_x_matrix, along_y_matrix)
    others[1] = [swap(after(block, here[1]), group) for block in others[1]]
    here[last] = swap(after(blocks[last], here[1]), last * group)
    here[planes] = swap(after(blocks[planes], here[last - 1]), last * group)
    x_near = x_first(every, parts[0], "x_first_near", 1)
    here[2] = after(here[2], x_near, others[0])
    others[2] = across_chips(here[2])
    x_two = x_first(every, [2], "x_first_2", 1)
    for d in parts[0]:
        twins[d] = across_cores([after(here[d], x_near)])
    here[last] = after(here[last], x_two)
    others[last] = across_chips(here[last])
    for d in parts[0]:
        others[d] = after(others[d], here[last])
        fars[d] = across_cores(others[d])
    sums = [None] * 3

    def near_sums(i, earlier):
        fields = block_pieces(i, 0)
        fields = [(after(fields[0][0], earlier), *fields[0][1:])] + fields[1:]
        sums[i] = y_call(
            partial_kernel, along_y_matrix, 0, [fields, block_pieces(1, 0) if i != 1 else [], []],
            [kept, kept], f"y_first_near_{i}", (), 36,
        )

    near_sums(1, here[last])
    twins[2] = across_cores([after(here[2], here[last])])
    others[2] = after(others[2], here[last])
    fars[2] = across_cores(others[2])
    here[last] = after(here[last], sums[1])
    x_last = x_first(every[:-1], [last], "x_first_last", 36)
    near_sums(0, x_last)
    here[planes] = after(here[planes], sums[0])
    others[planes] = across_chips(here[planes])
    twins[last] = across_cores([after(here[last], sums[1], twins[2], fars[2])])
    near_sums(2, here[planes])
    others[last] = after(others[last], sums[2])
    fars[last] = across_cores(others[last])
    totals = [
        (block, block.shape[0] // 8 - 1, 8)
        for d in range(planes) for block in [here[d]] + others[d] + twins[d] + fars[d]
    ]

    middle, base, square = [None] * 3, [None] * 3, [None] * 3
    middle_others, middle_twin, middle_far = [None] * 3, [None] * 3, [None] * 3

    def piece(x):
        return (x, 0, x.shape[0])

    def first_step(i, terms, earlier, weight=36):
        fields = block_pieces(i, 1)
        fields = [(after(fields[0][0], earlier), *fields[0][1:])] + fields[1:]
        middle[i], base[i], square[i] = y_call(
            functools.partial(first_kernel, cells), along_y_matrix, 1,
            [fields, block_pieces(1, 1) if i != 1 else [], [piece(x) for x in sums[i]],
             here_pieces(i, range(planes)), here_pieces(1, range(planes)), terms],
            [kept, kept, 8], f"y_first_far_{i}", totals, weight,
        )

    def terms_of(i):
        return [(x_near, i, len(parts[0]) * size), (x_two, i, size), (x_last, i, size)]

    first_step(1, terms_of(1), sums[2])
    middle_others[1] = across_chips(middle[1])
    first_step(0, terms_of(0), [middle[1], others[planes]], 36)
    twins[planes] = across_cores([after(here[planes], middle[1])])
    x_tail = x_first(every[-1:], [last], "x_first_tail", 36)
    others[planes] = after(others[planes], middle[1])
    fars[planes] = across_cores(others[planes])
    first_step(2, terms_of(2)[:-1] + [(x_tail, 0, size)], middle[0], 36)

    total = fold(square, "fold_own")
    total = [total] + [swap(total, d * group) for d in range(1, planes)]
    x_terms = [None] * 3
    x_terms[1] = along_x([piece(after(middle[1], total[0]))], [piece(middle[0])], along_x_matrix, "x_second_1")
    total = fold(after(total, x_terms[1]), "fold_planes")
    for i in range(3):
        middle_twin[i] = across_cores([after(middle[i], total)])
    middle_others[1] = after(middle_others[1], total)
    totals = [total] + [swap(after(total, middle_others[1]), m) for m in range(1, group)]
    middle_others[0] = across_chips(after(middle[0], middle_others[1]))
    totals = [piece(x) for x in totals]

    def middle_pieces(i):
        return [
            (x, part, kept // 2) for part in range(2) for pair in
            zip([middle[i]] + middle_others[i], middle_twin[i] + middle_far[i]) for x in pair
        ]

    def second_step(i):
        return y_call(
            functools.partial(second_kernel, cells), along_y_matrix, 0,
            [middle_pieces(i), middle_pieces(1) if i != 1 else [], [], [piece(middle[i])], [piece(middle[1])],
             [piece(x_terms[i])], [piece(base[i])]], [rows for _, _, rows in spots[i]], f"y_second_{i}", totals, {0: 1, 1: 36, 2: 1}[i],
        )

    whole = [(d, 0, size) for d in range(planes)]
    halved = [(d, 0, size) for d in parts[0]]
    halved += [(d, start, size // 2) for d in parts[1] for start in (0, size // 2)]
    spots = [halved, halved, whole]
    ends = [None] * 3

    def leave(i, second):
        gone = []
        for place, (d, start, _) in enumerate(spots[i]):
            if d and (start > 0) == second:
                ends[i][place] = swap(ends[i][place], d * group)
                gone.append(ends[i][place])
        return gone

    def put(i, out):
        return place_blocks(plane, ends[i], spots[i], i, velocity.shape, out)

    middle_far[1] = across_cores(middle_others[1])
    ends[1] = list(second_step(1))
    x_terms[0] = along_x([piece(after(middle[0], ends[1]))], [], along_x_matrix, "x_second_0", 1)
    gone = leave(1, False)
    x_terms[2] = along_x(
        [piece(after(middle[2], x_terms[0], gone, middle_twin[0]))], [piece(middle[0])], along_x_matrix, "x_second_2", 1
    )
    leave(1, True)
    middle_others[0] = after(middle_others[0], x_terms[2])
    middle_others[2] = across_chips(after(middle[2], middle_others[0]))
    middle_far[0] = across_cores(middle_others[0])
    ends[0] = list(second_step(0))
    gone = leave(0, False)
    out = put(1, None)
    middle_others[2] = after(middle_others[2], gone, out)
    rest = leave(0, True)
    middle_far[2] = across_cores(middle_others[2])
    ends[2] = list(after(second_step(2), rest))
    leave(2, False)
    return put(2, put(0, out))


def solution(mesh):
    placed = (P(None, "groups", "row", None), P(), P())
    return jax.shard_map(
        on_device,
        mesh=mesh,
        in_specs=placed,
        out_specs=P(None, "groups", "row", None),
        check_vma=False,
    )
```

```python
import functools

import jax
import jax.numpy as jnp
from jax import lax
from jax.experimental import pallas as pl
from jax.experimental.pallas import tpu as pltpu
from jax.sharding import PartitionSpec as P

viscosity = 0.2
power_input = 2.0
time_step = 0.5
first_weight = 8.0 / 15.0
second_weight = 5.0 / 12.0
back_weight = 17.0 / 60.0

BF16 = jnp.bfloat16
F32 = jnp.float32
VMEM_BYTES = 24 * 1024 * 1024


def halves(x):
    high = x.astype(BF16)
    return high, (x - high.astype(F32)).astype(BF16)


def product(a, b):
    return jnp.dot(a, b, preferred_element_type=F32)


def params():
    return pltpu.CompilerParams(vmem_limit_bytes=VMEM_BYTES)


def matrices_kernel(count, order_ref, own_ref, *refs):
    slope_parts, curve_parts = refs[:count], refs[count:2 * count]
    slope_ref, curve_ref, along_x_ref, along_y_ref, turned = refs[2 * count:]
    size = slope_parts[0].shape[0]
    for place, ref, scale in ((0, slope_ref, -0.5), (2, curve_ref, viscosity)):
        high, low = halves(ref[...] * scale)
        along_x_ref[place] = high
        along_x_ref[place + 1] = low
    for high_place, low_place, parts, scale in ((1, 0, slope_parts, -0.5), (2, 3, curve_parts, viscosity)):
        turned[...] = jnp.concatenate([part[...] for part in parts], axis=0).T
        for block in range(along_y_ref.shape[1] // size):
            source = pl.ds(pl.multiple_of(own_ref[block] * size, size), size)
            high, low = halves(turned[source, :] * scale)
            along_y_ref[high_place, block * size:(block + 1) * size, :] = high
            along_y_ref[low_place, block * size:(block + 1) * size, :] = low


def prepare_matrices(order, own, slope_matrix, curve_matrix, size):
    length = slope_matrix.shape[0]
    width = min(128, length)
    count = width // size
    kept = own.shape[0] * size

    def part(place):
        return pl.BlockSpec((size, length), lambda j, order_ref, own_ref: (order_ref[count * j + place], 0))

    parts = [part(place) for place in range(count)]
    straight = pl.BlockSpec((width, length), lambda j, order_ref, own_ref: (j, 0))
    return pl.pallas_call(
        functools.partial(matrices_kernel, count),
        grid_spec=pltpu.PrefetchScalarGridSpec(
            num_scalar_prefetch=2,
            grid=(length // width,),
            in_specs=parts + parts + [straight, straight],
            out_specs=[
                pl.BlockSpec((4, width, length), lambda j, order_ref, own_ref: (0, j, 0)),
                pl.BlockSpec((4, kept, width), lambda j, order_ref, own_ref: (0, 0, j)),
            ],
            scratch_shapes=[pltpu.VMEM((length, width), F32)],
        ),
        out_shape=[
            jax.ShapeDtypeStruct((4, length, length), BF16),
            jax.ShapeDtypeStruct((4, kept, length), BF16),
        ],
        compiler_params=params(),
        cost_estimate=pl.CostEstimate(flops=16 * length ** 3, bytes_accessed=32 * length * length, transcendentals=0),
    )(order, own, *([slope_matrix] * count), *([curve_matrix] * count), slope_matrix, curve_matrix)


def piece_spec(piece, width, column):
    _, place, rows = piece
    return pl.BlockSpec((rows, width), lambda n: (place, column(n)))


def joined(refs, columns=slice(None)):
    return jnp.concatenate([ref[:, columns] for ref in refs], axis=0)


def cut(refs, counts):
    pieces, start = [], 0
    for count in counts:
        pieces.append(refs[start:start + count])
        start += count
    return *pieces, refs[start:]


def pack_kernel(plane_ref, velocity_ref, *block_refs):
    components, planes, size, length = velocity_ref.shape
    plane = plane_ref[0]
    velocity = velocity_ref[...].reshape(components * planes * size // 8, 8, length)
    squares = jnp.sum(velocity * velocity, axis=0)
    *block_refs, tail_ref = block_refs
    for d, ref in enumerate(block_refs):
        count = components if d < planes - 1 else components - 1
        for i in range(count):
            ref[i * size:(i + 1) * size, :] = velocity_ref[i, plane ^ d]
        ref[count * size:, :] = squares
    tail_ref[...] = velocity_ref[components - 1, plane ^ (planes - 1)]


def pack(plane, velocity):
    components, planes, size, length = velocity.shape
    rows = [components * size + 8] * (planes - 1) + [(components - 1) * size + 8, size]
    return pl.pallas_call(
        pack_kernel,
        grid_spec=pltpu.PrefetchScalarGridSpec(
            num_scalar_prefetch=1,
            grid=(1,),
            in_specs=[pl.BlockSpec(velocity.shape, lambda n, plane_ref: (0, 0, 0, 0))],
            out_specs=[pl.BlockSpec((count, length), lambda n, plane_ref: (0, 0)) for count in rows],
        ),
        out_shape=[jax.ShapeDtypeStruct((count, length), F32) for count in rows],
        compiler_params=params(),
        name="pack",
    )(plane.reshape(1).astype(jnp.int32), velocity)


def along_x_kernel(counts, copies, *refs):
    fields, carriers, (matrix_ref, out_ref, stack) = cut(refs, counts)
    rows = out_ref.shape[0]
    carriers = (carriers or fields) * copies

    @pl.when(pl.program_id(0) == 0)
    def _():
        field = joined(fields)
        high, low = halves(field)
        stack[0:rows] = low
        stack[rows:2 * rows] = high
        high, low = halves(joined(carriers) * field)
        stack[2 * rows:3 * rows] = high
        stack[3 * rows:4 * rows] = low

    tile = out_ref.shape[1]
    columns = pl.ds(pl.multiple_of(pl.program_id(0) * tile, tile), tile)
    a = product(stack[...], matrix_ref[0])
    b = product(stack[rows:3 * rows], matrix_ref[1])
    c = product(stack[0:2 * rows], matrix_ref[2])
    d = product(stack[rows:2 * rows], matrix_ref[3])
    slope = a[0:rows] + a[rows:2 * rows] + b[0:rows]
    rest = a[2 * rows:3 * rows] + a[3 * rows:] + b[rows:] + c[0:rows] + c[rows:] + d
    out_ref[...] = joined(carriers, columns) * slope + rest


def along_x(fields, carriers, matrix, name, weight=36):
    rows, length = sum(piece[2] for piece in fields), fields[0][0].shape[1]
    copies = len(fields) // len(carriers) if carriers else 1
    tile = min(256, length)
    pieces = fields + carriers
    return pl.pallas_call(
        functools.partial(along_x_kernel, (len(fields), len(carriers)), copies),
        grid=(length // tile,),
        in_specs=[piece_spec(piece, length, lambda n: 0) for piece in pieces]
        + [pl.BlockSpec((4, length, tile), lambda n: (0, 0, n))],
        out_specs=pl.BlockSpec((rows, tile), lambda n: (0, n)),
        out_shape=jax.ShapeDtypeStruct((rows, length), F32),
        scratch_shapes=[pltpu.VMEM((4 * rows, length), BF16)],
        compiler_params=params(),
        cost_estimate=pl.CostEstimate(
            flops=weight * rows * length * length, bytes_accessed=4 * rows * length, transcendentals=0
        ),
        name=name,
    )(*[piece[0] for piece in pieces], matrix)


def y_sums(matrix_ref, fields, carriers, sums):
    rows, length = matrix_ref.shape[1:]
    field = joined(fields)
    carrier = joined(carriers) if carriers else field
    field_high, field_low = halves(field)
    flux_high, flux_low = halves(field * carrier)
    matrix = matrix_ref[...].reshape(4 * rows, length)
    a = product(matrix, field_high)
    b = product(matrix[rows:3 * rows], field_low)
    c = product(matrix[0:2 * rows], flux_high)
    d = product(matrix[rows:2 * rows], flux_low)
    slope = a[0:rows] + a[rows:2 * rows] + b[0:rows]
    rest = a[2 * rows:3 * rows] + a[3 * rows:] + b[rows:] + c[0:rows] + c[rows:] + d
    if sums:
        slope, rest = slope + sums[0][...], rest + sums[1][...]
    return slope, rest


def partial_kernel(counts, matrix_ref, *refs):
    fields, carriers, sums, (slope_ref, rest_ref) = cut(refs, counts)
    slope_ref[...], rest_ref[...] = y_sums(matrix_ref, fields, carriers, sums)


def tendency(cells, totals, field, carrier, x_terms, sums):
    total = jnp.sum(functools.reduce(jnp.add, [ref[...] for ref in totals]), keepdims=True)
    forcing = power_input / (total / cells)
    return joined(x_terms) + joined(carrier) * sums[0] + sums[1] + forcing * field


def first_kernel(cells, counts, matrix_ref, *refs):
    fields, carriers, sums, own, own_carrier, x_terms, totals, (middle_ref, base_ref, square_ref) = cut(refs, counts)
    rows = matrix_ref.shape[1]
    field = joined(own)
    first = tendency(cells, totals, field, own_carrier, x_terms, y_sums(matrix_ref, fields, carriers, sums))
    middle = field + (time_step * first_weight) * first
    middle_ref[...] = middle
    base_ref[...] = middle - (time_step * back_weight) * first
    square_ref[...] = jnp.sum((middle * middle).reshape(rows // 8, 8, middle.shape[1]), axis=0)


def second_kernel(cells, counts, matrix_ref, *refs):
    fields, carriers, sums, own, own_carrier, x_terms, totals, (base_ref, *out_refs) = cut(refs, counts)
    field = joined(own)
    second = tendency(cells, totals, field, own_carrier, x_terms, y_sums(matrix_ref, fields, carriers, sums))
    out = base_ref[...] + (time_step * second_weight) * second
    start = 0
    for out_ref in out_refs:
        out_ref[...] = out[start:start + out_ref.shape[0]]
        start += out_ref.shape[0]


def y_call(kernel, matrix, part, groups, out_rows, name, totals=(), weight=36):
    rows, length = matrix.shape[1], groups[0][0][0].shape[1]
    depth = sum(piece[2] for piece in groups[0])
    tile = min(256, length)
    pieces = [piece for group in groups for piece in group]
    counts = [len(group) for group in groups]
    specs = [piece_spec(piece, tile, lambda n: n) for piece in pieces]
    if totals:
        start = sum(counts[:6])
        pieces[start:start] = totals
        specs[start:start] = [piece_spec(piece, piece[0].shape[1], lambda n: 0) for piece in totals]
        counts[6:] = [len(totals)]
    return pl.pallas_call(
        functools.partial(kernel, tuple(counts)),
        grid=(length // tile,),
        in_specs=[pl.BlockSpec((4, rows, depth), lambda n: (0, 0, part))] + specs,
        out_specs=[pl.BlockSpec((count, tile), lambda n: (0, n)) for count in out_rows],
        out_shape=[jax.ShapeDtypeStruct((count, length), F32) for count in out_rows],
        compiler_params=params(),
        cost_estimate=pl.CostEstimate(
            flops=weight * rows * depth * length, bytes_accessed=4 * rows * length, transcendentals=0
        ),
        name=name,
    )(matrix, *[piece[0] for piece in pieces])


def fold_kernel(*refs):
    total = functools.reduce(jnp.add, [ref[...] for ref in refs[:-1]])
    refs[-1][...] = functools.reduce(jnp.add, [total[:, k:k + 128] for k in range(0, total.shape[1], 128)])


def fold(arrays, name):
    return pl.pallas_call(
        fold_kernel,
        out_shape=jax.ShapeDtypeStruct((8, 128), F32),
        compiler_params=params(),
        name=name,
    )(*arrays)


def place_kernel(spots, plane_ref, *refs):
    out_ref = refs[-1]
    for (d, start, rows), ref in zip(spots, refs):
        out_ref[plane_ref[0] ^ d, start:start + rows, :] = ref[...]


def place_blocks(plane, arrays, spots, component, shape, out):
    planes, size, length = shape[1:]
    before = [] if out is None else [out]
    return pl.pallas_call(
        functools.partial(place_kernel, spots),
        grid_spec=pltpu.PrefetchScalarGridSpec(
            num_scalar_prefetch=1,
            grid=(1,),
            in_specs=[pl.BlockSpec((rows, length), lambda n, plane_ref: (0, 0)) for _, _, rows in spots]
            + [pl.BlockSpec(memory_space=pl.ANY)] * len(before),
            out_specs=pl.BlockSpec((None, planes, size, length), lambda n, plane_ref: (component, 0, 0, 0)),
        ),
        out_shape=jax.ShapeDtypeStruct(shape, F32),
        input_output_aliases={1 + len(arrays): 0} if before else {},
        compiler_params=params(),
        name="place",
    )(plane.reshape(1).astype(jnp.int32), *arrays, *before)


def after(values, *earlier):
    return lax.optimization_barrier((values, earlier))[0]


def on_device(velocity, slope_matrix, curve_matrix):
    components, planes, size, length = velocity.shape
    devices = lax.axis_size("row")
    group = devices // planes
    chips = group // 2
    kept = length // group
    place = lax.axis_index("row")
    plane, member = place // group, place % group
    cells = components * planes * size * devices * length
    parts = [range(planes // 2), range(planes // 2, planes)]

    def swap(x, distance):
        return lax.ppermute(x, "row", [(r, r ^ distance) for r in range(devices)])

    def across_chips(x):
        return [swap(x, 2 * h) for h in range(1, chips)]

    def across_cores(pieces):
        return [swap(piece, 1) for piece in pieces]

    order = jnp.stack([
        (plane ^ d) * group + (member ^ (2 * h + core))
        for part in parts for h in range(chips) for core in range(2) for d in part
    ]).astype(jnp.int32)
    own_order = jnp.stack([(plane ^ d) * group + member for d in range(planes)]).astype(jnp.int32)

    last = planes - 1
    here, others, twins, fars = ([None] * (planes + 1) for _ in range(4))

    def piece_of(store, i, d):
        block = store[planes] if d == last and i == components - 1 else store[d]
        return lambda h: (block[h], 0 if d == last and i == components - 1 else i, size)

    def block_pieces(i, part):
        near = [[here[d]] + (others[d] or []) for d in range(planes + 1)]
        far = [(twins[d] or []) + (fars[d] or []) for d in range(planes + 1)]
        return [
            piece_of(store, i, d)(h) for h in range(chips) for store in (near, far) for d in parts[part]
        ]

    def here_pieces(i, distances):
        return [piece_of([[block] for block in here], i, d)(0) for d in distances]

    def x_first(components, distances, name, weight=36):
        fields = [piece for i in components for piece in here_pieces(i, distances)]
        return along_x(fields, here_pieces(0, distances), along_x_matrix, name, weight)

    every = range(components)
    blocks = list(pack(plane, velocity))
    here[0] = blocks[0]
    for d in range(1, last):
        here[d] = swap(blocks[d], d * group)
    others[0] = across_chips(here[0])
    others[1] = across_chips(blocks[1])
    along_x_matrix, along_y_matrix = prepare_matrices(order, own_order, slope_matrix, curve_matrix, size)

    here[1] = after(here[1], along_x_matrix, along_y_matrix)
    others[1] = [swap(after(block, here[1]), group) for block in others[1]]
    here[last] = swap(after(blocks[last], here[1]), last * group)
    here[planes] = swap(after(blocks[planes], here[last - 1]), last * group)
    x_near = x_first(every, parts[0], "x_first_near", 1)
    here[2] = after(here[2], x_near, others[0])
    others[2] = across_chips(here[2])
    x_two = x_first(every, [2], "x_first_2", 1)
    for d in parts[0]:
        twins[d] = across_cores([after(here[d], x_near)])
    here[last] = after(here[last], x_two)
    others[last] = across_chips(here[last])
    for d in parts[0]:
        others[d] = after(others[d], here[last])
        fars[d] = across_cores(others[d])
    sums = [None] * 3

    def near_sums(i, earlier):
        fields = block_pieces(i, 0)
        fields = [(after(fields[0][0], earlier), *fields[0][1:])] + fields[1:]
        sums[i] = y_call(
            partial_kernel, along_y_matrix, 0, [fields, block_pieces(1, 0) if i != 1 else [], []],
            [kept, kept], f"y_first_near_{i}", (), 36,
        )

    near_sums(1, here[last])
    twins[2] = across_cores([after(here[2], here[last])])
    others[2] = after(others[2], here[last])
    fars[2] = across_cores(others[2])
    here[last] = after(here[last], sums[1])
    x_last = x_first(every[:-1], [last], "x_first_last", 36)
    near_sums(0, x_last)
    here[planes] = after(here[planes], sums[0])
    others[planes] = across_chips(here[planes])
    twins[last] = across_cores([after(here[last], sums[1], twins[2], fars[2])])
    near_sums(2, here[planes])
    others[last] = after(others[last], sums[2])
    fars[last] = across_cores(others[last])
    totals = [
        (block, block.shape[0] // 8 - 1, 8)
        for d in range(planes) for block in [here[d]] + others[d] + twins[d] + fars[d]
    ]

    middle, base, square = [None] * 3, [None] * 3, [None] * 3
    middle_others, middle_twin, middle_far = [None] * 3, [None] * 3, [None] * 3

    def piece(x):
        return (x, 0, x.shape[0])

    def first_step(i, terms, earlier, weight=36):
        fields = block_pieces(i, 1)
        fields = [(after(fields[0][0], earlier), *fields[0][1:])] + fields[1:]
        middle[i], base[i], square[i] = y_call(
            functools.partial(first_kernel, cells), along_y_matrix, 1,
            [fields, block_pieces(1, 1) if i != 1 else [], [piece(x) for x in sums[i]],
             here_pieces(i, range(planes)), here_pieces(1, range(planes)), terms],
            [kept, kept, 8], f"y_first_far_{i}", totals, weight,
        )

    def terms_of(i):
        return [(x_near, i, len(parts[0]) * size), (x_two, i, size), (x_last, i, size)]

    first_step(1, terms_of(1), sums[2])
    middle_others[1] = across_chips(middle[1])
    first_step(0, terms_of(0), [middle[1], others[planes]], 36)
    twins[planes] = across_cores([after(here[planes], middle[1])])
    x_tail = x_first(every[-1:], [last], "x_first_tail", 36)
    others[planes] = after(others[planes], middle[1])
    fars[planes] = across_cores(others[planes])
    first_step(2, terms_of(2)[:-1] + [(x_tail, 0, size)], middle[0], 36)

    total = fold(square, "fold_own")
    total = [total] + [swap(total, d * group) for d in range(1, planes)]
    x_terms = [None] * 3
    x_terms[1] = along_x([piece(after(middle[1], total[0]))], [piece(middle[0])], along_x_matrix, "x_second_1")
    total = fold(after(total, x_terms[1]), "fold_planes")
    for i in range(3):
        middle_twin[i] = across_cores([after(middle[i], total)])
    middle_others[1] = after(middle_others[1], total)
    totals = [total] + [swap(after(total, middle_others[1]), m) for m in range(1, group)]
    middle_others[0] = across_chips(after(middle[0], middle_others[1]))
    totals = [piece(x) for x in totals]

    def middle_pieces(i):
        return [
            (x, part, kept // 2) for part in range(2) for pair in
            zip([middle[i]] + middle_others[i], middle_twin[i] + middle_far[i]) for x in pair
        ]

    def second_step(i):
        return y_call(
            functools.partial(second_kernel, cells), along_y_matrix, 0,
            [middle_pieces(i), middle_pieces(1) if i != 1 else [], [], [piece(middle[i])], [piece(middle[1])],
             [piece(x_terms[i])], [piece(base[i])]], [rows for _, _, rows in spots[i]], f"y_second_{i}", totals, {0: 1, 1: 36, 2: 1}[i],
        )

    whole = [(d, 0, size) for d in range(planes)]
    halved = [(d, 0, size) for d in parts[0]]
    halved += [(d, start, size // 2) for d in parts[1] for start in (0, size // 2)]
    spots = [halved, halved, whole]
    ends = [None] * 3

    def leave(i, second):
        gone = []
        for place, (d, start, _) in enumerate(spots[i]):
            if d and (start > 0) == second:
                ends[i][place] = swap(ends[i][place], d * group)
                gone.append(ends[i][place])
        return gone

    def put(i, out):
        return place_blocks(plane, ends[i], spots[i], i, velocity.shape, out)

    middle_far[1] = across_cores(middle_others[1])
    ends[1] = list(second_step(1))
    x_terms[0] = along_x([piece(after(middle[0], ends[1]))], [], along_x_matrix, "x_second_0", 1)
    gone = leave(1, False)
    leave(1, True)
    middle_others[0] = after(middle_others[0], x_terms[0], gone, middle_twin[0])
    middle_others[2] = across_chips(after(middle[2], middle_others[0]))
    x_terms[2] = along_x(
        [piece(after(middle[2], middle_others[0]))], [piece(middle[0])], along_x_matrix, "x_second_2", 36
    )
    middle_far[0] = across_cores(middle_others[0])
    middle_far[0] = after(middle_far[0], x_terms[2])
    ends[0] = list(second_step(0))
    ends[1] = after(ends[1], ends[0])
    out = put(1, None)
    ends[0][1:] = after(ends[0][1:], [ends[1][place] for place, spot in enumerate(spots[1]) if spot[1]])
    gone = leave(0, False)
    middle_others[2] = after(middle_others[2], gone, out)
    rest = leave(0, True)
    middle_far[2] = across_cores(middle_others[2])
    ends[2] = list(after(second_step(2), rest))
    leave(2, False)
    return put(2, put(0, out))


def solution(mesh):
    placed = (P(None, "groups", "row", None), P(), P())
    return jax.shard_map(
        on_device,
        mesh=mesh,
        in_specs=placed,
        out_specs=P(None, "groups", "row", None),
        check_vma=False,
    )
```
